32 devices in a mesh: past: 8 (over y, x, core), second: 4 (over z).
Axes of the slice: x: 2, y: 2, z: 4, core: 2. Of those that a mesh axis runs over, the one named last changes fastest.
Arguments:
- g_hist: bfloat16 [16384, 4096], P('past', 'second'), may hold values from -6 to 6
- sigma_hist: bfloat16 [1024, 16384], P(None, 'past'), may hold values from -0.0625 to 0.0625
- volterra: bfloat16 [2, 512, 1024], replicated, may hold values from -0.1875 to 0.1875
- sigma_edge: bfloat16 [512, 4096], P(None, 'second'), may hold values from -6 to 6
- coupling: float32 [32, 4096], P(None, 'second'), may hold values from 0.3 to 3
Outputs:
- g_new: bfloat16 [1024, 4096], P(None, 'second')
- sigma_new: bfloat16 [1024, 4096], P(None, 'second')
The draws below stay inside these ranges and needn't reach their ends.
All inputs are finite; a program needn't handle non-finite values.
Results may differ from the reference program's by a relative error of at most 0.0059.
Values may be sent and summed in bfloat16 or wider, within the bound.
No kernel may reach another device: no remote copies, remote signals or barrier semaphores. Data moves between devices by JAX's collectives and lax.ppermute only.
A program may use at most 64 MiB of HBM per device.

```python
import math
import jax
import jax.numpy as jnp

N = 32
BLK = 16
NB = 2
NS = 512
NC = 128


def with_spikes(values, own_key, source, target, parts, factor):
    owner, partner = [(jnp.arange(values.shape[dim]) // (values.shape[dim] // parts)).reshape([-1 if axis == dim else 1 for axis in range(values.ndim)]) for dim in (source, target)]
    chosen = jax.random.permutation(own_key, parts)[partner]
    strong = (owner == chosen) | (owner == (partner + parts // 2) % parts)
    return jnp.where(strong, factor * values, values)


def shard_levels(stream_key, extent, split, low, largest):
    def one(dim, blocks):
        draws = jax.random.uniform(jax.random.fold_in(jax.random.fold_in(stream_key, 6), dim), (blocks,), jnp.float32, low / len(split), largest / len(split))
        return jnp.repeat(jnp.exp(draws), extent[dim] // blocks).reshape((-1,) + (1,) * (len(extent) - dim - 1))

    gain = one(*split[0])
    for cut in split[1:]:
        gain = gain * one(*cut)
    return gain


def gaussian(stream_key, shape, deviation, bound, pieces=(), dtype=jnp.bfloat16):
    drawn = jax.random.normal(stream_key, shape, jnp.float32) * deviation
    if len(pieces) > 0:
        drawn = shard_levels(stream_key, shape, pieces, -0.22, 0.18) * drawn
    return jnp.clip(drawn, min=-bound, max=bound).astype(dtype)


def noise_with(rng, dims, scale, bound, cuts, heavy, kind=jnp.bfloat16):
    entries = scale * jax.random.normal(rng, dims, jnp.float32)
    if cuts:
        entries = entries * shard_levels(rng, dims, cuts, -0.22, 0.18)
    return jnp.clip(with_spikes(entries, jax.random.fold_in(rng, 3), *heavy), -bound, bound).astype(kind)


def setup_inputs(seed: int = 0) -> dict:
    streams_of = jax.random.split(jax.random.key(seed), 6)
    return {
        "g_hist": gaussian(streams_of[0], (NS * N, NC * N), 1.0, 6.0, ((0, 8), (1, 4))),
        "sigma_hist": noise_with(streams_of[1], (NB * BLK * N, NS * N), (NS * N) ** -0.5, 0.0625, ((1, 8),), (1, 0, 8, 2.0)),
        "volterra": gaussian(streams_of[2], (NB, BLK * N, 2 * BLK * N), (2 * BLK * N) ** -0.5, 0.1875),
        "sigma_edge": gaussian(streams_of[3], (BLK * N, NC * N), 1.0, 6.0, ((1, 4),)),
        "coupling": jnp.clip(jnp.exp(math.log(3.0) - 2.3025851 * jax.random.uniform(streams_of[4], (N, NC * N), jnp.float32) ** shard_levels(streams_of[4], (N, NC * N), ((1, 4),), -0.2, 0.2)), 0.3, 3.0),
    }


def reference(g_hist, sigma_hist, volterra, sigma_edge, coupling):
    rows = BLK * N
    prev = sigma_edge
    g_blocks = []
    s_blocks = []
    for block in range(NB):
        sig_rows = sigma_hist[block * rows:(block + 1) * rows, :]
        memory = jnp.dot(sig_rows, g_hist, preferred_element_type=jnp.float32).astype(jnp.bfloat16)
        stacked = jnp.concatenate([memory, prev], axis=0)
        gnew = jnp.dot(volterra[block], stacked, preferred_element_type=jnp.float32)
        cubic = gnew.reshape(BLK, N, -1) ** 3 * coupling[None]
        meansq = jnp.mean(cubic * cubic)
        sigma = (cubic / jnp.sqrt(meansq + 1e-06)).reshape(rows, -1).astype(jnp.bfloat16)
        g_blocks.append(gnew.astype(jnp.bfloat16))
        s_blocks.append(sigma)
        prev = sigma
    return (jnp.concatenate(g_blocks, axis=0), jnp.concatenate(s_blocks, axis=0))
```

```python
import functools

import jax
import jax.numpy as jnp
from jax import lax
from jax.experimental import pallas as pl
from jax.experimental.pallas import tpu as pltpu
from jax.sharding import PartitionSpec as P

VMEM = 48 * 1024 * 1024
F32 = jnp.float32
BF16 = jnp.bfloat16


def log2(n):
    bits = n.bit_length() - 1
    assert n == 1 << bits
    return bits


def level_bits(size, depth):
    bits = list(range(log2(size)))
    return bits, bits[:1] + bits[1:depth][::-1] + bits[depth:]


def reverse_bits(value, bits):
    result = value * 0
    for i in range(bits):
        result = result | (((value >> i) & 1) << (bits - 1 - i))
    return result


class Order:
    def __init__(self, depth):
        self.depth, self.half = depth, 1 << (depth - 1)

    def own(self, me):
        return reverse_bits(me, self.depth)

    def kept(self, me, j):
        return self.own(me) ^ jnp.where(me % 2 == 1, reverse_bits(j, self.depth - 1), j)

    def sent(self, me, j):
        return self.own(me) ^ self.half ^ jnp.where(me % 2 == 1, j, reverse_bits(j, self.depth - 1))

    def place(self, me, block):
        apart = block ^ self.own(me)
        low, top = apart & (self.half - 1), apart & self.half
        turned = (me + top // self.half) % 2 == 1
        return top + jnp.where(turned, reverse_bits(low, self.depth - 1), low)


def partial_kernel(count, me, sigma, *refs):
    parts, out, total = refs[:count], refs[count], refs[count + 1]
    step = pl.program_id(0)
    right = jnp.concatenate([part[...] for part in parts], axis=1)
    product = jnp.dot(sigma[...], right, preferred_element_type=F32)

    @pl.when(step == 0)
    def _():
        total[...] = product

    @pl.when(step > 0)
    def _():
        total[...] += product

    @pl.when(step == pl.num_programs(0) - 1)
    def _():
        out[...] = total[...].astype(out.dtype)


def partial_product(me, sigma_hist, g_hist, block, rows, blocks_of, count, width, dtype):
    depth = g_hist.shape[0]
    chunk = depth // 4
    columns = count * width

    def part(j):
        return pl.BlockSpec((chunk, width), lambda k, me: (k, blocks_of(me[0], j)))

    return pl.pallas_call(
        functools.partial(partial_kernel, count),
        grid_spec=pltpu.PrefetchScalarGridSpec(
            num_scalar_prefetch=1,
            grid=(depth // chunk,),
            in_specs=[pl.BlockSpec((rows, chunk), lambda k, me: (block, k))]
            + [part(j) for j in range(count)],
            out_specs=pl.BlockSpec((rows, columns), lambda k, me: (0, 0)),
            scratch_shapes=[pltpu.VMEM((rows, columns), F32)],
        ),
        out_shape=jax.ShapeDtypeStruct((rows, columns), dtype),
        compiler_params=pltpu.CompilerParams(vmem_limit_bytes=VMEM),
        cost_estimate=pl.CostEstimate(
            flops=2 * rows * depth * columns, bytes_accessed=2 * depth * (rows + columns), transcendentals=0
        ),
        name="partial_product",
    )(me, sigma_hist, *[g_hist] * count)


def cubed(g, coupling):
    orbitals = coupling.shape[0]
    g3 = g.reshape(g.shape[0] // orbitals, orbitals, g.shape[1])
    return (g3 * g3 * g3 * coupling[None]).reshape(g.shape)


def fold_rows(x):
    return jnp.sum(x.reshape(x.shape[0] // 8, 8, x.shape[1]), axis=0)


def scale_of(squares, count):
    return 1.0 / jnp.sqrt(jnp.sum(squares) / count + 1e-06)


def own_first_kernel(me, memory, w, prev, coupling, cubic, squares):
    rows = memory.shape[0]
    g = jnp.dot(w[0, :, :rows], memory[...], preferred_element_type=F32)
    g += jnp.dot(w[0, :, rows:], prev[...], preferred_element_type=F32)
    c = cubed(g, coupling[...])
    cubic[...] = c
    squares[...] = fold_rows(c * c)


def own_next_kernel(count_all, me, memory, w, prev_cubic, prev_squares, coupling, cubic, squares):
    rows = memory.shape[0]
    prev = (prev_cubic[...] * scale_of(prev_squares[...], count_all)).astype(BF16)
    g = jnp.dot(w[0, :, :rows], memory[...], preferred_element_type=F32)
    g += jnp.dot(w[0, :, rows:], prev, preferred_element_type=F32)
    c = cubed(g, coupling[...])
    cubic[...] = c
    squares[...] = fold_rows(c * c)


def own_columns(me, order, memory, volterra, block, prev, prev_squares, coupling, count_all):
    rows, width = memory.shape
    full = lambda shape: pl.BlockSpec(shape, lambda i, me: (0, 0))
    w_spec = pl.BlockSpec((1, rows, 2 * rows), lambda i, me: (block, 0, 0))
    coupling_spec = pl.BlockSpec((coupling.shape[0], width), lambda i, me: (0, order.own(me[0])))
    if prev_squares is None:
        kernel = own_first_kernel
        in_specs = [full((rows, width)), w_spec, pl.BlockSpec((rows, width), lambda i, me: (0, order.own(me[0])))]
        operands = [memory, volterra, prev]
    else:
        kernel = functools.partial(own_next_kernel, count_all)
        in_specs = [full((rows, width)), w_spec, full((rows, width)), full(prev_squares.shape)]
        operands = [memory, volterra, prev, prev_squares]
    return pl.pallas_call(
        kernel,
        grid_spec=pltpu.PrefetchScalarGridSpec(
            num_scalar_prefetch=1,
            grid=(1,),
            in_specs=in_specs + [coupling_spec],
            out_specs=[full((rows, width)), full((8, width))],
        ),
        out_shape=[jax.ShapeDtypeStruct((rows, width), F32), jax.ShapeDtypeStruct((8, width), F32)],
        compiler_params=pltpu.CompilerParams(vmem_limit_bytes=VMEM),
        cost_estimate=pl.CostEstimate(
            flops=4 * rows * rows * width, bytes_accessed=4 * rows * rows + 8 * rows * width, transcendentals=0
        ),
        name="own_columns",
    )(me, *operands, coupling)


def finish_kernel(count_all, first, last, me, left, right, w, prev, squares, coupling, *refs):
    refs = list(refs)
    w_next = None if last else refs.pop(0)
    refs = refs if first else refs[2:]
    g_out, s_out = refs[:2]
    rows = left.shape[0]
    memory = jnp.concatenate([left[...], right[...]], axis=1)
    g = jnp.dot(w[0, :, :rows], memory, preferred_element_type=F32)
    if first:
        g += jnp.dot(w[0, :, rows:], prev[...], preferred_element_type=F32)
    else:
        g += prev[...]
    g_out[...] = g.astype(BF16)
    sigma = (cubed(g, coupling[...]) * scale_of(squares[...], count_all)).astype(BF16)
    s_out[...] = sigma
    if not last:
        refs[2][...] = jnp.dot(w_next[0, :, rows:], sigma, preferred_element_type=F32)


def finish(me, order, memory, volterra, block, prev, squares, coupling, outs, count_all, width):
    rows, columns = memory.shape
    blocks = volterra.shape[0]
    pair = 2 * width
    first, last = block == 0, block == blocks - 1
    place = lambda side: pl.BlockSpec((rows, width), lambda q, me: (0, order.place(me[0], 2 * q + side)))
    w_spec = lambda k: pl.BlockSpec((1, rows, 2 * rows), lambda q, me: (k, 0, 0))
    straight = lambda size, row=0: pl.BlockSpec((size, pair), lambda q, me: (row, q))
    operands = [memory, memory, volterra, prev, squares, coupling]
    in_specs = [
        place(0),
        place(1),
        w_spec(block),
        straight(rows),
        pl.BlockSpec(squares.shape, lambda q, me: (0, 0)),
        straight(coupling.shape[0]),
    ]
    out_specs = [straight(rows, block)] * 2
    out_shape = [jax.ShapeDtypeStruct((blocks * rows, columns), BF16)] * 2
    aliases = {}
    if not last:
        operands.append(volterra)
        in_specs.append(w_spec(block + 1))
        out_specs.append(straight(rows))
        out_shape.append(jax.ShapeDtypeStruct((rows, columns), F32))
    if not first:
        aliases = {1 + len(operands): 0, 2 + len(operands): 1}
        operands += outs
        in_specs += [pl.BlockSpec(memory_space=pl.ANY)] * 2
    return pl.pallas_call(
        functools.partial(finish_kernel, count_all, first, last),
        grid_spec=pltpu.PrefetchScalarGridSpec(
            num_scalar_prefetch=1, grid=(columns // pair,), in_specs=in_specs, out_specs=out_specs
        ),
        out_shape=out_shape,
        input_output_aliases=aliases,
        compiler_params=pltpu.CompilerParams(vmem_limit_bytes=VMEM),
        cost_estimate=pl.CostEstimate(
            flops=4 * rows * rows * columns, bytes_accessed=4 * rows * rows + 6 * rows * columns, transcendentals=0
        ),
        name="finish_block",
    )(me, *operands)


def per_device(past, second, g_hist, sigma_hist, volterra, sigma_edge, coupling):
    blocks, rows = volterra.shape[:2]
    columns = g_hist.shape[1]
    count_all = rows * columns * second
    depth = min(log2(past), log2(max(columns // 128, 2)))
    width = columns >> depth
    even, odd = level_bits(past, depth)
    order = Order(depth)
    me = lax.axis_index("past").astype(jnp.int32).reshape(1)

    def swap(x, level):
        pairs = [(d, d ^ (1 << (odd if d % 2 else even)[level])) for d in range(past)]
        return lax.ppermute(x, "past", pairs)

    def reduced(block):
        send = partial_product(me, sigma_hist, g_hist, block, rows, order.sent, order.half, width, BF16)
        arrived = swap(send, 0)
        total = partial_product(me, sigma_hist, g_hist, block, rows, order.kept, order.half, width, F32)
        for level in range(1, depth):
            kept = total.shape[1] // 2
            send = (total[:, kept:] + arrived[:, kept:].astype(F32)).astype(BF16)
            total = total[:, :kept] + arrived[:, :kept].astype(F32)
            arrived = swap(send, level)
        total = total + arrived.astype(F32)
        for level in range(depth, len(even)):
            rounded = total.astype(BF16)
            total = rounded.astype(F32) + swap(rounded, level).astype(F32)
        return total.astype(BF16)

    def gathered(piece):
        for level in reversed(range(depth)):
            piece = jnp.concatenate([piece, swap(piece, level)], axis=1)
        return piece

    def summed(squares):
        for level in range(log2(second)):
            squares = squares + lax.ppermute(squares, "second", [(d, d ^ (1 << level)) for d in range(second)])
        for level in range(depth):
            squares = squares + swap(squares, level)
        return squares

    own, whole, squares = [], [], []
    cubic, total = sigma_edge, None
    for block in range(blocks):
        own.append(reduced(block))
    for block in range(blocks):
        cubic, local = own_columns(me, order, own[block], volterra, block, cubic, total, coupling, count_all)
        total = summed(local)
        squares.append(total)
        whole.append(gathered(own[block]))
    outs, start = None, sigma_edge
    for block in range(blocks):
        results = finish(
            me, order, whole[block], volterra, block, start, squares[block], coupling, outs, count_all, width
        )
        outs = results[:2]
        start = results[2] if block < blocks - 1 else None
    return tuple(outs)


def solution(mesh):
    return jax.shard_map(
        functools.partial(per_device, mesh.shape["past"], mesh.shape["second"]),
        mesh=mesh,
        in_specs=(P("past", "second"), P(None, "past"), P(), P(None, "second"), P(None, "second")),
        out_specs=(P(None, "second"), P(None, "second")),
        check_vma=False,
    )
```

```python
import functools

import jax
import jax.numpy as jnp
from jax import lax
from jax.experimental import pallas as pl
from jax.experimental.pallas import tpu as pltpu
from jax.sharding import PartitionSpec as P

VMEM = 48 * 1024 * 1024
F32 = jnp.float32
BF16 = jnp.bfloat16


def log2(n):
    bits = n.bit_length() - 1
    assert n == 1 << bits
    return bits


def level_bits(size, depth):
    bits = list(range(log2(size)))
    return bits, bits[:1] + bits[1:depth][::-1] + bits[depth:]


def reverse_bits(value, bits):
    result = value * 0
    for i in range(bits):
        result = result | (((value >> i) & 1) << (bits - 1 - i))
    return result


class Order:
    def __init__(self, depth):
        self.depth, self.half = depth, 1 << (depth - 1)

    def own(self, me):
        return reverse_bits(me, self.depth)

    def kept(self, me, j):
        return self.own(me) ^ jnp.where(me % 2 == 1, reverse_bits(j, self.depth - 1), j)

    def sent(self, me, j):
        return self.own(me) ^ self.half ^ jnp.where(me % 2 == 1, j, reverse_bits(j, self.depth - 1))

    def owner(self, block):
        return reverse_bits(block, self.depth)


def partial_kernel(me, sigma, left, right, out):
    both = jnp.concatenate([left[...], right[...]], axis=1)
    out[...] = jnp.dot(sigma[...], both, preferred_element_type=F32).astype(out.dtype)


def partial_product(me, sigma_hist, g_hist, block, rows, blocks_of, count, width, dtype):
    depth = g_hist.shape[0]
    columns = count * width

    def part(side):
        return pl.BlockSpec((depth, width), lambda q, me: (0, blocks_of(me[0], 2 * q + side)))

    return pl.pallas_call(
        partial_kernel,
        grid_spec=pltpu.PrefetchScalarGridSpec(
            num_scalar_prefetch=1,
            grid=(count // 2,),
            in_specs=[pl.BlockSpec((rows, depth), lambda q, me: (block, 0)), part(0), part(1)],
            out_specs=pl.BlockSpec((rows, 2 * width), lambda q, me: (0, q)),
        ),
        out_shape=jax.ShapeDtypeStruct((rows, columns), dtype),
        compiler_params=pltpu.CompilerParams(vmem_limit_bytes=VMEM),
        cost_estimate=pl.CostEstimate(
            flops=2 * rows * depth * columns, bytes_accessed=2 * depth * (rows + columns), transcendentals=0
        ),
        name="partial_product",
    )(me, sigma_hist, g_hist, g_hist)


def cubed(g, coupling):
    orbitals = coupling.shape[0]
    g3 = g.reshape(g.shape[0] // orbitals, orbitals, g.shape[1])
    return (g3 * g3 * g3 * coupling[None]).reshape(g.shape)


def fold_rows(x):
    return jnp.sum(x.reshape(x.shape[0] // 8, 8, x.shape[1]), axis=0)


def scale_of(squares, count):
    return 1.0 / jnp.sqrt(jnp.sum(squares) / count + 1e-06)


def own_first_kernel(me, memory, w, prev, coupling, cubic, squares):
    rows = memory.shape[0]
    g = jnp.dot(w[0, :, :rows], memory[...], preferred_element_type=F32)
    g += jnp.dot(w[0, :, rows:], prev[...], preferred_element_type=F32)
    c = cubed(g, coupling[...])
    cubic[...] = c
    squares[...] = fold_rows(c * c)


def own_next_kernel(count_all, me, memory, w, prev_cubic, prev_squares, coupling, cubic, squares):
    rows = memory.shape[0]
    prev = (prev_cubic[...] * scale_of(prev_squares[...], count_all)).astype(BF16)
    g = jnp.dot(w[0, :, :rows], memory[...], preferred_element_type=F32)
    g += jnp.dot(w[0, :, rows:], prev, preferred_element_type=F32)
    c = cubed(g, coupling[...])
    cubic[...] = c
    squares[...] = fold_rows(c * c)


def own_columns(me, order, memory, volterra, block, prev, prev_squares, coupling, count_all):
    rows, width = memory.shape
    full = lambda shape: pl.BlockSpec(shape, lambda i, me: (0, 0))
    w_spec = pl.BlockSpec((1, rows, 2 * rows), lambda i, me: (block, 0, 0))
    coupling_spec = pl.BlockSpec((coupling.shape[0], width), lambda i, me: (0, order.own(me[0])))
    if prev_squares is None:
        kernel = own_first_kernel
        in_specs = [full((rows, width)), w_spec, pl.BlockSpec((rows, width), lambda i, me: (0, order.own(me[0])))]
        operands = [memory, volterra, prev]
    else:
        kernel = functools.partial(own_next_kernel, count_all)
        in_specs = [full((rows, width)), w_spec, full((rows, width)), pl.BlockSpec(prev_squares.shape, lambda i, me: (0, 0, 0))]
        operands = [memory, volterra, prev, prev_squares]
    return pl.pallas_call(
        kernel,
        grid_spec=pltpu.PrefetchScalarGridSpec(
            num_scalar_prefetch=1,
            grid=(1,),
            in_specs=in_specs + [coupling_spec],
            out_specs=[full((rows, width)), full((8, width))],
        ),
        out_shape=[jax.ShapeDtypeStruct((rows, width), F32), jax.ShapeDtypeStruct((8, width), F32)],
        compiler_params=pltpu.CompilerParams(vmem_limit_bytes=VMEM),
        cost_estimate=pl.CostEstimate(
            flops=4 * rows * rows * width, bytes_accessed=4 * rows * rows + 8 * rows * width, transcendentals=0
        ),
        name="own_columns",
    )(me, *operands, coupling)


def finish_kernel(count_all, first, last, me, left, right, w, prev, squares, coupling, *refs):
    refs = list(refs)
    w_next = None if last else refs.pop(0)
    refs = refs if first else refs[2:]
    g_out, s_out = refs[:2]
    rows = left.shape[0]
    memory = jnp.concatenate([left[...], right[...]], axis=1)
    g = jnp.dot(w[0, :, :rows], memory, preferred_element_type=F32)
    if first:
        g += jnp.dot(w[0, :, rows:], prev[...], preferred_element_type=F32)
    else:
        g += prev[...]
    g_out[...] = g.astype(BF16)
    sigma = (cubed(g, coupling[...]) * scale_of(squares[...], count_all)).astype(BF16)
    s_out[...] = sigma
    if not last:
        refs[2][...] = jnp.dot(w_next[0, :, rows:], sigma, preferred_element_type=F32)


def finish(me, order, memory, volterra, block, prev, squares, coupling, outs, count_all, width):
    rows, columns = memory.shape[1], coupling.shape[1]
    blocks = volterra.shape[0]
    pair = 2 * width
    first, last = block == 0, block == blocks - 1
    place = lambda side: pl.BlockSpec((None, rows, width), lambda q, me: (order.owner(2 * q + side), 0, 0))
    w_spec = lambda k: pl.BlockSpec((1, rows, 2 * rows), lambda q, me: (k, 0, 0))
    straight = lambda size, row=0: pl.BlockSpec((size, pair), lambda q, me: (row, q))
    operands = [memory, memory, volterra, prev, squares, coupling]
    in_specs = [
        place(0),
        place(1),
        w_spec(block),
        straight(rows),
        pl.BlockSpec(squares.shape, lambda q, me: (0, 0, 0)),
        straight(coupling.shape[0]),
    ]
    out_specs = [straight(rows, block)] * 2
    out_shape = [jax.ShapeDtypeStruct((blocks * rows, columns), BF16)] * 2
    aliases = {}
    if not last:
        operands.append(volterra)
        in_specs.append(w_spec(block + 1))
        out_specs.append(straight(rows))
        out_shape.append(jax.ShapeDtypeStruct((rows, columns), F32))
    if not first:
        aliases = {1 + len(operands): 0, 2 + len(operands): 1}
        operands += outs
        in_specs += [pl.BlockSpec(memory_space=pl.ANY)] * 2
    return pl.pallas_call(
        functools.partial(finish_kernel, count_all, first, last),
        grid_spec=pltpu.PrefetchScalarGridSpec(
            num_scalar_prefetch=1, grid=(columns // pair,), in_specs=in_specs, out_specs=out_specs
        ),
        out_shape=out_shape,
        input_output_aliases=aliases,
        compiler_params=pltpu.CompilerParams(vmem_limit_bytes=VMEM),
        cost_estimate=pl.CostEstimate(
            flops=4 * rows * rows * columns, bytes_accessed=4 * rows * rows + 6 * rows * columns, transcendentals=0
        ),
        name="finish_block",
    )(me, *operands)


def per_device(past, second, g_hist, sigma_hist, volterra, sigma_edge, coupling):
    blocks, rows = volterra.shape[:2]
    columns = g_hist.shape[1]
    count_all = rows * columns * second * (past >> min(log2(past), log2(max(columns // 128, 2))))
    depth = min(log2(past), log2(max(columns // 128, 2)))
    width = columns >> depth
    even, odd = level_bits(past, depth)
    order = Order(depth)
    me = lax.axis_index("past").astype(jnp.int32).reshape(1)

    def swap(x, level):
        pairs = [(d, d ^ (1 << (odd if d % 2 else even)[level])) for d in range(past)]
        return lax.ppermute(x, "past", pairs)

    def reduced(block):
        send = partial_product(me, sigma_hist, g_hist, block, rows, order.sent, order.half, width, BF16)
        arrived = swap(send, 0)
        total = partial_product(me, sigma_hist, g_hist, block, rows, order.kept, order.half, width, F32)
        for level in range(1, depth):
            kept = total.shape[1] // 2
            send = (total[:, kept:] + arrived[:, kept:].astype(F32)).astype(BF16)
            total = total[:, :kept] + arrived[:, :kept].astype(F32)
            arrived = swap(send, level)
        total = total + arrived.astype(F32)
        for level in range(depth, len(even)):
            rounded = total.astype(BF16)
            total = rounded.astype(F32) + swap(rounded, level).astype(F32)
        return total.astype(BF16)

    own, whole, squares = [], [], []
    cubic, total = sigma_edge, None
    for block in range(blocks):
        own.append(reduced(block))
    for block in range(blocks):
        cubic, local = own_columns(me, order, own[block], volterra, block, cubic, total, coupling, count_all)
        total = lax.all_gather(local, ("past", "second"))
        squares.append(total)
        whole.append(lax.all_gather(own[block], "past"))
    outs, start = None, sigma_edge
    for block in range(blocks):
        results = finish(
            me, order, whole[block], volterra, block, start, squares[block], coupling, outs, count_all, width
        )
        outs = results[:2]
        start = results[2] if block < blocks - 1 else None
    return tuple(outs)


def solution(mesh):
    return jax.shard_map(
        functools.partial(per_device, mesh.shape["past"], mesh.shape["second"]),
        mesh=mesh,
        in_specs=(P("past", "second"), P(None, "past"), P(), P(None, "second"), P(None, "second")),
        out_specs=(P(None, "second"), P(None, "second")),
        check_vma=False,
    )
```

```python
import functools

import jax
import jax.numpy as jnp
from jax import lax
from jax.experimental import pallas as pl
from jax.experimental.pallas import tpu as pltpu
from jax.sharding import Mesh, PartitionSpec as P

VMEM = 48 * 1024 * 1024
F32 = jnp.float32
BF16 = jnp.bfloat16
PAST = ("outer", "chip", "core")


def cost(flops, size):
    return pl.CostEstimate(flops=flops, bytes_accessed=size, transcendentals=0)


def cubed(g, coupling):
    orbitals = coupling.shape[0]
    g3 = g.reshape(g.shape[0] // orbitals, orbitals, g.shape[1])
    return (g3 * g3 * g3 * coupling[None]).reshape(g.shape)


def fold_rows(x):
    return jnp.sum(x.reshape(x.shape[0] // 8, 8, x.shape[1]), axis=0)


def scale_of(squares, count):
    return 1.0 / jnp.sqrt(jnp.sum(squares) / count + 1e-06)


def partial_kernel(core, sigma, g, out):
    width = out.shape[2]
    product = jnp.dot(sigma[...], g[...], preferred_element_type=F32).astype(out.dtype)
    for j in range(out.shape[0]):
        out[j] = product[:, j * width : (j + 1) * width]


def partial_product(core, sigma_hist, g_hist, block, rows, chips, other, dtype):
    depth, columns = g_hist.shape
    width = columns // (2 * chips)
    group = min(chips, 2)
    steps = chips // group
    return pl.pallas_call(
        partial_kernel,
        grid_spec=pltpu.PrefetchScalarGridSpec(
            num_scalar_prefetch=1,
            grid=(steps,),
            in_specs=[
                pl.BlockSpec((rows, depth), lambda q, core: (block, 0)),
                pl.BlockSpec((depth, group * width), lambda q, core: (0, (core[0] ^ other) * steps + q)),
            ],
            out_specs=pl.BlockSpec((group, rows, width), lambda q, core: (q, 0, 0)),
        ),
        out_shape=jax.ShapeDtypeStruct((chips, rows, width), dtype),
        compiler_params=pltpu.CompilerParams(vmem_limit_bytes=VMEM),
        cost_estimate=cost(rows * depth * columns, depth * (2 * rows + columns)),
        name="partial_product",
    )(core, sigma_hist, g_hist)


def own_kernel(count_all, place, memory, w, prev, *refs):
    squares = refs[0] if count_all else None
    coupling, cubic, total = refs[-3:]
    rows = memory.shape[0]
    if count_all:
        before = (prev[...] * scale_of(squares[...], count_all)).astype(BF16)
    else:
        before = prev[...]
    g = jnp.dot(w[0, :, :rows], memory[...], preferred_element_type=F32)
    g += jnp.dot(w[0, :, rows:], before, preferred_element_type=F32)
    c = cubed(g, coupling[...])
    cubic[...] = c
    total[...] = fold_rows(c * c)


def own_columns(place, memory, volterra, block, prev, squares, coupling, count_all):
    rows, width = memory.shape
    full = lambda *shape: pl.BlockSpec(shape, lambda i, place: (0,) * len(shape))
    here = lambda size: pl.BlockSpec((size, width), lambda i, place: (0, place[0]))
    w_spec = pl.BlockSpec((1, rows, 2 * rows), lambda i, place: (block, 0, 0))
    in_specs, operands = [full(rows, width), w_spec], [memory, volterra, prev]
    if squares is None:
        in_specs.append(here(rows))
    else:
        in_specs += [full(rows, width), full(*squares.shape)]
        operands.append(squares)
    return pl.pallas_call(
        functools.partial(own_kernel, None if squares is None else count_all),
        grid_spec=pltpu.PrefetchScalarGridSpec(
            num_scalar_prefetch=1,
            grid=(1,),
            in_specs=in_specs + [here(coupling.shape[0])],
            out_specs=[full(rows, width), full(8, width)],
        ),
        out_shape=[jax.ShapeDtypeStruct((rows, width), F32), jax.ShapeDtypeStruct((8, width), F32)],
        compiler_params=pltpu.CompilerParams(vmem_limit_bytes=VMEM),
        cost_estimate=cost(4 * rows * rows * width, 4 * rows * rows + 8 * rows * width),
        name="own_columns",
    )(place, *operands, coupling)


def finish_kernel(count_all, first, last, core, left, right, w, prev, squares, coupling, *refs):
    refs = list(refs)
    w_next = None if last else refs.pop(0)
    refs = refs if first else refs[2:]
    g_out, s_out = refs[:2]
    rows = left.shape[0]
    memory = jnp.concatenate([left[...], right[...]], axis=1)
    g = jnp.dot(w[0, :, :rows], memory, preferred_element_type=F32)
    if first:
        g += jnp.dot(w[0, :, rows:], prev[...], preferred_element_type=F32)
    else:
        g += prev[...]
    g_out[...] = g.astype(BF16)
    sigma = (cubed(g, coupling[...]) * scale_of(squares[...], count_all)).astype(BF16)
    s_out[...] = sigma
    if not last:
        refs[2][...] = jnp.dot(w_next[0, :, rows:], sigma, preferred_element_type=F32)


def finish(core, memory, volterra, block, prev, squares, coupling, outs, count_all):
    rows, width = memory.shape[1:]
    columns = coupling.shape[1]
    chips = memory.shape[0] // 2
    blocks = volterra.shape[0]
    pair = 2 * width
    first, last = block == 0, block == blocks - 1

    def place(side):
        def at(q, core):
            column = 2 * q + side
            return ((column // chips) ^ core[0]) * chips + column % chips, 0, 0

        return pl.BlockSpec((None, rows, width), at)

    w_spec = lambda k: pl.BlockSpec((1, rows, 2 * rows), lambda q, core: (k, 0, 0))
    straight = lambda size, row=0: pl.BlockSpec((size, pair), lambda q, core: (row, q))
    operands = [memory, memory, volterra, prev, squares, coupling]
    in_specs = [
        place(0),
        place(1),
        w_spec(block),
        straight(rows),
        pl.BlockSpec(squares.shape, lambda q, core: (0, 0, 0)),
        straight(coupling.shape[0]),
    ]
    out_specs = [straight(rows, block)] * 2
    out_shape = [jax.ShapeDtypeStruct((blocks * rows, columns), BF16)] * 2
    aliases = {}
    if not last:
        operands.append(volterra)
        in_specs.append(w_spec(block + 1))
        out_specs.append(straight(rows))
        out_shape.append(jax.ShapeDtypeStruct((rows, columns), F32))
    if not first:
        aliases = {1 + len(operands): 0, 2 + len(operands): 1}
        operands += outs
        in_specs += [pl.BlockSpec(memory_space=pl.ANY)] * 2
    return pl.pallas_call(
        functools.partial(finish_kernel, count_all, first, last),
        grid_spec=pltpu.PrefetchScalarGridSpec(
            num_scalar_prefetch=1, grid=(columns // pair,), in_specs=in_specs, out_specs=out_specs
        ),
        out_shape=out_shape,
        input_output_aliases=aliases,
        compiler_params=pltpu.CompilerParams(vmem_limit_bytes=VMEM),
        cost_estimate=cost(4 * rows * rows * columns, 4 * rows * rows + 6 * rows * columns),
        name="finish_block",
    )(core, *operands)


def per_device(sizes, g_hist, sigma_hist, volterra, sigma_edge, coupling):
    outer, chips, cores, second = (sizes[axis] for axis in (*PAST, "second"))
    blocks, rows = volterra.shape[:2]
    columns = g_hist.shape[1]
    count_all = rows * columns * second * outer
    core_id = lax.axis_index("core").astype(jnp.int32)
    core = core_id.reshape(1)
    place = (core_id * chips + lax.axis_index("chip").astype(jnp.int32)).reshape(1)
    everyone = outer * chips * cores * second

    def swap_cores(x):
        return lax.ppermute(x, "core", [(0, 1), (1, 0)])

    def reduced(block):
        send = partial_product(core, sigma_hist, g_hist, block, rows, chips, 1, BF16)
        arrived = swap_cores(send)
        kept = partial_product(core, sigma_hist, g_hist, block, rows, chips, 0, F32)
        both = (kept + arrived.astype(F32)).astype(BF16)
        parts = lax.all_to_all(both, "chip", 0, 0)
        total = jnp.sum(parts.astype(F32), axis=0)
        if outer > 1:
            total = lax.psum(total, "outer")
        return total.astype(BF16)

    def gathered(piece):
        mine = lax.all_to_all(jnp.broadcast_to(piece, (chips,) + piece.shape), "chip", 0, 0)
        return jnp.concatenate([mine, swap_cores(mine)], axis=0)

    def shared(squares):
        copies = jnp.broadcast_to(squares, (everyone,) + squares.shape)
        return lax.all_to_all(copies, (*PAST, "second"), 0, 0)

    own = [reduced(block) for block in range(blocks)]
    whole, squares = [], []
    cubic, total = sigma_edge, None
    for block in range(blocks):
        cubic, local = own_columns(place, own[block], volterra, block, cubic, total, coupling, count_all)
        whole.append(gathered(own[block]))
        total = shared(local)
        squares.append(total)
    outs, start = None, sigma_edge
    for block in range(blocks):
        results = finish(core, whole[block], volterra, block, start, squares[block], coupling, outs, count_all)
        outs = results[:2]
        start = results[2] if block < blocks - 1 else None
    return tuple(outs)


def solution(mesh):
    past, second = mesh.shape["past"], mesh.shape["second"]
    chips = min(past // 2, 4)
    split = Mesh(mesh.devices.reshape(past // (2 * chips), chips, 2, second), (*PAST, "second"))
    return jax.shard_map(
        functools.partial(per_device, dict(split.shape)),
        mesh=split,
        in_specs=(P(PAST, "second"), P(None, PAST), P(), P(None, "second"), P(None, "second")),
        out_specs=(P(None, "second"), P(None, "second")),
        check_vma=False,
    )
```

```python
import functools

import jax
import jax.numpy as jnp
from jax import lax
from jax.experimental import pallas as pl
from jax.experimental.pallas import tpu as pltpu
from jax.sharding import PartitionSpec as P

VMEM = 20 * 1024 * 1024
F32 = jnp.float32
BF16 = jnp.bfloat16
EPS = 1e-06
BINOMIAL = (1.0, 6.0, 15.0, 20.0, 15.0, 6.0, 1.0)

WHOLE = pl.BlockSpec(memory_space=pltpu.VMEM)
FAR = pl.BlockSpec(memory_space=pl.ANY)
SCALAR = pl.BlockSpec(memory_space=pltpu.SMEM)


def log2(n):
    bits = n.bit_length() - 1
    assert n == 1 << bits
    return bits


def call(kernel, name, flops, size, **kwargs):
    return pl.pallas_call(
        kernel,
        name=name,
        compiler_params=pltpu.CompilerParams(vmem_limit_bytes=VMEM),
        cost_estimate=pl.CostEstimate(flops=flops, bytes_accessed=size, transcendentals=0),
        **kwargs,
    )


class Place:
    def __init__(self, me, bits):
        low, high = (me >> 1) & 1, (me >> (bits - 1)) & 1
        self.core = me & 1
        self.side = jnp.where(self.core == 1, high, low)
        self.other_side = jnp.where(self.core == 1, low, high)

    def quarter(self):
        return self.core * 2 + self.side

    def slot(self, quarter):
        same = (quarter >> 1) == self.core
        return jnp.where(same, (quarter & 1) ^ self.side, 2 + ((quarter & 1) ^ self.other_side))


def product(me, sigma, g, block, rows, half, bits, send, after=None):
    load_sigma, load_g = sigma.shape[0] != rows, g.shape[1] != half
    depth = g.shape[0]
    quarter = half // 2
    dtype = BF16 if send else F32
    pieces = 4 if load_sigma and load_g else 2
    out_shape = [jax.ShapeDtypeStruct((2, rows, quarter), dtype)]
    if load_sigma:
        out_shape.append(jax.ShapeDtypeStruct((rows, depth), BF16))
    if load_g:
        out_shape.append(jax.ShapeDtypeStruct((depth, half), BF16))

    def kernel(me_ref, sigma_ref, g_ref, *refs):
        refs = list(refs)
        if after is not None:
            refs.pop(0)
        out = refs.pop(0)
        sigma_v = refs.pop(0) if load_sigma else sigma_ref
        g_v = refs.pop(0) if load_g else g_ref
        total, sems = refs
        place = Place(me_ref[0], bits)
        first = pl.multiple_of((place.core ^ int(send)) * half, half)
        side = place.other_side if send else place.side

        def put(j, value):
            out[1 ^ j ^ side] = value.astype(dtype)

        if load_sigma and load_g:
            chunk = depth // pieces
            copies = []
            for k in range(pieces):
                at = pl.ds(k * chunk, chunk)
                copies.append(
                    (
                        pltpu.make_async_copy(
                            sigma_ref.at[pl.ds(block * rows, rows), at], sigma_v.at[:, at], sems.at[2 * k]
                        ),
                        pltpu.make_async_copy(g_ref.at[at, pl.ds(first, half)], g_v.at[at, :], sems.at[2 * k + 1]),
                    )
                )
            for pair in copies:
                for copy in pair:
                    copy.start()
            for k in range(pieces):
                for copy in copies[k]:
                    copy.wait()
                at = pl.ds(k * chunk, chunk)
                term = jnp.dot(sigma_v[:, at], g_v[at, :], preferred_element_type=F32)
                if k == 0:
                    total[...] = term
                elif k < pieces - 1:
                    total[...] += term
                else:
                    term += total[...]
                    for j in range(2):
                        put(j, term[:, j * quarter : (j + 1) * quarter])
        elif load_g:
            copies = [
                pltpu.make_async_copy(
                    g_ref.at[:, pl.ds(first + j * quarter, quarter)], g_v.at[:, pl.ds(j * quarter, quarter)], sems.at[j]
                )
                for j in range(2)
            ]
            for copy in copies:
                copy.start()
            for j in range(2):
                copies[j].wait()
                put(j, jnp.dot(sigma_v[...], g_v[:, pl.ds(j * quarter, quarter)], preferred_element_type=F32))
        elif load_sigma:
            tall = rows // 2
            copies = [
                pltpu.make_async_copy(
                    sigma_ref.at[pl.ds(block * rows + i * tall, tall), :], sigma_v.at[pl.ds(i * tall, tall), :], sems.at[i]
                )
                for i in range(2)
            ]
            for copy in copies:
                copy.start()
            for i in range(2):
                copies[i].wait()
                here = pl.ds(i * tall, tall)
                term = jnp.dot(sigma_v[here, :], g_v[...], preferred_element_type=F32).astype(dtype)
                for j in range(2):
                    out[1 ^ j ^ side, here, :] = term[:, j * quarter : (j + 1) * quarter]
        else:
            term = jnp.dot(sigma_v[...], g_v[...], preferred_element_type=F32)
            for j in range(2):
                put(j, term[:, j * quarter : (j + 1) * quarter])

    return call(
        kernel,
        "memory_product",
        2 * rows * depth * half,
        2 * depth * (rows * load_sigma + half * load_g),
        in_specs=[SCALAR, FAR if load_sigma else WHOLE, FAR if load_g else WHOLE] + [FAR] * (after is not None),
        out_specs=[WHOLE] * len(out_shape),
        out_shape=out_shape,
        scratch_shapes=[pltpu.VMEM((rows, half), F32), pltpu.SemaphoreType.DMA((2 * pieces,))],
    )(me, sigma, g, *([] if after is None else [after]))


def cubed(g, coupling):
    orbitals = coupling.shape[0]
    g3 = g.reshape(g.shape[0] // orbitals, orbitals, g.shape[1])
    return (g3 * g3 * g3 * coupling[None]).reshape(g.shape)


def folded(x):
    line = jnp.sum(x, axis=0, keepdims=True)
    parts = [line[:, i : i + 128] for i in range(0, line.shape[1], 128)]
    return functools.reduce(lambda a, b: a + b, parts)


def own_first(me, memory, volterra, edge, coupling, bits):
    rows, quarter = memory.shape

    def kernel(me_ref, memory, w, edge, coupling, response, squares):
        at = pl.ds(pl.multiple_of(Place(me_ref[0], bits).quarter() * quarter, quarter), quarter)
        g = jnp.dot(w[0, :, :rows], memory[...], preferred_element_type=F32)
        g += jnp.dot(w[0, :, rows:], edge[:, at], preferred_element_type=F32)
        cubic = cubed(g, coupling[:, at])
        line = folded(cubic * cubic * (1.0 / (rows * quarter)))
        squares[...] = line
        scale = lax.rsqrt(jnp.sum(line) + EPS)
        response[...] = jnp.dot(w[1, :, rows:], (cubic * scale).astype(BF16), preferred_element_type=F32)

    return call(
        kernel,
        "own_first",
        6 * rows * rows * quarter,
        8 * rows * rows,
        in_specs=[SCALAR] + [WHOLE] * 4,
        out_specs=[WHOLE] * 2,
        out_shape=[jax.ShapeDtypeStruct((rows, quarter), F32), jax.ShapeDtypeStruct((1, 128), F32)],
    )(me, memory, volterra, edge, coupling)


def own_second(me, memory, volterra, response, squares, coupling, bits):
    rows, quarter = memory.shape
    orbitals = coupling.shape[0]

    def kernel(me_ref, memory, w, response, squares, coupling, out):
        at = pl.ds(pl.multiple_of(Place(me_ref[0], bits).quarter() * quarter, quarter), quarter)
        c = coupling[:, at]
        c2 = (c * c * (1.0 / (rows * quarter)))[None]
        a = jnp.dot(w[1, :, :rows], memory[...], preferred_element_type=F32)
        b = response[...]
        a2, b2 = a * a, b * b
        a3, b3, a2b, ab2 = a2 * a, b2 * b, a2 * b, a * b2
        out[0:1, :] = squares[...]
        terms = (a3 * a3, a3 * a2b, a2b * a2b, a3 * b3, ab2 * ab2, ab2 * b3, b3 * b3)
        for k, term in enumerate(terms):
            weighted = (term.reshape(rows // orbitals, orbitals, quarter) * c2).reshape(rows, quarter)
            out[k + 1 : k + 2, :] = folded(weighted)

    return call(
        kernel,
        "own_second",
        2 * rows * rows * quarter,
        4 * rows * rows,
        in_specs=[SCALAR] + [WHOLE] * 5,
        out_specs=WHOLE,
        out_shape=jax.ShapeDtypeStruct((8, 128), F32),
    )(me, memory, volterra, response, squares, coupling)


def finish_first(me, memory, volterra, edge, coupling, bits):
    rows, quarter = memory.shape[1:]
    columns = coupling.shape[1]

    def kernel(me_ref, memory, w, edge, coupling, g_out, cubic):
        q = pl.program_id(0)
        g = jnp.dot(w[0, :, :rows], memory[Place(me_ref[0], bits).slot(q)], preferred_element_type=F32)
        g += jnp.dot(w[0, :, rows:], edge[...], preferred_element_type=F32)
        g_out[...] = g.astype(BF16)
        cubic[q] = cubed(g, coupling[...])

    straight = lambda size: pl.BlockSpec((size, quarter), lambda q: (0, q))
    return call(
        kernel,
        "finish_first",
        4 * rows * rows * columns,
        4 * rows * columns,
        grid=(4,),
        in_specs=[SCALAR, WHOLE, WHOLE, straight(rows), straight(coupling.shape[0])],
        out_specs=[straight(rows), WHOLE],
        out_shape=[
            jax.ShapeDtypeStruct((2 * rows, columns), BF16),
            jax.ShapeDtypeStruct((4, rows, quarter), F32),
        ],
    )(me, memory, volterra, edge, coupling)


def finish_second(me, memory, volterra, cubic, shares, coupling, g_first, bits):
    rows, quarter = memory.shape[1:]
    columns = coupling.shape[1]
    everyone = shares.shape[0]

    def kernel(me_ref, memory, w, cubic, shares, coupling, _, g_out, sigma, scales):
        q = pl.program_id(0)

        @pl.when(q == 0)
        def _():
            sums = jnp.sum(shares[...], axis=2, keepdims=True)
            means = sums[:, 0:1, :]
            mean = jnp.sum(means) / everyone
            ratio = jnp.sqrt((means + EPS) / (mean + EPS))
            power, series = jnp.ones_like(ratio), jnp.zeros_like(ratio)
            for k, weight in enumerate(BINOMIAL):
                series += weight * sums[:, k + 1 : k + 2, :] * power
                power = power * ratio
            scales[0] = 1.0 / jnp.sqrt(mean + EPS)
            scales[1] = 1.0 / jnp.sqrt(jnp.maximum(jnp.sum(series) / everyone, 0.0) + EPS)

        before = (cubic[q] * scales[0]).astype(BF16)
        g = jnp.dot(w[1, :, :rows], memory[Place(me_ref[0], bits).slot(q)], preferred_element_type=F32)
        g += jnp.dot(w[1, :, rows:], before, preferred_element_type=F32)
        g_out[...] = g.astype(BF16)
        sigma[:rows, :] = before
        sigma[rows:, :] = (cubed(g, coupling[...]) * scales[1]).astype(BF16)

    return call(
        kernel,
        "finish_second",
        4 * rows * rows * columns,
        10 * rows * columns,
        grid=(4,),
        in_specs=[
            SCALAR,
            WHOLE,
            WHOLE,
            WHOLE,
            WHOLE,
            pl.BlockSpec((coupling.shape[0], quarter), lambda q: (0, q)),
            FAR,
        ],
        out_specs=[
            pl.BlockSpec((rows, quarter), lambda q: (1, q)),
            pl.BlockSpec((2 * rows, quarter), lambda q: (0, q)),
        ],
        out_shape=[jax.ShapeDtypeStruct((2 * rows, columns), BF16)] * 2,
        scratch_shapes=[pltpu.SMEM((2,), F32)],
        input_output_aliases={6: 0},
    )(me, memory, volterra, cubic, shares, coupling, g_first)


def per_device(past, second, g_hist, sigma_hist, volterra, sigma_edge, coupling):
    blocks, rows = volterra.shape[:2]
    assert blocks == 2 and past >= 4
    bits = log2(past)
    half = g_hist.shape[1] // 2
    me = lax.axis_index("past").astype(jnp.int32).reshape(1)
    even = list(range(bits))
    odd = even[:1] + even[1:][::-1]

    def swap(x, level):
        pairs = [(d, d ^ (1 << (odd if d % 2 else even)[level])) for d in range(past)]
        return lax.ppermute(x, "past", pairs)

    def summed(kept, arrived, sent):
        total = kept[1] + arrived[1].astype(F32) + swap(sent, 1).astype(F32)
        for level in range(2, bits):
            rounded = total.astype(BF16)
            total = rounded.astype(F32) + swap(rounded, level).astype(F32)
        return total.astype(BF16)

    def passed_on(kept, arrived):
        return (kept[0] + arrived[0].astype(F32)).astype(BF16)

    def gathered(own):
        partner = swap(own, 1)
        return jnp.stack([own, partner, swap(own, 0), swap(partner, 0)])

    send, sigma_0, g_send = product(me, sigma_hist, g_hist, 0, rows, half, bits, True)
    arrived_0 = swap(send, 0)
    kept_0, g_keep = product(me, sigma_0, g_hist, 0, rows, half, bits, False)
    sent_0 = passed_on(kept_0, arrived_0)
    send, sigma_1 = product(me, sigma_hist, g_send, 1, rows, half, bits, True, after=sent_0)
    arrived_1 = swap(send, 0)
    (kept_1,) = product(me, sigma_1, g_keep, 1, rows, half, bits, False)
    sent_1 = passed_on(kept_1, arrived_1)

    own_0 = summed(kept_0, arrived_0, sent_0)
    own_1 = summed(kept_1, arrived_1, sent_1)
    response, squares = own_first(me, own_0, volterra, sigma_edge, coupling, bits)
    share = own_second(me, own_1, volterra, response, squares, coupling, bits)
    copies = jnp.broadcast_to(share, (past * second,) + share.shape)
    shares = lax.all_to_all(copies, ("past", "second"), 0, 0)

    g_first, cubic = finish_first(me, gathered(own_0), volterra, sigma_edge, coupling, bits)
    return tuple(finish_second(me, gathered(own_1), volterra, cubic, shares, coupling, g_first, bits))


def solution(mesh):
    return jax.shard_map(
        functools.partial(per_device, mesh.shape["past"], mesh.shape["second"]),
        mesh=mesh,
        in_specs=(P("past", "second"), P(None, "past"), P(), P(None, "second"), P(None, "second")),
        out_specs=(P(None, "second"), P(None, "second")),
        check_vma=False,
    )
```

```python
import functools

import jax
import jax.numpy as jnp
from jax import lax
from jax.experimental import pallas as pl
from jax.experimental.pallas import tpu as pltpu
from jax.sharding import PartitionSpec as P

VMEM = 20 * 1024 * 1024
F32 = jnp.float32
BF16 = jnp.bfloat16
EPS = 1e-06
BINOMIAL = (1.0, 6.0, 15.0, 20.0, 15.0, 6.0, 1.0)

WHOLE = pl.BlockSpec(memory_space=pltpu.VMEM)
FAR = pl.BlockSpec(memory_space=pl.ANY)
HBM = pl.BlockSpec(memory_space=pltpu.HBM)
SCALAR = pl.BlockSpec(memory_space=pltpu.SMEM)


def log2(n):
    bits = n.bit_length() - 1
    assert n == 1 << bits
    return bits


def call(kernel, name, **kwargs):
    return pl.pallas_call(
        kernel,
        name=name,
        compiler_params=pltpu.CompilerParams(vmem_limit_bytes=VMEM),
        cost_estimate=pl.CostEstimate(flops=1024, bytes_accessed=1024, transcendentals=0),
        **kwargs,
    )


class Place:
    def __init__(self, me, bits):
        low, high = (me >> 1) & 1, (me >> (bits - 1)) & 1
        self.core = me & 1
        self.side = jnp.where(self.core == 1, high, low)
        self.other_side = jnp.where(self.core == 1, low, high)

    def quarter(self):
        return self.core * 2 + self.side

    def quarter_of(self, slot):
        if slot < 2:
            return self.core * 2 + (self.side ^ slot)
        return (self.core ^ 1) * 2 + (self.other_side ^ (slot - 2))


def product(me, sigma, g, block, rows, half, bits, send, after=None):
    load_sigma, load_g = sigma.shape[0] != rows, g.shape[1] != half
    depth = g.shape[0]
    quarter = half // 2
    dtype = BF16 if send else F32
    pieces = 4 if load_sigma and load_g else 2
    out_shape = [jax.ShapeDtypeStruct((2, rows, quarter), dtype)]
    if load_sigma:
        out_shape.append(jax.ShapeDtypeStruct((rows, depth), BF16))
    if load_g:
        out_shape.append(jax.ShapeDtypeStruct((depth, half), BF16))

    def kernel(me_ref, sigma_ref, g_ref, *refs):
        refs = list(refs)
        if after is not None:
            refs.pop(0)
        out = refs.pop(0)
        sigma_v = refs.pop(0) if load_sigma else sigma_ref
        g_v = refs.pop(0) if load_g else g_ref
        total, sems = refs
        place = Place(me_ref[0], bits)
        first = pl.multiple_of((place.core ^ int(send)) * half, half)
        side = place.other_side if send else place.side

        def put(j, value):
            out[1 ^ j ^ side] = value.astype(dtype)

        if load_sigma and load_g:
            chunk = depth // pieces
            copies = []
            for k in range(pieces):
                at = pl.ds(k * chunk, chunk)
                copies.append(
                    (
                        pltpu.make_async_copy(
                            sigma_ref.at[pl.ds(block * rows, rows), at], sigma_v.at[:, at], sems.at[2 * k]
                        ),
                        pltpu.make_async_copy(g_ref.at[at, pl.ds(first, half)], g_v.at[at, :], sems.at[2 * k + 1]),
                    )
                )
            for pair in copies:
                for copy in pair:
                    copy.start()
            for k in range(pieces):
                for copy in copies[k]:
                    copy.wait()
                at = pl.ds(k * chunk, chunk)
                term = jnp.dot(sigma_v[:, at], g_v[at, :], preferred_element_type=F32)
                if k == 0:
                    total[...] = term
                elif k < pieces - 1:
                    total[...] += term
                else:
                    term += total[...]
                    for j in range(2):
                        put(j, term[:, j * quarter : (j + 1) * quarter])
        elif load_g:
            copies = [
                pltpu.make_async_copy(
                    g_ref.at[:, pl.ds(first + j * quarter, quarter)], g_v.at[:, pl.ds(j * quarter, quarter)], sems.at[j]
                )
                for j in range(2)
            ]
            for copy in copies:
                copy.start()
            for j in range(2):
                copies[j].wait()
                put(j, jnp.dot(sigma_v[...], g_v[:, pl.ds(j * quarter, quarter)], preferred_element_type=F32))
        elif load_sigma:
            tall = rows // 2
            copies = [
                pltpu.make_async_copy(
                    sigma_ref.at[pl.ds(block * rows + i * tall, tall), :], sigma_v.at[pl.ds(i * tall, tall), :], sems.at[i]
                )
                for i in range(2)
            ]
            for copy in copies:
                copy.start()
            for i in range(2):
                copies[i].wait()
                here = pl.ds(i * tall, tall)
                term = jnp.dot(sigma_v[here, :], g_v[...], preferred_element_type=F32).astype(dtype)
                for j in range(2):
                    out[1 ^ j ^ side, here, :] = term[:, j * quarter : (j + 1) * quarter]
        else:
            term = jnp.dot(sigma_v[...], g_v[...], preferred_element_type=F32)
            for j in range(2):
                put(j, term[:, j * quarter : (j + 1) * quarter])

    return call(
        kernel,
        "memory_product",
        in_specs=[SCALAR, HBM if load_sigma else WHOLE, HBM if load_g else WHOLE] + [FAR] * (after is not None),
        out_specs=[WHOLE] * len(out_shape),
        out_shape=out_shape,
        scratch_shapes=[pltpu.VMEM((rows, half), F32), pltpu.SemaphoreType.DMA((2 * pieces,))],
    )(me, sigma, g, *([] if after is None else [after]))


def cubed(g, coupling):
    orbitals = coupling.shape[0]
    g3 = g.reshape(g.shape[0] // orbitals, orbitals, g.shape[1])
    return (g3 * g3 * g3 * coupling[None]).reshape(g.shape)


def folded(x):
    line = jnp.sum(x, axis=0, keepdims=True)
    parts = [line[:, i : i + 128] for i in range(0, line.shape[1], 128)]
    return functools.reduce(lambda a, b: a + b, parts)


def columns_of(quarter, width):
    return pl.ds(pl.multiple_of(quarter * width, width), width)


def own_first(me, mine, theirs, volterra, edge, coupling, bits):
    rows, width = mine.shape

    def kernel(me_ref, mine, theirs, w, edge, coupling, memory, response, squares):
        at = columns_of(Place(me_ref[0], bits).quarter(), width)
        summed = (mine[...].astype(F32) + theirs[...].astype(F32)).astype(BF16)
        memory[...] = summed
        g = jnp.dot(w[0, :, :rows], summed, preferred_element_type=F32)
        g += jnp.dot(w[0, :, rows:], edge[:, at], preferred_element_type=F32)
        cubic = cubed(g, coupling[:, at])
        line = folded(cubic * cubic * (1.0 / (rows * width)))
        squares[...] = line
        scale = lax.rsqrt(jnp.sum(line) + EPS)
        response[...] = jnp.dot(w[1, :, rows:], (cubic * scale).astype(BF16), preferred_element_type=F32)

    return call(
        kernel,
        "own_first",
        in_specs=[SCALAR] + [WHOLE] * 5,
        out_specs=[WHOLE] * 3,
        out_shape=[
            jax.ShapeDtypeStruct((rows, width), BF16),
            jax.ShapeDtypeStruct((rows, width), F32),
            jax.ShapeDtypeStruct((1, 128), F32),
        ],
    )(me, mine, theirs, volterra, edge, coupling)


def own_second(me, mine, theirs, volterra, response, squares, coupling, bits):
    rows, width = mine.shape
    orbitals = coupling.shape[0]

    def kernel(me_ref, mine, theirs, w, response, squares, coupling, memory, out):
        at = columns_of(Place(me_ref[0], bits).quarter(), width)
        summed = (mine[...].astype(F32) + theirs[...].astype(F32)).astype(BF16)
        memory[...] = summed
        c = coupling[:, at]
        c2 = (c * c * (1.0 / (rows * width)))[None]
        a = jnp.dot(w[1, :, :rows], summed, preferred_element_type=F32)
        b = response[...]
        a2, b2 = a * a, b * b
        a3, b3, a2b, ab2 = a2 * a, b2 * b, a2 * b, a * b2
        out[0:1, :] = squares[...]
        terms = (a3 * a3, a3 * a2b, a2b * a2b, a3 * b3, ab2 * ab2, ab2 * b3, b3 * b3)
        for k, term in enumerate(terms):
            weighted = (term.reshape(rows // orbitals, orbitals, width) * c2).reshape(rows, width)
            out[k + 1 : k + 2, :] = folded(weighted)

    return call(
        kernel,
        "own_second",
        in_specs=[SCALAR] + [WHOLE] * 6,
        out_specs=[WHOLE] * 2,
        out_shape=[jax.ShapeDtypeStruct((rows, width), BF16), jax.ShapeDtypeStruct((8, 128), F32)],
    )(me, mine, theirs, volterra, response, squares, coupling)


def finish_first(me, pieces, volterra, edge, coupling, bits):
    rows, width = pieces[0].shape
    columns = coupling.shape[1]

    def kernel(me_ref, *refs):
        pieces, (w, edge, coupling, g_out, cubic, held, sems) = refs[:4], refs[4:]
        place = Place(me_ref[0], bits)
        copies = []
        for slot in range(4):
            at = columns_of(place.quarter_of(slot), width)
            g = jnp.dot(w[0, :, :rows], pieces[slot][...], preferred_element_type=F32)
            g += jnp.dot(w[0, :, rows:], edge[:, at], preferred_element_type=F32)
            held[slot] = g.astype(BF16)
            copies.append(pltpu.make_async_copy(held.at[slot], g_out.at[pl.ds(0, rows), at], sems.at[slot]))
            copies[-1].start()
            cubic[slot] = cubed(g, coupling[:, at])
        for copy in copies:
            copy.wait()

    return call(
        kernel,
        "finish_first",
        in_specs=[SCALAR] + [WHOLE] * 7,
        out_specs=[HBM, WHOLE],
        out_shape=[jax.ShapeDtypeStruct((2 * rows, columns), BF16), jax.ShapeDtypeStruct((4, rows, width), F32)],
        scratch_shapes=[pltpu.VMEM((4, rows, width), BF16), pltpu.SemaphoreType.DMA((4,))],
    )(me, *pieces, volterra, edge, coupling)


def finish_second(me, pieces, volterra, cubic, shares, coupling, g_first, bits):
    rows, width = pieces[0].shape
    columns = coupling.shape[1]
    everyone = shares.shape[0]

    def kernel(me_ref, *refs):
        pieces, (w, cubic, shares, coupling, _, g_out, sigma, g_held, s_held, sems) = refs[:4], refs[4:]
        place = Place(me_ref[0], bits)
        sums = jnp.sum(shares[...], axis=2, keepdims=True)
        means = sums[:, 0:1, :]
        mean = jnp.sum(means) / everyone
        ratio = jnp.sqrt((means + EPS) / (mean + EPS))
        power, series = jnp.ones_like(ratio), jnp.zeros_like(ratio)
        for k, weight in enumerate(BINOMIAL):
            series += weight * sums[:, k + 1 : k + 2, :] * power
            power = power * ratio
        scale_0 = 1.0 / jnp.sqrt(mean + EPS)
        scale_1 = 1.0 / jnp.sqrt(jnp.maximum(jnp.sum(series) / everyone, 0.0) + EPS)

        copies = []

        def write(value, held, slot, out, block, at):
            held[slot] = value
            sem = sems.at[len(copies)]
            copies.append(pltpu.make_async_copy(held.at[slot], out.at[pl.ds(block * rows, rows), at], sem))
            copies[-1].start()

        for slot in range(4):
            at = columns_of(place.quarter_of(slot), width)
            before = (cubic[slot] * scale_0).astype(BF16)
            write(before, s_held, slot, sigma, 0, at)
            g = jnp.dot(w[1, :, :rows], pieces[slot][...], preferred_element_type=F32)
            g += jnp.dot(w[1, :, rows:], before, preferred_element_type=F32)
            write(g.astype(BF16), g_held, slot, g_out, 1, at)
            write((cubed(g, coupling[:, at]) * scale_1).astype(BF16), s_held, 4 + slot, sigma, 1, at)
        for copy in copies:
            copy.wait()

    return call(
        kernel,
        "finish_second",
        in_specs=[SCALAR] + [WHOLE] * 8 + [HBM],
        out_specs=[HBM, HBM],
        out_shape=[jax.ShapeDtypeStruct((2 * rows, columns), BF16)] * 2,
        scratch_shapes=[
            pltpu.VMEM((4, rows, width), BF16),
            pltpu.VMEM((8, rows, width), BF16),
            pltpu.SemaphoreType.DMA((12,)),
        ],
        input_output_aliases={9: 0},
    )(me, *pieces, volterra, cubic, shares, coupling, g_first)


def per_device(past, second, g_hist, sigma_hist, volterra, sigma_edge, coupling):
    blocks, rows = volterra.shape[:2]
    assert blocks == 2 and past >= 8
    bits = log2(past)
    half = g_hist.shape[1] // 2
    me = lax.axis_index("past").astype(jnp.int32).reshape(1)
    even = list(range(bits))
    odd = even[:1] + even[1:][::-1]

    def swap(x, level):
        pairs = [(d, d ^ (1 << (odd if d % 2 else even)[level])) for d in range(past)]
        return lax.ppermute(x, "past", pairs)

    def exchanged(kept, arrived, sent):
        total = kept[1] + arrived[1].astype(F32) + swap(sent, 1).astype(F32)
        for level in range(2, bits):
            mine = total.astype(BF16)
            theirs = swap(mine, level)
            total = mine.astype(F32) + theirs.astype(F32)
        return mine, theirs

    def passed_on(kept, arrived):
        return (kept[0] + arrived[0].astype(F32)).astype(BF16)

    def gathered(own):
        partner = swap(own, 1)
        return [own, partner, swap(own, 0), swap(partner, 0)]

    send, sigma_0, g_send = product(me, sigma_hist, g_hist, 0, rows, half, bits, True)
    arrived_0 = swap(send, 0)
    kept_0, g_keep = product(me, sigma_0, g_hist, 0, rows, half, bits, False)
    sent_0 = passed_on(kept_0, arrived_0)
    send, sigma_1 = product(me, sigma_hist, g_send, 1, rows, half, bits, True, after=sent_0)
    arrived_1 = swap(send, 0)
    (kept_1,) = product(me, sigma_1, g_keep, 1, rows, half, bits, False)
    sent_1 = passed_on(kept_1, arrived_1)

    mine, theirs = exchanged(kept_0, arrived_0, sent_0)
    own_0, response, squares = own_first(me, mine, theirs, volterra, sigma_edge, coupling, bits)
    mine, theirs = exchanged(kept_1, arrived_1, sent_1)
    own_1, share = own_second(me, mine, theirs, volterra, response, squares, coupling, bits)
    copies = jnp.broadcast_to(share, (past * second,) + share.shape)
    shares = lax.all_to_all(copies, ("past", "second"), 0, 0)

    g_first, cubic = finish_first(me, gathered(own_0), volterra, sigma_edge, coupling, bits)
    return tuple(finish_second(me, gathered(own_1), volterra, cubic, shares, coupling, g_first, bits))


def solution(mesh):
    return jax.shard_map(
        functools.partial(per_device, mesh.shape["past"], mesh.shape["second"]),
        mesh=mesh,
        in_specs=(P("past", "second"), P(None, "past"), P(), P(None, "second"), P(None, "second")),
        out_specs=(P(None, "second"), P(None, "second")),
        check_vma=False,
    )
```

```python
import functools

import jax
import jax.numpy as jnp
from jax import lax
from jax.experimental import pallas as pl
from jax.experimental.pallas import tpu as pltpu
from jax.sharding import PartitionSpec as P

VMEM = 20 * 1024 * 1024
F32 = jnp.float32
BF16 = jnp.bfloat16
EPS = 1e-06
BINOMIAL = (1.0, 6.0, 15.0, 20.0, 15.0, 6.0, 1.0)

WHOLE = pl.BlockSpec(memory_space=pltpu.VMEM)
FAR = pl.BlockSpec(memory_space=pl.ANY)
HBM = pl.BlockSpec(memory_space=pltpu.HBM)
SCALAR = pl.BlockSpec(memory_space=pltpu.SMEM)


def log2(n):
    bits = n.bit_length() - 1
    assert n == 1 << bits
    return bits


def near(shape, dtype):
    return pltpu.VMEM(shape, dtype)


def far(x):
    return pltpu.with_memory_space_constraint(x, pltpu.HBM)


def call(kernel, name, **kwargs):
    return pl.pallas_call(
        kernel,
        name=name,
        compiler_params=pltpu.CompilerParams(vmem_limit_bytes=VMEM),
        cost_estimate=pl.CostEstimate(flops=1024, bytes_accessed=1024, transcendentals=0),
        **kwargs,
    )


class Place:
    def __init__(self, me, bits):
        low, high = (me >> 1) & 1, (me >> (bits - 1)) & 1
        self.core = me & 1
        self.side = jnp.where(self.core == 1, high, low)
        self.other_side = jnp.where(self.core == 1, low, high)

    def quarter(self):
        return self.core * 2 + self.side

    def quarter_of(self, slot):
        if slot < 2:
            return self.core * 2 + (self.side ^ slot)
        return (self.core ^ 1) * 2 + (self.other_side ^ (slot - 2))


def product(me, sigma, g, block, rows, half, bits, send, after=None):
    load_sigma, load_g = sigma.shape[0] != rows, g.shape[1] != half
    depth = g.shape[0]
    quarter = half // 2
    dtype = BF16 if send else F32
    pieces = 4 if load_sigma and load_g else 2
    out_shape = [near((2, rows, quarter), dtype)]
    if load_sigma:
        out_shape.append(near((rows, depth), BF16))
    if load_g:
        out_shape.append(near((depth, half), BF16))

    def kernel(me_ref, sigma_ref, g_ref, *refs):
        refs = list(refs)
        if after is not None:
            refs.pop(0)
        out = refs.pop(0)
        sigma_v = refs.pop(0) if load_sigma else sigma_ref
        g_v = refs.pop(0) if load_g else g_ref
        total, sems = refs
        place = Place(me_ref[0], bits)
        first = pl.multiple_of((place.core ^ int(send)) * half, half)
        side = place.other_side if send else place.side

        def put(j, value):
            out[1 ^ j ^ side] = value.astype(dtype)

        if load_sigma and load_g:
            chunk = depth // pieces
            copies = []
            for k in range(pieces):
                at = pl.ds(k * chunk, chunk)
                copies.append(
                    (
                        pltpu.make_async_copy(
                            sigma_ref.at[pl.ds(block * rows, rows), at], sigma_v.at[:, at], sems.at[2 * k]
                        ),
                        pltpu.make_async_copy(g_ref.at[at, pl.ds(first, half)], g_v.at[at, :], sems.at[2 * k + 1]),
                    )
                )
            for pair in copies:
                for copy in pair:
                    copy.start()
            for k in range(pieces):
                for copy in copies[k]:
                    copy.wait()
                at = pl.ds(k * chunk, chunk)
                term = jnp.dot(sigma_v[:, at], g_v[at, :], preferred_element_type=F32)
                if k == 0:
                    total[...] = term
                elif k < pieces - 1:
                    total[...] += term
                else:
                    term += total[...]
                    for j in range(2):
                        put(j, term[:, j * quarter : (j + 1) * quarter])
        elif load_g:
            copies = [
                pltpu.make_async_copy(
                    g_ref.at[:, pl.ds(first + j * quarter, quarter)], g_v.at[:, pl.ds(j * quarter, quarter)], sems.at[j]
                )
                for j in range(2)
            ]
            for copy in copies:
                copy.start()
            for j in range(2):
                copies[j].wait()
                put(j, jnp.dot(sigma_v[...], g_v[:, pl.ds(j * quarter, quarter)], preferred_element_type=F32))
        elif load_sigma:
            tall = rows // 2
            copies = [
                pltpu.make_async_copy(
                    sigma_ref.at[pl.ds(block * rows + i * tall, tall), :], sigma_v.at[pl.ds(i * tall, tall), :], sems.at[i]
                )
                for i in range(2)
            ]
            for copy in copies:
                copy.start()
            for i in range(2):
                copies[i].wait()
                here = pl.ds(i * tall, tall)
                term = jnp.dot(sigma_v[here, :], g_v[...], preferred_element_type=F32).astype(dtype)
                for j in range(2):
                    out[1 ^ j ^ side, here, :] = term[:, j * quarter : (j + 1) * quarter]
        else:
            term = jnp.dot(sigma_v[...], g_v[...], preferred_element_type=F32)
            for j in range(2):
                put(j, term[:, j * quarter : (j + 1) * quarter])

    return call(
        kernel,
        "memory_product",
        in_specs=[SCALAR, HBM if load_sigma else WHOLE, HBM if load_g else WHOLE] + [FAR] * (after is not None),
        out_specs=[WHOLE] * len(out_shape),
        out_shape=out_shape,
        scratch_shapes=[pltpu.VMEM((rows, half), F32), pltpu.SemaphoreType.DMA((2 * pieces,))],
    )(me, far(sigma) if load_sigma else sigma, far(g) if load_g else g, *([] if after is None else [after]))


def combined(kept, arrived, more, after):
    rows, width = more.shape
    if after is None:
        return (kept[1] + arrived[1].astype(F32) + more.astype(F32)).astype(BF16)

    def kernel(kept, arrived, more, _, out):
        out[...] = (kept[1] + arrived[1].astype(F32) + more[...].astype(F32)).astype(BF16)

    return call(
        kernel, "combined", in_specs=[WHOLE] * 3 + [FAR], out_specs=WHOLE, out_shape=near((rows, width), BF16)
    )(kept, arrived, more, after)


def cubed(g, coupling):
    orbitals = coupling.shape[0]
    g3 = g.reshape(g.shape[0] // orbitals, orbitals, g.shape[1])
    return (g3 * g3 * g3 * coupling[None]).reshape(g.shape)


def folded(x):
    line = jnp.sum(x, axis=0, keepdims=True)
    parts = [line[:, i : i + 128] for i in range(0, line.shape[1], 128)]
    return functools.reduce(lambda a, b: a + b, parts)


def columns_of(quarter, width):
    return pl.ds(pl.multiple_of(quarter * width, width), width)


def over_halves(x):
    while x.shape[0] > 1:
        half = x.shape[0] // 2
        x = x[:half] + x[half:]
    return x


def own_first(me, mine, theirs, volterra, edge, coupling, bits, after):
    rows, width = mine.shape

    def kernel(me_ref, mine, theirs, w, edge, coupling, _, memory, response, squares):
        at = columns_of(Place(me_ref[0], bits).quarter(), width)
        summed = (mine[...].astype(F32) + theirs[...].astype(F32)).astype(BF16)
        memory[...] = summed
        g = jnp.dot(w[0, :, :rows], summed, preferred_element_type=F32)
        g += jnp.dot(w[0, :, rows:], edge[:, at], preferred_element_type=F32)
        cubic = cubed(g, coupling[:, at])
        line = folded(cubic * cubic * (1.0 / (rows * width)))
        squares[...] = line
        scale = lax.rsqrt(jnp.sum(line) + EPS)
        response[...] = jnp.dot(w[1, :, rows:], (cubic * scale).astype(BF16), preferred_element_type=F32)

    return call(
        kernel,
        "own_first",
        in_specs=[SCALAR] + [WHOLE] * 5 + [FAR],
        out_specs=[WHOLE] * 3,
        out_shape=[
            near((rows, width), BF16),
            near((rows, width), F32),
            near((1, 128), F32),
        ],
    )(me, mine, theirs, volterra, edge, coupling, after)


def own_second(me, mine, theirs, volterra, response, squares, coupling, bits):
    rows, width = mine.shape
    orbitals = coupling.shape[0]

    def kernel(me_ref, mine, theirs, w, response, squares, coupling, memory, out):
        at = columns_of(Place(me_ref[0], bits).quarter(), width)
        summed = (mine[...].astype(F32) + theirs[...].astype(F32)).astype(BF16)
        memory[...] = summed
        c = coupling[:, at]
        c2 = (c * c * (1.0 / (rows * width)))[None]
        a = jnp.dot(w[1, :, :rows], summed, preferred_element_type=F32)
        b = response[...]
        a2, b2 = a * a, b * b
        a3, b3, a2b, ab2 = a2 * a, b2 * b, a2 * b, a * b2
        lines = [squares[...]]
        terms = (a3 * a3, a3 * a2b, a2b * a2b, a3 * b3, ab2 * ab2, ab2 * b3, b3 * b3)
        for term in terms:
            weighted = (term.reshape(rows // orbitals, orbitals, width) * c2).reshape(rows, width)
            lines.append(folded(weighted))
        out[0] = jnp.concatenate(lines, axis=0)

    return call(
        kernel,
        "own_second",
        in_specs=[SCALAR] + [WHOLE] * 6,
        out_specs=[WHOLE] * 2,
        out_shape=[near((rows, width), BF16), near((1, 8, 128), F32)],
    )(me, mine, theirs, volterra, response, squares, coupling)


def finish_first(me, pieces, volterra, edge, coupling, bits):
    rows, width = pieces[0].shape
    columns = coupling.shape[1]

    def kernel(me_ref, *refs):
        pieces, (w, edge, coupling, g_out, cubic, held, sems) = refs[:4], refs[4:]
        place = Place(me_ref[0], bits)
        copies = []
        for slot in range(4):
            at = columns_of(place.quarter_of(slot), width)
            g = jnp.dot(w[0, :, :rows], pieces[slot][...], preferred_element_type=F32)
            g += jnp.dot(w[0, :, rows:], edge[:, at], preferred_element_type=F32)
            held[slot] = g.astype(BF16)
            copies.append(pltpu.make_async_copy(held.at[slot], g_out.at[pl.ds(0, rows), at], sems.at[slot]))
            copies[-1].start()
            cubic[slot] = cubed(g, coupling[:, at])
        for copy in copies:
            copy.wait()

    return call(
        kernel,
        "finish_first",
        in_specs=[SCALAR] + [WHOLE] * 7,
        out_specs=[HBM, WHOLE],
        out_shape=[
            jax.ShapeDtypeStruct((2 * rows, columns), BF16),
            near((4, rows, width), F32),
        ],
        scratch_shapes=[pltpu.VMEM((4, rows, width), BF16), pltpu.SemaphoreType.DMA((4,))],
    )(me, *pieces, volterra, edge, coupling)


def finish_second(me, pieces, volterra, cubic, shares, coupling, g_first, bits):
    rows, width = pieces[0].shape
    columns = coupling.shape[1]
    everyone = shares.shape[0]

    def kernel(me_ref, *refs):
        pieces, (w, cubic, shares, coupling, _, g_out, sigma, g_held, s_held, sems) = refs[:4], refs[4:]
        place = Place(me_ref[0], bits)
        sums = jnp.sum(shares[...], axis=2, keepdims=True)
        means = sums[:, 0:1, :]
        mean = jnp.sum(over_halves(means)) / everyone
        ratio = jnp.sqrt((means + EPS) / (mean + EPS))
        power, series = jnp.ones_like(ratio), jnp.zeros_like(ratio)
        for k, weight in enumerate(BINOMIAL):
            series += weight * sums[:, k + 1 : k + 2, :] * power
            power = power * ratio
        scale_0 = 1.0 / jnp.sqrt(mean + EPS)
        scale_1 = 1.0 / jnp.sqrt(jnp.maximum(jnp.sum(over_halves(series)) / everyone, 0.0) + EPS)

        copies = []

        def write(value, held, slot, out, block, at):
            held[slot] = value
            sem = sems.at[len(copies)]
            copies.append(pltpu.make_async_copy(held.at[slot], out.at[pl.ds(block * rows, rows), at], sem))
            copies[-1].start()

        for slot in range(4):
            at = columns_of(place.quarter_of(slot), width)
            before = (cubic[slot] * scale_0).astype(BF16)
            write(before, s_held, slot, sigma, 0, at)
            g = jnp.dot(w[1, :, :rows], pieces[slot][...], preferred_element_type=F32)
            g += jnp.dot(w[1, :, rows:], before, preferred_element_type=F32)
            write(g.astype(BF16), g_held, slot, g_out, 1, at)
            write((cubed(g, coupling[:, at]) * scale_1).astype(BF16), s_held, 4 + slot, sigma, 1, at)
        for copy in copies:
            copy.wait()

    return call(
        kernel,
        "finish_second",
        in_specs=[SCALAR] + [WHOLE] * 8 + [HBM],
        out_specs=[HBM, HBM],
        out_shape=[jax.ShapeDtypeStruct((2 * rows, columns), BF16)] * 2,
        scratch_shapes=[
            pltpu.VMEM((4, rows, width), BF16),
            pltpu.VMEM((8, rows, width), BF16),
            pltpu.SemaphoreType.DMA((12,)),
        ],
        input_output_aliases={9: 0},
    )(me, *pieces, volterra, cubic, shares, coupling, g_first)


def per_device(past, second, g_hist, sigma_hist, volterra, sigma_edge, coupling):
    blocks, rows = volterra.shape[:2]
    assert blocks == 2 and past >= 8
    bits = log2(past)
    half = g_hist.shape[1] // 2
    me = lax.axis_index("past").astype(jnp.int32).reshape(1)
    even = list(range(bits))
    odd = even[:1] + even[1:][::-1]

    def swap(x, level):
        pairs = [(d, d ^ (1 << (odd if d % 2 else even)[level])) for d in range(past)]
        return lax.ppermute(x, "past", pairs)

    def exchanged(kept, arrived, sent, after=None):
        mine = combined(kept, arrived, swap(sent, 1), after)
        theirs = swap(mine, 2)
        for level in range(3, bits):
            mine = (mine.astype(F32) + theirs.astype(F32)).astype(BF16)
            theirs = swap(mine, level)
        return mine, theirs

    def passed_on(kept, arrived):
        return (kept[0] + arrived[0].astype(F32)).astype(BF16)

    def gathered(own):
        partner = swap(own, 1)
        return [own, partner, swap(own, 0), swap(partner, 0)]

    def shared(share):
        for level in range(log2(second)):
            pairs = [(z, z ^ (1 << level)) for z in range(second)]
            share = jnp.concatenate([share, lax.ppermute(share, "second", pairs)], axis=0)
        for level in (1, 0):
            share = jnp.concatenate([share, swap(share, level)], axis=0)
        return share

    send, sigma_0, g_send = product(me, sigma_hist, g_hist, 0, rows, half, bits, True)
    arrived_0 = swap(send, 0)
    kept_0, g_keep = product(me, sigma_0, g_hist, 0, rows, half, bits, False)
    sent_0 = passed_on(kept_0, arrived_0)
    send, sigma_1 = product(me, sigma_hist, g_send, 1, rows, half, bits, True, after=sent_0)
    arrived_1 = swap(send, 0)
    (kept_1,) = product(me, sigma_1, g_keep, 1, rows, half, bits, False)
    sent_1 = passed_on(kept_1, arrived_1)

    mine, theirs = exchanged(kept_0, arrived_0, sent_0, after=sent_1)
    mine_1, theirs_1 = exchanged(kept_1, arrived_1, sent_1)
    own_0, response, squares = own_first(me, mine, theirs, volterra, sigma_edge, coupling, bits, after=mine_1)
    own_1, share = own_second(me, mine_1, theirs_1, volterra, response, squares, coupling, bits)
    shares = shared(share)

    g_first, cubic = finish_first(me, gathered(own_0), volterra, sigma_edge, coupling, bits)
    pieces = gathered(own_1)
    return tuple(finish_second(me, pieces, volterra, cubic, shares, coupling, g_first, bits))


def solution(mesh):
    return jax.shard_map(
        functools.partial(per_device, mesh.shape["past"], mesh.shape["second"]),
        mesh=mesh,
        in_specs=(P("past", "second"), P(None, "past"), P(), P(None, "second"), P(None, "second")),
        out_specs=(P(None, "second"), P(None, "second")),
        check_vma=False,
    )
```

```python
import functools

import jax
import jax.numpy as jnp
from jax import lax
from jax.experimental import pallas as pl
from jax.experimental.pallas import tpu as pltpu
from jax.sharding import PartitionSpec as P

VMEM = 20 * 1024 * 1024
F32 = jnp.float32
BF16 = jnp.bfloat16
EPS = 1e-06
BINOMIAL = (1.0, 6.0, 15.0, 20.0, 15.0, 6.0, 1.0)

WHOLE = pl.BlockSpec(memory_space=pltpu.VMEM)
FAR = pl.BlockSpec(memory_space=pl.ANY)
HBM = pl.BlockSpec(memory_space=pltpu.HBM)
SCALAR = pl.BlockSpec(memory_space=pltpu.SMEM)


def log2(n):
    bits = n.bit_length() - 1
    assert n == 1 << bits
    return bits


def near(shape, dtype):
    return pltpu.VMEM(shape, dtype)


def far(x):
    return pltpu.with_memory_space_constraint(x, pltpu.HBM)


def call(kernel, name, **kwargs):
    return pl.pallas_call(
        kernel,
        name=name,
        compiler_params=pltpu.CompilerParams(vmem_limit_bytes=VMEM),
        cost_estimate=pl.CostEstimate(flops=1024, bytes_accessed=1024, transcendentals=0),
        **kwargs,
    )


class Place:
    def __init__(self, me, bits):
        low, high = (me >> 1) & 1, (me >> (bits - 1)) & 1
        self.core = me & 1
        self.side = jnp.where(self.core == 1, high, low)
        self.other_side = jnp.where(self.core == 1, low, high)

    def quarter(self):
        return self.core * 2 + self.side

    def quarter_of(self, slot):
        if slot < 2:
            return self.core * 2 + (self.side ^ slot)
        return (self.core ^ 1) * 2 + (self.other_side ^ (slot - 2))


def product(me, sigma, g, block, rows, half, bits, send, after=None):
    load_sigma, load_g = sigma.shape[0] != rows, g.shape[1] != half
    depth = g.shape[0]
    quarter = half // 2
    dtype = BF16 if send else F32
    out_shape = [near((2, rows, quarter), dtype)]
    if load_sigma:
        out_shape.append(near((rows, depth), BF16))
    if load_g:
        out_shape.append(near((depth, half), BF16))

    def kernel(me_ref, sigma_ref, g_ref, *refs):
        refs = list(refs)
        if after is not None:
            refs.pop(0)
        out = refs.pop(0)
        sigma_v = refs.pop(0) if load_sigma else sigma_ref
        g_v = refs.pop(0) if load_g else g_ref
        total, sems = refs
        place = Place(me_ref[0], bits)
        first = pl.multiple_of((place.core ^ int(send)) * half, half)
        side = place.other_side if send else place.side

        def put(j, value):
            out[1 ^ j ^ side] = value.astype(dtype)

        started = []

        def load(source, target, row, column, at, where):
            part = at[0].size // 4
            copies = []
            for i in range(4):
                into = pl.ds(at[0].start + i * part, part)
                from_rows = pl.ds(row + at[0].start + i * part, part)
                from_columns = pl.ds(column + at[1].start, at[1].size) if where is None else where
                copies.append(
                    pltpu.make_async_copy(
                        source.at[from_rows, from_columns], target.at[into, at[1]], sems.at[len(started)]
                    )
                )
                copies[-1].start()
                started.append(copies[-1])
            return copies

        chunk = depth // 4
        if load_g:
            pieces = []
            for k in range(4):
                deep = pl.ds(k * chunk, chunk)
                piece = []
                if load_sigma:
                    piece += load(sigma_ref, sigma_v, block * rows, 0, (pl.ds(0, rows), deep), None)
                piece += load(g_ref, g_v, 0, 0, (deep, pl.ds(0, half)), pl.ds(first, half))
                pieces.append(piece)
            for k, piece in enumerate(pieces):
                for copy in piece:
                    copy.wait()
                deep = pl.ds(k * chunk, chunk)
                term = jnp.dot(sigma_v[:, deep], g_v[deep, :], preferred_element_type=F32)
                if k == 0:
                    total[...] = term
                elif k < 3:
                    total[...] += term
                else:
                    term += total[...]
                    for j in range(2):
                        put(j, term[:, j * quarter : (j + 1) * quarter])
        elif load_sigma:
            tall = rows // 2
            pieces = [
                load(sigma_ref, sigma_v, block * rows, 0, (pl.ds(i * tall, tall), pl.ds(0, depth)), None)
                for i in range(2)
            ]
            for i, piece in enumerate(pieces):
                for copy in piece:
                    copy.wait()
                here = pl.ds(i * tall, tall)
                term = jnp.dot(sigma_v[here, :], g_v[...], preferred_element_type=F32).astype(dtype)
                for j in range(2):
                    out[1 ^ j ^ side, here, :] = term[:, j * quarter : (j + 1) * quarter]
        else:
            term = jnp.dot(sigma_v[...], g_v[...], preferred_element_type=F32)
            for j in range(2):
                put(j, term[:, j * quarter : (j + 1) * quarter])

    return call(
        kernel,
        "memory_product",
        in_specs=[SCALAR, HBM if load_sigma else WHOLE, HBM if load_g else WHOLE] + [FAR] * (after is not None),
        out_specs=[WHOLE] * len(out_shape),
        out_shape=out_shape,
        scratch_shapes=[pltpu.VMEM((rows, half), F32), pltpu.SemaphoreType.DMA((32,))],
    )(me, far(sigma) if load_sigma else sigma, far(g) if load_g else g, *([] if after is None else [after]))


def combined(kept, arrived, more, after):
    rows, width = more.shape
    if after is None:
        return (kept[1] + arrived[1].astype(F32) + more.astype(F32)).astype(BF16)

    def kernel(kept, arrived, more, _, out):
        out[...] = (kept[1] + arrived[1].astype(F32) + more[...].astype(F32)).astype(BF16)

    return call(
        kernel, "combined", in_specs=[WHOLE] * 3 + [FAR], out_specs=WHOLE, out_shape=near((rows, width), BF16)
    )(kept, arrived, more, after)


def cubed(g, coupling):
    orbitals = coupling.shape[0]
    g3 = g.reshape(g.shape[0] // orbitals, orbitals, g.shape[1])
    return (g3 * g3 * g3 * coupling[None]).reshape(g.shape)


def folded(x):
    line = jnp.sum(x, axis=0, keepdims=True)
    parts = [line[:, i : i + 128] for i in range(0, line.shape[1], 128)]
    return functools.reduce(lambda a, b: a + b, parts)


def columns_of(quarter, width):
    return pl.ds(pl.multiple_of(quarter * width, width), width)


def over_halves(x):
    while x.shape[0] > 1:
        half = x.shape[0] // 2
        x = x[:half] + x[half:]
    return x


def own_first(me, mine, theirs, volterra, edge, coupling, bits, after):
    rows, width = mine.shape

    def kernel(me_ref, mine, theirs, w, edge, coupling, _, memory, response, squares):
        at = columns_of(Place(me_ref[0], bits).quarter(), width)
        summed = (mine[...].astype(F32) + theirs[...].astype(F32)).astype(BF16)
        memory[...] = summed
        g = jnp.dot(w[0, :, :rows], summed, preferred_element_type=F32)
        g += jnp.dot(w[0, :, rows:], edge[:, at], preferred_element_type=F32)
        cubic = cubed(g, coupling[:, at])
        line = folded(cubic * cubic * (1.0 / (rows * width)))
        squares[...] = line
        scale = lax.rsqrt(jnp.sum(line) + EPS)
        response[...] = jnp.dot(w[1, :, rows:], (cubic * scale).astype(BF16), preferred_element_type=F32)

    return call(
        kernel,
        "own_first",
        in_specs=[SCALAR] + [WHOLE] * 5 + [FAR],
        out_specs=[WHOLE] * 3,
        out_shape=[
            near((rows, width), BF16),
            near((rows, width), F32),
            near((1, 128), F32),
        ],
    )(me, mine, theirs, volterra, edge, coupling, after)


def own_second(me, mine, theirs, volterra, response, squares, coupling, bits):
    rows, width = mine.shape
    orbitals = coupling.shape[0]

    def kernel(me_ref, mine, theirs, w, response, squares, coupling, memory, out):
        at = columns_of(Place(me_ref[0], bits).quarter(), width)
        summed = (mine[...].astype(F32) + theirs[...].astype(F32)).astype(BF16)
        memory[...] = summed
        c = coupling[:, at]
        c2 = (c * c * (1.0 / (rows * width)))[None]
        a = jnp.dot(w[1, :, :rows], summed, preferred_element_type=F32)
        b = response[...]
        a2, b2 = a * a, b * b
        a3, b3, a2b, ab2 = a2 * a, b2 * b, a2 * b, a * b2
        lines = [squares[...]]
        terms = (a3 * a3, a3 * a2b, a2b * a2b, a3 * b3, ab2 * ab2, ab2 * b3, b3 * b3)
        for term in terms:
            weighted = (term.reshape(rows // orbitals, orbitals, width) * c2).reshape(rows, width)
            lines.append(folded(weighted))
        out[0] = jnp.concatenate(lines, axis=0)

    return call(
        kernel,
        "own_second",
        in_specs=[SCALAR] + [WHOLE] * 6,
        out_specs=[WHOLE] * 2,
        out_shape=[near((rows, width), BF16), near((1, 8, 128), F32)],
    )(me, mine, theirs, volterra, response, squares, coupling)


def finish_first(me, pieces, volterra, edge, coupling, bits):
    rows, width = pieces[0].shape
    columns = coupling.shape[1]

    def kernel(me_ref, *refs):
        pieces, (w, edge, coupling, g_out, cubic, held, sems) = refs[:4], refs[4:]
        place = Place(me_ref[0], bits)
        copies = []
        for slot in range(4):
            at = columns_of(place.quarter_of(slot), width)
            g = jnp.dot(w[0, :, :rows], pieces[slot][...], preferred_element_type=F32)
            g += jnp.dot(w[0, :, rows:], edge[:, at], preferred_element_type=F32)
            held[slot] = g.astype(BF16)
            copies.append(pltpu.make_async_copy(held.at[slot], g_out.at[pl.ds(0, rows), at], sems.at[slot]))
            copies[-1].start()
            cubic[slot] = cubed(g, coupling[:, at])
        for copy in copies:
            copy.wait()

    return call(
        kernel,
        "finish_first",
        in_specs=[SCALAR] + [WHOLE] * 7,
        out_specs=[HBM, WHOLE],
        out_shape=[
            jax.ShapeDtypeStruct((2 * rows, columns), BF16),
            near((4, rows, width), F32),
        ],
        scratch_shapes=[pltpu.VMEM((4, rows, width), BF16), pltpu.SemaphoreType.DMA((4,))],
    )(me, *pieces, volterra, edge, coupling)


def memory_terms(pieces, volterra):
    rows, width = pieces[0].shape
    count = len(pieces)

    def kernel(*refs):
        pieces, (w, out) = refs[:count], refs[count:]
        for slot in range(count):
            out[slot] = jnp.dot(w[1, :, :rows], pieces[slot][...], preferred_element_type=F32)

    return call(
        kernel,
        "memory_terms",
        in_specs=[WHOLE] * (count + 1),
        out_specs=WHOLE,
        out_shape=near((count, rows, width), F32),
    )(*pieces, volterra)


def joined(a, b, *after):
    size = a.shape[0]

    def kernel(a, b, *refs):
        out = refs[-1]
        out[:size] = a[...]
        out[size:] = b[...]

    shape = (2 * size,) + a.shape[1:]
    in_specs = [WHOLE] * 2 + [FAR] * len(after)
    return call(kernel, "joined", in_specs=in_specs, out_specs=WHOLE, out_shape=near(shape, F32))(a, b, *after)


def ordered(x, after):
    def kernel(x, _, out):
        out[...] = x[...]

    return call(kernel, "ordered", in_specs=[WHOLE, FAR], out_specs=WHOLE, out_shape=near(x.shape, x.dtype))(x, after)


def finish_second(me, last, terms, volterra, cubic, shares, coupling, g_first, bits):
    rows, width = last.shape
    columns = coupling.shape[1]
    everyone = shares.shape[0]

    def kernel(me_ref, last, terms, w, cubic, shares, coupling, _, g_out, sigma, g_held, s_held, sems):
        place = Place(me_ref[0], bits)
        last_term = jnp.dot(w[1, :, :rows], last[...], preferred_element_type=F32)
        sums = jnp.sum(shares[...], axis=2, keepdims=True)
        means = sums[:, 0:1, :]
        mean = jnp.sum(over_halves(means)) / everyone
        ratio = jnp.sqrt((means + EPS) / (mean + EPS))
        power, series = jnp.ones_like(ratio), jnp.zeros_like(ratio)
        for k, weight in enumerate(BINOMIAL):
            series += weight * sums[:, k + 1 : k + 2, :] * power
            power = power * ratio
        scale_0 = 1.0 / jnp.sqrt(mean + EPS)
        scale_1 = 1.0 / jnp.sqrt(jnp.maximum(jnp.sum(over_halves(series)) / everyone, 0.0) + EPS)

        copies = []

        def write(value, held, slot, out, block, at):
            held[slot] = value
            sem = sems.at[len(copies)]
            copies.append(pltpu.make_async_copy(held.at[slot], out.at[pl.ds(block * rows, rows), at], sem))
            copies[-1].start()

        for slot in (3, 0, 1, 2):
            at = columns_of(place.quarter_of(slot), width)
            before = (cubic[slot] * scale_0).astype(BF16)
            write(before, s_held, slot, sigma, 0, at)
            g = last_term if slot == 3 else terms[slot]
            g += jnp.dot(w[1, :, rows:], before, preferred_element_type=F32)
            write(g.astype(BF16), g_held, slot, g_out, 1, at)
            write((cubed(g, coupling[:, at]) * scale_1).astype(BF16), s_held, 4 + slot, sigma, 1, at)
        for copy in copies:
            copy.wait()

    return call(
        kernel,
        "finish_second",
        in_specs=[SCALAR] + [WHOLE] * 6 + [HBM],
        out_specs=[HBM, HBM],
        out_shape=[jax.ShapeDtypeStruct((2 * rows, columns), BF16)] * 2,
        scratch_shapes=[
            pltpu.VMEM((4, rows, width), BF16),
            pltpu.VMEM((8, rows, width), BF16),
            pltpu.SemaphoreType.DMA((12,)),
        ],
        input_output_aliases={7: 0},
    )(me, last, terms, volterra, cubic, shares, coupling, g_first)


def per_device(past, second, g_hist, sigma_hist, volterra, sigma_edge, coupling):
    blocks, rows = volterra.shape[:2]
    assert blocks == 2 and past >= 8
    bits = log2(past)
    half = g_hist.shape[1] // 2
    me = lax.axis_index("past").astype(jnp.int32).reshape(1)
    even = list(range(bits))
    odd = even[:1] + even[1:][::-1]

    def swap(x, level):
        pairs = [(d, d ^ (1 << (odd if d % 2 else even)[level])) for d in range(past)]
        return lax.ppermute(x, "past", pairs)

    def exchanged(kept, arrived, sent, after=None):
        mine = combined(kept, arrived, swap(sent, 1), after)
        theirs = swap(mine, 2)
        for level in range(3, bits):
            mine = (mine.astype(F32) + theirs.astype(F32)).astype(BF16)
            theirs = swap(mine, level)
        return mine, theirs

    def passed_on(kept, arrived):
        return (kept[0] + arrived[0].astype(F32)).astype(BF16)

    def widened(share, level):
        return lax.ppermute(share, "second", [(z, z ^ (1 << level)) for z in range(second)])

    send, sigma_0, g_send = product(me, sigma_hist, g_hist, 0, rows, half, bits, True)
    arrived_0 = swap(send, 0)
    kept_0, g_keep = product(me, sigma_0, g_hist, 0, rows, half, bits, False)
    sent_0 = passed_on(kept_0, arrived_0)
    send, sigma_1 = product(me, sigma_hist, g_send, 1, rows, half, bits, True, after=sent_0)
    arrived_1 = swap(send, 0)
    (kept_1,) = product(me, sigma_1, g_keep, 1, rows, half, bits, False)
    sent_1 = passed_on(kept_1, arrived_1)

    mine, theirs = exchanged(kept_0, arrived_0, sent_0, after=sent_1)
    mine_1, theirs_1 = exchanged(kept_1, arrived_1, sent_1)
    own_0, response, squares = own_first(me, mine, theirs, volterra, sigma_edge, coupling, bits, after=mine_1)
    own_1, share = own_second(me, mine_1, theirs_1, volterra, response, squares, coupling, bits)
    rounds = log2(second)
    share = jnp.concatenate([share, widened(share, 0)])
    partner = ordered(swap(own_0, 1), share)
    pieces = [own_0, partner, swap(own_0, 0), swap(partner, 0)]
    g_first, cubic = finish_first(me, pieces, volterra, sigma_edge, coupling, bits)
    for level in range(1, rounds):
        share = jnp.concatenate([share, widened(share, level)])
    partner = ordered(swap(own_1, 1), share)
    terms = memory_terms([own_1, partner, swap(own_1, 0)], volterra)
    last = swap(partner, 0)
    share = joined(share, swap(share, 1), cubic, terms)
    shares = jnp.concatenate([share, swap(share, 0)])
    return tuple(finish_second(me, last, terms, volterra, cubic, shares, coupling, g_first, bits))


def solution(mesh):
    return jax.shard_map(
        functools.partial(per_device, mesh.shape["past"], mesh.shape["second"]),
        mesh=mesh,
        in_specs=(P("past", "second"), P(None, "past"), P(), P(None, "second"), P(None, "second")),
        out_specs=(P(None, "second"), P(None, "second")),
        check_vma=False,
    )
```

```python
import functools

import jax
import jax.numpy as jnp
from jax import lax
from jax.experimental import pallas as pl
from jax.experimental.pallas import tpu as pltpu
from jax.sharding import PartitionSpec as P

VMEM = 20 * 1024 * 1024
F32 = jnp.float32
BF16 = jnp.bfloat16
EPS = 1e-06
BINOMIAL = (1.0, 6.0, 15.0, 20.0, 15.0, 6.0, 1.0)

WHOLE = pl.BlockSpec(memory_space=pltpu.VMEM)
FAR = pl.BlockSpec(memory_space=pl.ANY)
HBM = pl.BlockSpec(memory_space=pltpu.HBM)
SCALAR = pl.BlockSpec(memory_space=pltpu.SMEM)


def log2(n):
    bits = n.bit_length() - 1
    assert n == 1 << bits
    return bits


def near(shape, dtype):
    return pltpu.VMEM(shape, dtype)


def far(x):
    return pltpu.with_memory_space_constraint(x, pltpu.HBM)


def call(kernel, name, **kwargs):
    return pl.pallas_call(
        kernel,
        name=name,
        compiler_params=pltpu.CompilerParams(vmem_limit_bytes=VMEM),
        cost_estimate=pl.CostEstimate(flops=1024, bytes_accessed=1024, transcendentals=0),
        **kwargs,
    )


class Place:
    def __init__(self, me, bits):
        low, high = (me >> 1) & 1, (me >> (bits - 1)) & 1
        self.core = me & 1
        self.side = jnp.where(self.core == 1, high, low)
        self.other_side = jnp.where(self.core == 1, low, high)

    def quarter(self):
        return self.core * 2 + self.side

    def quarter_of(self, slot):
        if slot < 2:
            return self.core * 2 + (self.side ^ slot)
        return (self.core ^ 1) * 2 + (self.other_side ^ (slot - 2))


def first_product(me, sigma_hist, g_hist, rows, half, bits):
    depth = g_hist.shape[0]
    quarter = half // 2
    chunks, parts = 4, 4
    chunk = depth // chunks

    def kernel(me_ref, sigma_ref, g_ref, out, sigma, g_sent, g_kept, total, sems):
        place = Place(me_ref[0], bits)
        sent_at = pl.ds(pl.multiple_of((place.core ^ 1) * half, half), half)
        kept_at = pl.ds(pl.multiple_of(place.core * half, half), half)
        started = []

        def load(source, target):
            started.append(pltpu.make_async_copy(source, target, sems.at[len(started)]))
            started[-1].start()
            return started[-1]

        pieces = []
        for k in range(chunks):
            deep = pl.ds(k * chunk, chunk)
            piece = []
            for i in range(parts):
                here = pl.ds(i * (rows // parts), rows // parts)
                piece.append(load(sigma_ref.at[here, deep], sigma.at[here, deep]))
                here = pl.ds(k * chunk + i * (chunk // parts), chunk // parts)
                piece.append(load(g_ref.at[here, sent_at], g_sent.at[here, :]))
            pieces.append(piece)
        ahead = []
        for i in range(8):
            here = pl.ds(i * (depth // 8), depth // 8)
            ahead.append(load(g_ref.at[here, kept_at], g_kept.at[here, :]))
        for k in range(chunks):
            for copy in pieces[k]:
                copy.wait()
            deep = pl.ds(k * chunk, chunk)
            term = jnp.dot(sigma[:, deep], g_sent[deep, :], preferred_element_type=F32)
            if k == 0:
                total[...] = term
            elif k < chunks - 1:
                total[...] += term
            else:
                term += total[...]
                for j in range(2):
                    out[1 ^ j ^ place.other_side] = term[:, j * quarter : (j + 1) * quarter].astype(BF16)
        for copy in ahead:
            copy.wait()

    return call(
        kernel,
        "first_product",
        in_specs=[SCALAR, HBM, HBM],
        out_specs=[WHOLE] * 4,
        out_shape=[
            near((2, rows, quarter), BF16),
            near((rows, depth), BF16),
            near((depth, half), BF16),
            near((depth, half), BF16),
        ],
        scratch_shapes=[pltpu.VMEM((rows, half), F32), pltpu.SemaphoreType.DMA((2 * chunks * parts + 8,))],
    )(me, far(sigma_hist), far(g_hist))


def product(me, sigma, g, bits, send, after=None, sigma_hist=None):
    rows, depth = sigma.shape
    half = g.shape[1]
    quarter = half // 2
    dtype = BF16 if send else F32
    parts = 8

    def kernel(me_ref, sigma, g, *refs):
        refs = refs[after is not None :]
        copies = []
        if sigma_hist is not None:
            source, out, target, sems = refs
            for i in range(parts):
                here = pl.ds(i * (rows // parts), rows // parts)
                there = pl.ds(rows + i * (rows // parts), rows // parts)
                copies.append(pltpu.make_async_copy(source.at[there, :], target.at[here, :], sems.at[i]))
                copies[-1].start()
        else:
            (out,) = refs
        place = Place(me_ref[0], bits)
        side = place.other_side if send else place.side
        term = jnp.dot(sigma[...], g[...], preferred_element_type=F32)
        for j in range(2):
            out[1 ^ j ^ side] = term[:, j * quarter : (j + 1) * quarter].astype(dtype)
        for copy in copies:
            copy.wait()

    loads = sigma_hist is not None
    return call(
        kernel,
        "memory_product",
        in_specs=[SCALAR, WHOLE, WHOLE] + [FAR] * (after is not None) + [HBM] * loads,
        out_specs=[WHOLE] * (1 + loads),
        out_shape=[near((2, rows, quarter), dtype)] + [near((rows, depth), BF16)] * loads,
        scratch_shapes=[pltpu.SemaphoreType.DMA((parts,))] * loads,
    )(me, sigma, g, *([] if after is None else [after]), *([far(sigma_hist)] if loads else []))


def combined(kept, arrived, more, after):
    rows, width = more.shape
    if after is None:
        return (kept[1] + arrived[1].astype(F32) + more.astype(F32)).astype(BF16)

    def kernel(kept, arrived, more, _, out):
        out[...] = (kept[1] + arrived[1].astype(F32) + more[...].astype(F32)).astype(BF16)

    return call(
        kernel, "combined", in_specs=[WHOLE] * 3 + [FAR], out_specs=WHOLE, out_shape=near((rows, width), BF16)
    )(kept, arrived, more, after)


def cubed(g, coupling):
    orbitals = coupling.shape[0]
    g3 = g.reshape(g.shape[0] // orbitals, orbitals, g.shape[1])
    return (g3 * g3 * g3 * coupling[None]).reshape(g.shape)


def folded(x):
    line = jnp.sum(x, axis=0, keepdims=True)
    parts = [line[:, i : i + 128] for i in range(0, line.shape[1], 128)]
    return functools.reduce(lambda a, b: a + b, parts)


def columns_of(quarter, width):
    return pl.ds(pl.multiple_of(quarter * width, width), width)


def over_halves(x):
    while x.shape[0] > 1:
        half = x.shape[0] // 2
        x = x[:half] + x[half:]
    return x


def own_first(me, mine, theirs, volterra, edge, coupling, bits, after):
    rows, width = mine.shape

    def kernel(me_ref, mine, theirs, w, edge, coupling, _, memory, response, squares):
        at = columns_of(Place(me_ref[0], bits).quarter(), width)
        summed = (mine[...].astype(F32) + theirs[...].astype(F32)).astype(BF16)
        memory[...] = summed
        g = jnp.dot(w[0, :, :rows], summed, preferred_element_type=F32)
        g += jnp.dot(w[0, :, rows:], edge[:, at], preferred_element_type=F32)
        cubic = cubed(g, coupling[:, at])
        line = folded(cubic * cubic * (1.0 / (rows * width)))
        squares[...] = line
        scale = lax.rsqrt(jnp.sum(line) + EPS)
        response[...] = jnp.dot(w[1, :, rows:], (cubic * scale).astype(BF16), preferred_element_type=F32)

    return call(
        kernel,
        "own_first",
        in_specs=[SCALAR] + [WHOLE] * 5 + [FAR],
        out_specs=[WHOLE] * 3,
        out_shape=[
            near((rows, width), BF16),
            near((rows, width), F32),
            near((1, 128), F32),
        ],
    )(me, mine, theirs, volterra, edge, coupling, after)


def own_second(me, mine, theirs, volterra, response, squares, coupling, bits):
    rows, width = mine.shape
    orbitals = coupling.shape[0]

    def kernel(me_ref, mine, theirs, w, response, squares, coupling, memory, out):
        at = columns_of(Place(me_ref[0], bits).quarter(), width)
        summed = (mine[...].astype(F32) + theirs[...].astype(F32)).astype(BF16)
        memory[...] = summed
        c = coupling[:, at]
        c2 = (c * c * (1.0 / (rows * width)))[None]
        a = jnp.dot(w[1, :, :rows], summed, preferred_element_type=F32)
        b = response[...]
        a2, b2 = a * a, b * b
        a3, b3, a2b, ab2 = a2 * a, b2 * b, a2 * b, a * b2
        lines = [squares[...]]
        terms = (a3 * a3, a3 * a2b, a2b * a2b, a3 * b3, ab2 * ab2, ab2 * b3, b3 * b3)
        for term in terms:
            weighted = (term.reshape(rows // orbitals, orbitals, width) * c2).reshape(rows, width)
            lines.append(folded(weighted))
        out[0] = jnp.concatenate(lines, axis=0)

    return call(
        kernel,
        "own_second",
        in_specs=[SCALAR] + [WHOLE] * 6,
        out_specs=[WHOLE] * 2,
        out_shape=[near((rows, width), BF16), near((1, 8, 128), F32)],
    )(me, mine, theirs, volterra, response, squares, coupling)


def finish_first(me, pieces, volterra, edge, coupling, bits):
    rows, width = pieces[0].shape
    columns = coupling.shape[1]

    def kernel(me_ref, *refs):
        pieces, (w, edge, coupling, g_out, cubic, held, sems) = refs[:4], refs[4:]
        place = Place(me_ref[0], bits)
        copies = []
        for slot in range(4):
            at = columns_of(place.quarter_of(slot), width)
            g = jnp.dot(w[0, :, :rows], pieces[slot][...], preferred_element_type=F32)
            g += jnp.dot(w[0, :, rows:], edge[:, at], preferred_element_type=F32)
            held[slot] = g.astype(BF16)
            copies.append(pltpu.make_async_copy(held.at[slot], g_out.at[pl.ds(0, rows), at], sems.at[slot]))
            copies[-1].start()
            cubic[slot] = cubed(g, coupling[:, at])
        for copy in copies:
            copy.wait()

    return call(
        kernel,
        "finish_first",
        in_specs=[SCALAR] + [WHOLE] * 7,
        out_specs=[HBM, WHOLE],
        out_shape=[
            jax.ShapeDtypeStruct((2 * rows, columns), BF16),
            near((4, rows, width), F32),
        ],
        scratch_shapes=[pltpu.VMEM((4, rows, width), BF16), pltpu.SemaphoreType.DMA((4,))],
    )(me, *pieces, volterra, edge, coupling)


def memory_terms(pieces, volterra):
    rows, width = pieces[0].shape
    count = len(pieces)

    def kernel(*refs):
        pieces, (w, out) = refs[:count], refs[count:]
        for slot in range(count):
            out[slot] = jnp.dot(w[1, :, :rows], pieces[slot][...], preferred_element_type=F32)

    return call(
        kernel,
        "memory_terms",
        in_specs=[WHOLE] * (count + 1),
        out_specs=WHOLE,
        out_shape=near((count, rows, width), F32),
    )(*pieces, volterra)


def joined(a, b, *after):
    size = a.shape[0]

    def kernel(a, b, *refs):
        out = refs[-1]
        out[:size] = a[...]
        out[size:] = b[...]

    shape = (2 * size,) + a.shape[1:]
    in_specs = [WHOLE] * 2 + [FAR] * len(after)
    return call(kernel, "joined", in_specs=in_specs, out_specs=WHOLE, out_shape=near(shape, F32))(a, b, *after)


def ordered(x, after):
    def kernel(x, _, out):
        out[...] = x[...]

    return call(kernel, "ordered", in_specs=[WHOLE, FAR], out_specs=WHOLE, out_shape=near(x.shape, x.dtype))(x, after)


def finish_second(me, last, terms, volterra, cubic, shares, coupling, g_first, bits):
    rows, width = last.shape
    columns = coupling.shape[1]
    everyone = shares.shape[0]

    def kernel(me_ref, last, terms, w, cubic, shares, coupling, _, g_out, sigma, g_held, s_held, sems):
        place = Place(me_ref[0], bits)
        last_term = jnp.dot(w[1, :, :rows], last[...], preferred_element_type=F32)
        sums = jnp.sum(shares[...], axis=2, keepdims=True)
        means = sums[:, 0:1, :]
        mean = jnp.sum(over_halves(means)) / everyone
        ratio = jnp.sqrt((means + EPS) / (mean + EPS))
        power, series = jnp.ones_like(ratio), jnp.zeros_like(ratio)
        for k, weight in enumerate(BINOMIAL):
            series += weight * sums[:, k + 1 : k + 2, :] * power
            power = power * ratio
        scale_0 = 1.0 / jnp.sqrt(mean + EPS)
        scale_1 = 1.0 / jnp.sqrt(jnp.maximum(jnp.sum(over_halves(series)) / everyone, 0.0) + EPS)

        copies = []

        def write(value, held, slot, out, block, at):
            held[slot] = value
            sem = sems.at[len(copies)]
            copies.append(pltpu.make_async_copy(held.at[slot], out.at[pl.ds(block * rows, rows), at], sem))
            copies[-1].start()

        for slot in (3, 0, 1, 2):
            at = columns_of(place.quarter_of(slot), width)
            before = (cubic[slot] * scale_0).astype(BF16)
            write(before, s_held, slot, sigma, 0, at)
            g = last_term if slot == 3 else terms[slot]
            g += jnp.dot(w[1, :, rows:], before, preferred_element_type=F32)
            write(g.astype(BF16), g_held, slot, g_out, 1, at)
            write((cubed(g, coupling[:, at]) * scale_1).astype(BF16), s_held, 4 + slot, sigma, 1, at)
        for copy in copies:
            copy.wait()

    return call(
        kernel,
        "finish_second",
        in_specs=[SCALAR] + [WHOLE] * 6 + [HBM],
        out_specs=[HBM, HBM],
        out_shape=[jax.ShapeDtypeStruct((2 * rows, columns), BF16)] * 2,
        scratch_shapes=[
            pltpu.VMEM((4, rows, width), BF16),
            pltpu.VMEM((8, rows, width), BF16),
            pltpu.SemaphoreType.DMA((12,)),
        ],
        input_output_aliases={7: 0},
    )(me, last, terms, volterra, cubic, shares, coupling, g_first)


def per_device(past, second, g_hist, sigma_hist, volterra, sigma_edge, coupling):
    blocks, rows = volterra.shape[:2]
    assert blocks == 2 and past >= 8
    bits = log2(past)
    half = g_hist.shape[1] // 2
    me = lax.axis_index("past").astype(jnp.int32).reshape(1)
    even = list(range(bits))
    odd = even[:1] + even[1:][::-1]

    def swap(x, level):
        pairs = [(d, d ^ (1 << (odd if d % 2 else even)[level])) for d in range(past)]
        return lax.ppermute(x, "past", pairs)

    def exchanged(kept, arrived, sent, after=None):
        mine = combined(kept, arrived, swap(sent, 1), after)
        theirs = swap(mine, 2)
        for level in range(3, bits):
            mine = (mine.astype(F32) + theirs.astype(F32)).astype(BF16)
            theirs = swap(mine, level)
        return mine, theirs

    def passed_on(kept, arrived):
        return (kept[0] + arrived[0].astype(F32)).astype(BF16)

    def widened(share, level):
        return lax.ppermute(share, "second", [(z, z ^ (1 << level)) for z in range(second)])

    send, sigma_0, g_sent, g_kept = first_product(me, sigma_hist, g_hist, rows, half, bits)
    arrived_0 = swap(send, 0)
    kept_0, sigma_1 = product(me, sigma_0, g_kept, bits, False, sigma_hist=sigma_hist)
    sent_0 = passed_on(kept_0, arrived_0)
    (send,) = product(me, sigma_1, g_sent, bits, True, after=sent_0)
    arrived_1 = swap(send, 0)
    (kept_1,) = product(me, sigma_1, g_kept, bits, False, after=arrived_1)
    sent_1 = passed_on(kept_1, arrived_1)

    mine, theirs = exchanged(kept_0, arrived_0, sent_0, after=sent_1)
    mine_1, theirs_1 = exchanged(kept_1, arrived_1, sent_1)
    own_0, response, squares = own_first(me, mine, theirs, volterra, sigma_edge, coupling, bits, after=mine_1)
    own_1, share = own_second(me, mine_1, theirs_1, volterra, response, squares, coupling, bits)

    rounds = log2(second)
    share = jnp.concatenate([share, widened(share, 0)])
    partner = ordered(swap(own_0, 1), share)
    pieces = [own_0, partner, swap(own_0, 0), swap(partner, 0)]
    g_first, cubic = finish_first(me, pieces, volterra, sigma_edge, coupling, bits)
    for level in range(1, rounds):
        share = jnp.concatenate([share, widened(share, level)])
    partner = ordered(swap(own_1, 1), share)
    terms = memory_terms([own_1, partner, swap(own_1, 0)], volterra)
    last = swap(partner, 0)
    share = joined(share, swap(share, 1), cubic, terms)
    shares = jnp.concatenate([share, swap(share, 0)])
    return tuple(finish_second(me, last, terms, volterra, cubic, shares, coupling, g_first, bits))


def solution(mesh):
    return jax.shard_map(
        functools.partial(per_device, mesh.shape["past"], mesh.shape["second"]),
        mesh=mesh,
        in_specs=(P("past", "second"), P(None, "past"), P(), P(None, "second"), P(None, "second")),
        out_specs=(P(None, "second"), P(None, "second")),
        check_vma=False,
    )
```

```python
import functools

import jax
import jax.numpy as jnp
from jax import lax
from jax.experimental import pallas as pl
from jax.experimental.pallas import tpu as pltpu
from jax.sharding import PartitionSpec as P

VMEM = 20 * 1024 * 1024
F32 = jnp.float32
BF16 = jnp.bfloat16
EPS = 1e-06
BINOMIAL = (1.0, 6.0, 15.0, 20.0, 15.0, 6.0, 1.0)

WHOLE = pl.BlockSpec(memory_space=pltpu.VMEM)
FAR = pl.BlockSpec(memory_space=pl.ANY)
HBM = pl.BlockSpec(memory_space=pltpu.HBM)
SCALAR = pl.BlockSpec(memory_space=pltpu.SMEM)


def log2(n):
    bits = n.bit_length() - 1
    assert n == 1 << bits
    return bits


def near(shape, dtype):
    return pltpu.VMEM(shape, dtype)


def far(x):
    return pltpu.with_memory_space_constraint(x, pltpu.HBM)


def call(kernel, name, **kwargs):
    return pl.pallas_call(
        kernel,
        name=name,
        compiler_params=pltpu.CompilerParams(vmem_limit_bytes=VMEM),
        cost_estimate=pl.CostEstimate(flops=1024, bytes_accessed=1024, transcendentals=0),
        **kwargs,
    )


class Place:
    def __init__(self, me, bits):
        low, high = (me >> 1) & 1, (me >> (bits - 1)) & 1
        self.core = me & 1
        self.side = jnp.where(self.core == 1, high, low)
        self.other_side = jnp.where(self.core == 1, low, high)

    def quarter(self):
        return self.core * 2 + self.side

    def quarter_of(self, slot):
        if slot < 2:
            return self.core * 2 + (self.side ^ slot)
        return (self.core ^ 1) * 2 + (self.other_side ^ (slot - 2))


def first_product(me, sigma_hist, g_hist, rows, half, bits):
    depth = g_hist.shape[0]
    quarter = half // 2
    chunks, parts = 4, 4
    chunk = depth // chunks

    def kernel(me_ref, sigma_ref, g_ref, out, sigma, g_sent, g_kept, total, sems):
        place = Place(me_ref[0], bits)
        sent_at = pl.ds(pl.multiple_of((place.core ^ 1) * half, half), half)
        kept_at = pl.ds(pl.multiple_of(place.core * half, half), half)
        started = []

        def load(source, target):
            started.append(pltpu.make_async_copy(source, target, sems.at[len(started)]))
            started[-1].start()
            return started[-1]

        pieces = []
        for k in range(chunks):
            deep = pl.ds(k * chunk, chunk)
            piece = []
            for i in range(parts):
                here = pl.ds(i * (rows // parts), rows // parts)
                piece.append(load(sigma_ref.at[here, deep], sigma.at[here, deep]))
                here = pl.ds(k * chunk + i * (chunk // parts), chunk // parts)
                piece.append(load(g_ref.at[here, sent_at], g_sent.at[here, :]))
            pieces.append(piece)
        ahead = []
        for i in range(8):
            here = pl.ds(i * (depth // 8), depth // 8)
            ahead.append(load(g_ref.at[here, kept_at], g_kept.at[here, :]))
        for k in range(chunks):
            for copy in pieces[k]:
                copy.wait()
            deep = pl.ds(k * chunk, chunk)
            term = jnp.dot(sigma[:, deep], g_sent[deep, :], preferred_element_type=F32)
            if k == 0:
                total[...] = term
            elif k < chunks - 1:
                total[...] += term
            else:
                term += total[...]
                for j in range(2):
                    out[1 ^ j ^ place.other_side] = term[:, j * quarter : (j + 1) * quarter].astype(BF16)
        for copy in ahead:
            copy.wait()

    return call(
        kernel,
        "first_product",
        in_specs=[SCALAR, HBM, HBM],
        out_specs=[WHOLE] * 4,
        out_shape=[
            near((2, rows, quarter), BF16),
            near((rows, depth), BF16),
            near((depth, half), BF16),
            near((depth, half), BF16),
        ],
        scratch_shapes=[pltpu.VMEM((rows, half), F32), pltpu.SemaphoreType.DMA((2 * chunks * parts + 8,))],
    )(me, far(sigma_hist), far(g_hist))


def product(me, sigma, g, bits, send, after=None, sigma_hist=None):
    rows, depth = sigma.shape
    half = g.shape[1]
    quarter = half // 2
    dtype = BF16 if send else F32
    parts = 8

    def kernel(me_ref, sigma, g, *refs):
        refs = refs[after is not None :]
        copies = []
        if sigma_hist is not None:
            source, out, target, sems = refs
            for i in range(parts):
                here = pl.ds(i * (rows // parts), rows // parts)
                there = pl.ds(rows + i * (rows // parts), rows // parts)
                copies.append(pltpu.make_async_copy(source.at[there, :], target.at[here, :], sems.at[i]))
                copies[-1].start()
        else:
            (out,) = refs
        place = Place(me_ref[0], bits)
        side = place.other_side if send else place.side
        term = jnp.dot(sigma[...], g[...], preferred_element_type=F32)
        for j in range(2):
            out[1 ^ j ^ side] = term[:, j * quarter : (j + 1) * quarter].astype(dtype)
        for copy in copies:
            copy.wait()

    loads = sigma_hist is not None
    return call(
        kernel,
        "memory_product",
        in_specs=[SCALAR, WHOLE, WHOLE] + [FAR] * (after is not None) + [HBM] * loads,
        out_specs=[WHOLE] * (1 + loads),
        out_shape=[near((2, rows, quarter), dtype)] + [near((rows, depth), BF16)] * loads,
        scratch_shapes=[pltpu.SemaphoreType.DMA((parts,))] * loads,
    )(me, sigma, g, *([] if after is None else [after]), *([far(sigma_hist)] if loads else []))


def combined(kept, arrived, more, after):
    rows, width = more.shape
    if after is None:
        return (kept[1] + arrived[1].astype(F32) + more.astype(F32)).astype(BF16)

    def kernel(kept, arrived, more, _, out):
        out[...] = (kept[1] + arrived[1].astype(F32) + more[...].astype(F32)).astype(BF16)

    return call(
        kernel, "combined", in_specs=[WHOLE] * 3 + [FAR], out_specs=WHOLE, out_shape=near((rows, width), BF16)
    )(kept, arrived, more, after)


def cubed(g, coupling):
    orbitals = coupling.shape[0]
    g3 = g.reshape(g.shape[0] // orbitals, orbitals, g.shape[1])
    return (g3 * g3 * g3 * coupling[None]).reshape(g.shape)


def folded(x):
    line = jnp.sum(x, axis=0, keepdims=True)
    parts = [line[:, i : i + 128] for i in range(0, line.shape[1], 128)]
    return functools.reduce(lambda a, b: a + b, parts)


def columns_of(quarter, width):
    return pl.ds(pl.multiple_of(quarter * width, width), width)


def over_halves(x):
    while x.shape[0] > 1:
        half = x.shape[0] // 2
        x = x[:half] + x[half:]
    return x


def own_first(me, mine, theirs, volterra, edge, coupling, bits, after):
    rows, width = mine.shape

    def kernel(me_ref, mine, theirs, w, edge, coupling, _, memory, response, squares):
        at = columns_of(Place(me_ref[0], bits).quarter(), width)
        summed = (mine[...].astype(F32) + theirs[...].astype(F32)).astype(BF16)
        memory[...] = summed
        g = jnp.dot(w[0, :, :rows], summed, preferred_element_type=F32)
        g += jnp.dot(w[0, :, rows:], edge[:, at], preferred_element_type=F32)
        cubic = cubed(g, coupling[:, at])
        line = folded(cubic * cubic * (1.0 / (rows * width)))
        squares[...] = line
        scale = lax.rsqrt(jnp.sum(line) + EPS)
        response[...] = jnp.dot(w[1, :, rows:], (cubic * scale).astype(BF16), preferred_element_type=F32)

    return call(
        kernel,
        "own_first",
        in_specs=[SCALAR] + [WHOLE] * 5 + [FAR],
        out_specs=[WHOLE] * 3,
        out_shape=[
            near((rows, width), BF16),
            near((rows, width), F32),
            near((1, 128), F32),
        ],
    )(me, mine, theirs, volterra, edge, coupling, after)


def own_second(me, mine, theirs, first, volterra, response, squares, coupling, bits):
    rows, width = mine.shape
    orbitals = coupling.shape[0]

    def kernel(me_ref, mine, theirs, first, w, response, squares, coupling, passed, memory, out):
        at = columns_of(Place(me_ref[0], bits).quarter(), width)
        summed = (mine[...].astype(F32) + theirs[...].astype(F32)).astype(BF16)
        memory[...] = summed
        passed[...] = first[...]
        c = coupling[:, at]
        c2 = (c * c * (1.0 / (rows * width)))[None]
        a = jnp.dot(w[1, :, :rows], summed, preferred_element_type=F32)
        b = response[...]
        a2, b2 = a * a, b * b
        a3, b3, a2b, ab2 = a2 * a, b2 * b, a2 * b, a * b2
        lines = [squares[...]]
        terms = (a3 * a3, a3 * a2b, a2b * a2b, a3 * b3, ab2 * ab2, ab2 * b3, b3 * b3)
        for term in terms:
            weighted = (term.reshape(rows // orbitals, orbitals, width) * c2).reshape(rows, width)
            lines.append(folded(weighted))
        out[0] = jnp.concatenate(lines, axis=0)

    return call(
        kernel,
        "own_second",
        in_specs=[SCALAR] + [WHOLE] * 7,
        out_specs=[WHOLE] * 3,
        out_shape=[near((rows, width), BF16)] * 2 + [near((1, 8, 128), F32)],
    )(me, mine, theirs, first, volterra, response, squares, coupling)


def finish_first(me, pieces, volterra, edge, coupling, bits):
    rows, width = pieces[0].shape
    columns = coupling.shape[1]

    def kernel(me_ref, *refs):
        pieces, (w, edge, coupling, g_out, cubic, held, sems) = refs[:4], refs[4:]
        place = Place(me_ref[0], bits)
        copies = []
        for slot in range(4):
            at = columns_of(place.quarter_of(slot), width)
            g = jnp.dot(w[0, :, :rows], pieces[slot][...], preferred_element_type=F32)
            g += jnp.dot(w[0, :, rows:], edge[:, at], preferred_element_type=F32)
            held[slot] = g.astype(BF16)
            copies.append(pltpu.make_async_copy(held.at[slot], g_out.at[pl.ds(0, rows), at], sems.at[slot]))
            copies[-1].start()
            cubic[slot] = cubed(g, coupling[:, at])
        for copy in copies:
            copy.wait()

    return call(
        kernel,
        "finish_first",
        in_specs=[SCALAR] + [WHOLE] * 7,
        out_specs=[HBM, WHOLE],
        out_shape=[
            jax.ShapeDtypeStruct((2 * rows, columns), BF16),
            near((4, rows, width), F32),
        ],
        scratch_shapes=[pltpu.VMEM((4, rows, width), BF16), pltpu.SemaphoreType.DMA((4,))],
    )(me, *pieces, volterra, edge, coupling)


def memory_terms(pieces, volterra):
    rows, width = pieces[0].shape
    count = len(pieces)

    def kernel(*refs):
        pieces, (w, out) = refs[:count], refs[count:]
        for slot in range(count):
            out[slot] = jnp.dot(w[1, :, :rows], pieces[slot][...], preferred_element_type=F32)

    return call(
        kernel,
        "memory_terms",
        in_specs=[WHOLE] * (count + 1),
        out_specs=WHOLE,
        out_shape=near((count, rows, width), F32),
    )(*pieces, volterra)


def joined(a, b, *after):
    size = a.shape[0]

    def kernel(a, b, *refs):
        out = refs[-1]
        out[:size] = a[...]
        out[size:] = b[...]

    shape = (2 * size,) + a.shape[1:]
    in_specs = [WHOLE] * 2 + [FAR] * len(after)
    return call(kernel, "joined", in_specs=in_specs, out_specs=WHOLE, out_shape=near(shape, F32))(a, b, *after)


def chosen(me, even, odd, after):
    def kernel(me_ref, even, odd, _, out):
        out[...] = jnp.where(me_ref[0] % 2 == 1, odd[...], even[...])

    return call(
        kernel,
        "chosen",
        in_specs=[SCALAR, WHOLE, WHOLE, FAR],
        out_specs=WHOLE,
        out_shape=near(even.shape, even.dtype),
    )(me, even, odd, after)


def ordered(x, after):
    def kernel(x, _, out):
        out[...] = x[...]

    return call(kernel, "ordered", in_specs=[WHOLE, FAR], out_specs=WHOLE, out_shape=near(x.shape, x.dtype))(x, after)


def finish_second(me, last, terms, volterra, cubic, shares, coupling, g_first, bits):
    rows, width = last.shape
    columns = coupling.shape[1]
    everyone = shares.shape[0]

    def kernel(me_ref, last, terms, w, cubic, shares, coupling, _, g_out, sigma, g_held, s_held, sems):
        place = Place(me_ref[0], bits)
        last_term = jnp.dot(w[1, :, :rows], last[...], preferred_element_type=F32)
        sums = jnp.sum(shares[...], axis=2, keepdims=True)
        means = sums[:, 0:1, :]
        mean = over_halves(means) * (1.0 / everyone)
        ratio = jnp.sqrt((means + EPS) / (mean + EPS))
        power, series = jnp.ones_like(ratio), jnp.zeros_like(ratio)
        for k, weight in enumerate(BINOMIAL):
            series += weight * sums[:, k + 1 : k + 2, :] * power
            power = power * ratio
        scale_0 = (1.0 / jnp.sqrt(mean + EPS))[0]
        scale_1 = (1.0 / jnp.sqrt(jnp.maximum(over_halves(series) * (1.0 / everyone), 0.0) + EPS))[0]

        copies = []

        def write(value, held, slot, out, block, at):
            held[slot] = value
            sem = sems.at[len(copies)]
            copies.append(pltpu.make_async_copy(held.at[slot], out.at[pl.ds(block * rows, rows), at], sem))
            copies[-1].start()

        for slot in (3, 0, 1, 2):
            at = columns_of(place.quarter_of(slot), width)
            before = (cubic[slot] * scale_0).astype(BF16)
            write(before, s_held, slot, sigma, 0, at)
            g = last_term if slot == 3 else terms[slot]
            g += jnp.dot(w[1, :, rows:], before, preferred_element_type=F32)
            write(g.astype(BF16), g_held, slot, g_out, 1, at)
            write((cubed(g, coupling[:, at]) * scale_1).astype(BF16), s_held, 4 + slot, sigma, 1, at)
        for copy in copies:
            copy.wait()

    return call(
        kernel,
        "finish_second",
        in_specs=[SCALAR] + [WHOLE] * 6 + [HBM],
        out_specs=[HBM, HBM],
        out_shape=[jax.ShapeDtypeStruct((2 * rows, columns), BF16)] * 2,
        scratch_shapes=[
            pltpu.VMEM((4, rows, width), BF16),
            pltpu.VMEM((8, rows, width), BF16),
            pltpu.SemaphoreType.DMA((12,)),
        ],
        input_output_aliases={7: 0},
    )(me, last, terms, volterra, cubic, shares, coupling, g_first)


def per_device(past, second, g_hist, sigma_hist, volterra, sigma_edge, coupling):
    blocks, rows = volterra.shape[:2]
    assert blocks == 2 and past >= 8
    bits = log2(past)
    half = g_hist.shape[1] // 2
    me = lax.axis_index("past").astype(jnp.int32).reshape(1)
    even = list(range(bits))
    odd = even[:1] + even[1:][::-1]

    def swap(x, level, devices=range(past)):
        pairs = [(d, d ^ (1 << (odd if d % 2 else even)[level])) for d in devices]
        return lax.ppermute(x, "past", pairs)

    def exchanged(kept, arrived, sent, after=None):
        mine = combined(kept, arrived, swap(sent, 1), after)
        theirs = swap(mine, 2)
        for level in range(3, bits):
            mine = (mine.astype(F32) + theirs.astype(F32)).astype(BF16)
            theirs = swap(mine, level)
        return mine, theirs

    def passed_on(kept, arrived):
        return (kept[0] + arrived[0].astype(F32)).astype(BF16)

    def widened(share, level):
        return lax.ppermute(share, "second", [(z, z ^ (1 << level)) for z in range(second)])

    send, sigma_0, g_sent, g_kept = first_product(me, sigma_hist, g_hist, rows, half, bits)
    arrived_0 = swap(send, 0)
    kept_0, sigma_1 = product(me, sigma_0, g_kept, bits, False, sigma_hist=sigma_hist)
    sent_0 = passed_on(kept_0, arrived_0)
    (send,) = product(me, sigma_1, g_sent, bits, True, after=sent_0)
    arrived_1 = swap(send, 0)
    (kept_1,) = product(me, sigma_1, g_kept, bits, False, after=arrived_1)
    sent_1 = passed_on(kept_1, arrived_1)

    mine, theirs = exchanged(kept_0, arrived_0, sent_0, after=sent_1)
    mine_1, theirs_1 = exchanged(kept_1, arrived_1, sent_1)
    own_0, response, squares = own_first(me, mine, theirs, volterra, sigma_edge, coupling, bits, after=mine_1)
    own_0_late, own_1, share = own_second(me, mine_1, theirs_1, own_0, volterra, response, squares, coupling, bits)

    rounds = log2(second)
    share = jnp.concatenate([share, widened(share, 0)])
    for level in range(1, rounds):
        share = jnp.concatenate([share, widened(share, level)])
    partner = chosen(me, swap(own_0, 1, range(0, past, 2)), swap(own_0_late, 1, range(1, past, 2)), share)
    pieces = [own_0, partner, swap(own_0, 0), swap(partner, 0)]
    g_first, cubic = finish_first(me, pieces, volterra, sigma_edge, coupling, bits)
    partner = ordered(swap(own_1, 1), share)
    terms = memory_terms([own_1, partner, swap(own_1, 0)], volterra)
    last = swap(partner, 0)
    share = joined(share, swap(share, 1), cubic, terms)
    shares = jnp.concatenate([share, swap(share, 0)])
    return tuple(finish_second(me, last, terms, volterra, cubic, shares, coupling, g_first, bits))


def solution(mesh):
    return jax.shard_map(
        functools.partial(per_device, mesh.shape["past"], mesh.shape["second"]),
        mesh=mesh,
        in_specs=(P("past", "second"), P(None, "past"), P(), P(None, "second"), P(None, "second")),
        out_specs=(P(None, "second"), P(None, "second")),
        check_vma=False,
    )
```

```python
import functools

import jax
import jax.numpy as jnp
from jax import lax
from jax.experimental import pallas as pl
from jax.experimental.pallas import tpu as pltpu
from jax.sharding import PartitionSpec as P

VMEM = 20 * 1024 * 1024
F32 = jnp.float32
BF16 = jnp.bfloat16
EPS = 1e-06
BINOMIAL = (1.0, 6.0, 15.0, 20.0, 15.0, 6.0, 1.0)

WHOLE = pl.BlockSpec(memory_space=pltpu.VMEM)
FAR = pl.BlockSpec(memory_space=pl.ANY)
HBM = pl.BlockSpec(memory_space=pltpu.HBM)
SCALAR = pl.BlockSpec(memory_space=pltpu.SMEM)


def log2(n):
    bits = n.bit_length() - 1
    assert n == 1 << bits
    return bits


def near(shape, dtype):
    return pltpu.VMEM(shape, dtype)


def far(x):
    return pltpu.with_memory_space_constraint(x, pltpu.HBM)


def call(kernel, name, **kwargs):
    return pl.pallas_call(
        kernel,
        name=name,
        compiler_params=pltpu.CompilerParams(vmem_limit_bytes=VMEM),
        cost_estimate=pl.CostEstimate(flops=1024, bytes_accessed=1024, transcendentals=0),
        **kwargs,
    )


class Place:
    def __init__(self, me, bits):
        low, high = (me >> 1) & 1, (me >> (bits - 1)) & 1
        self.core = me & 1
        self.side = jnp.where(self.core == 1, high, low)
        self.other_side = jnp.where(self.core == 1, low, high)

    def quarter(self):
        return self.core * 2 + self.side

    def quarter_of(self, slot):
        if slot < 2:
            return self.core * 2 + (self.side ^ slot)
        return (self.core ^ 1) * 2 + (self.other_side ^ (slot - 2))


def first_product(me, sigma_hist, g_hist, rows, half, bits):
    depth = g_hist.shape[0]
    quarter = half // 2
    chunks, parts = 4, 4
    chunk = depth // chunks

    def kernel(me_ref, sigma_ref, g_ref, out, sigma, g_sent, g_kept, total, sems):
        place = Place(me_ref[0], bits)
        sent_at = pl.ds(pl.multiple_of((place.core ^ 1) * half, half), half)
        kept_at = pl.ds(pl.multiple_of(place.core * half, half), half)
        started = []

        def load(source, target):
            started.append(pltpu.make_async_copy(source, target, sems.at[len(started)]))
            started[-1].start()
            return started[-1]

        pieces = []
        for k in range(chunks):
            deep = pl.ds(k * chunk, chunk)
            piece = []
            for i in range(parts):
                here = pl.ds(i * (rows // parts), rows // parts)
                piece.append(load(sigma_ref.at[here, deep], sigma.at[here, deep]))
                here = pl.ds(k * chunk + i * (chunk // parts), chunk // parts)
                piece.append(load(g_ref.at[here, sent_at], g_sent.at[here, :]))
            pieces.append(piece)
        ahead = []
        for i in range(8):
            here = pl.ds(i * (depth // 8), depth // 8)
            ahead.append(load(g_ref.at[here, kept_at], g_kept.at[here, :]))
        for k in range(chunks):
            for copy in pieces[k]:
                copy.wait()
            deep = pl.ds(k * chunk, chunk)
            term = jnp.dot(sigma[:, deep], g_sent[deep, :], preferred_element_type=F32)
            if k == 0:
                total[...] = term
            elif k < chunks - 1:
                total[...] += term
            else:
                term += total[...]
                halves_to(out, term, place.other_side)
        for copy in ahead:
            copy.wait()

    return call(
        kernel,
        "first_product",
        in_specs=[SCALAR, HBM, HBM],
        out_specs=[WHOLE] * 4,
        out_shape=[
            near((2, rows, quarter), BF16),
            near((rows, depth), BF16),
            near((depth, half), BF16),
            near((depth, half), BF16),
        ],
        scratch_shapes=[pltpu.VMEM((rows, half), F32), pltpu.SemaphoreType.DMA((2 * chunks * parts + 8,))],
    )(me, far(sigma_hist), far(g_hist))


def halves_to(out, value, side, here=slice(None)):
    quarter = out.shape[2]
    for j in range(2):
        out[1 ^ j ^ side, here, :] = value[:, j * quarter : (j + 1) * quarter].astype(out.dtype)


def middle_products(me, sigma, g_kept, g_sent, sigma_hist, bits):
    rows, depth = sigma.shape
    half = g_kept.shape[1]
    parts, chunks = 8, 2

    def kernel(me_ref, sigma, g_kept, g_sent, source, kept, sent, target, sems):
        copies = []
        for i in range(parts):
            here = pl.ds(i * (rows // parts), rows // parts)
            there = pl.ds(rows + i * (rows // parts), rows // parts)
            copies.append(pltpu.make_async_copy(source.at[there, :], target.at[here, :], sems.at[i]))
            copies[-1].start()
        place = Place(me_ref[0], bits)
        halves_to(kept, jnp.dot(sigma[...], g_kept[...], preferred_element_type=F32), place.side)
        for k in range(chunks):
            for copy in copies[k * (parts // chunks) : (k + 1) * (parts // chunks)]:
                copy.wait()
            here = pl.ds(k * (rows // chunks), rows // chunks)
            term = jnp.dot(target[here, :], g_sent[...], preferred_element_type=F32)
            halves_to(sent, term, place.other_side, here)

    return call(
        kernel,
        "middle_products",
        in_specs=[SCALAR] + [WHOLE] * 3 + [HBM],
        out_specs=[WHOLE] * 3,
        out_shape=[near((2, rows, half // 2), F32), near((2, rows, half // 2), BF16), near((rows, depth), BF16)],
        scratch_shapes=[pltpu.SemaphoreType.DMA((parts,))],
    )(me, sigma, g_kept, g_sent, far(sigma_hist))


def last_product(me, sigma, g_kept, bits, after):
    rows, half = sigma.shape[0], g_kept.shape[1]

    def kernel(me_ref, sigma, g_kept, _, kept):
        halves_to(kept, jnp.dot(sigma[...], g_kept[...], preferred_element_type=F32), Place(me_ref[0], bits).side)

    return call(
        kernel,
        "last_product",
        in_specs=[SCALAR, WHOLE, WHOLE, FAR],
        out_specs=WHOLE,
        out_shape=near((2, rows, half // 2), F32),
    )(me, sigma, g_kept, after)


def combined(kept, arrived, more, after):
    rows, width = more.shape
    if after is None:
        return (kept[1] + arrived[1].astype(F32) + more.astype(F32)).astype(BF16)

    def kernel(kept, arrived, more, _, out):
        out[...] = (kept[1] + arrived[1].astype(F32) + more[...].astype(F32)).astype(BF16)

    return call(
        kernel, "combined", in_specs=[WHOLE] * 3 + [FAR], out_specs=WHOLE, out_shape=near((rows, width), BF16)
    )(kept, arrived, more, after)


def cubed(g, coupling):
    orbitals = coupling.shape[0]
    g3 = g.reshape(g.shape[0] // orbitals, orbitals, g.shape[1])
    return (g3 * g3 * g3 * coupling[None]).reshape(g.shape)


def folded(x):
    line = jnp.sum(x, axis=0, keepdims=True)
    parts = [line[:, i : i + 128] for i in range(0, line.shape[1], 128)]
    return functools.reduce(lambda a, b: a + b, parts)


def columns_of(quarter, width):
    return pl.ds(pl.multiple_of(quarter * width, width), width)


def over_halves(x):
    while x.shape[0] > 1:
        half = x.shape[0] // 2
        x = x[:half] + x[half:]
    return x


def own_first(me, mine, theirs, volterra, edge, coupling, bits, after):
    rows, width = mine.shape

    def kernel(me_ref, mine, theirs, w, edge, coupling, _, memory, response, squares, g_own, cubic_own):
        at = columns_of(Place(me_ref[0], bits).quarter(), width)
        summed = (mine[...].astype(F32) + theirs[...].astype(F32)).astype(BF16)
        memory[...] = summed
        g = jnp.dot(w[0, :, :rows], summed, preferred_element_type=F32)
        g += jnp.dot(w[0, :, rows:], edge[:, at], preferred_element_type=F32)
        g_own[...] = g.astype(BF16)
        cubic = cubed(g, coupling[:, at])
        cubic_own[...] = cubic
        line = folded(cubic * cubic * (1.0 / (rows * width)))
        squares[...] = line
        scale = lax.rsqrt(jnp.sum(line) + EPS)
        response[...] = jnp.dot(w[1, :, rows:], (cubic * scale).astype(BF16), preferred_element_type=F32)

    return call(
        kernel,
        "own_first",
        in_specs=[SCALAR] + [WHOLE] * 5 + [FAR],
        out_specs=[WHOLE] * 5,
        out_shape=[
            near((rows, width), BF16),
            near((rows, width), F32),
            near((1, 128), F32),
            near((rows, width), BF16),
            near((rows, width), F32),
        ],
    )(me, mine, theirs, volterra, edge, coupling, after)


def own_second(me, mine, theirs, volterra, response, squares, coupling, bits):
    rows, width = mine.shape
    orbitals = coupling.shape[0]

    def kernel(me_ref, mine, theirs, w, response, squares, coupling, memory, out, term_own):
        at = columns_of(Place(me_ref[0], bits).quarter(), width)
        summed = (mine[...].astype(F32) + theirs[...].astype(F32)).astype(BF16)
        memory[...] = summed
        c = coupling[:, at]
        c2 = (c * c * (1.0 / (rows * width)))[None]
        a = jnp.dot(w[1, :, :rows], summed, preferred_element_type=F32)
        term_own[...] = a
        b = response[...]
        a2, b2 = a * a, b * b
        a3, b3, a2b, ab2 = a2 * a, b2 * b, a2 * b, a * b2
        lines = [squares[...]]
        terms = (a3 * a3, a3 * a2b, a2b * a2b, a3 * b3, ab2 * ab2, ab2 * b3, b3 * b3)
        for term in terms:
            weighted = (term.reshape(rows // orbitals, orbitals, width) * c2).reshape(rows, width)
            lines.append(folded(weighted))
        out[0] = jnp.concatenate(lines, axis=0)

    return call(
        kernel,
        "own_second",
        in_specs=[SCALAR] + [WHOLE] * 6,
        out_specs=[WHOLE] * 3,
        out_shape=[near((rows, width), BF16), near((1, 8, 128), F32), near((rows, width), F32)],
    )(me, mine, theirs, volterra, response, squares, coupling)


def finish_first(me, pieces, g_own, volterra, edge, coupling, bits):
    rows, width = pieces[0].shape
    columns = coupling.shape[1]

    def kernel(me_ref, *refs):
        pieces, (g_own, w, edge, coupling, g_out, cubic, held, sems) = refs[:3], refs[3:]
        place = Place(me_ref[0], bits)

        def write(source, slot):
            at = columns_of(place.quarter_of(slot), width)
            copies.append(pltpu.make_async_copy(source, g_out.at[pl.ds(0, rows), at], sems.at[slot]))
            copies[-1].start()

        copies = []
        write(g_own, 0)
        for i in range(3):
            at = columns_of(place.quarter_of(i + 1), width)
            g = jnp.dot(w[0, :, :rows], pieces[i][...], preferred_element_type=F32)
            g += jnp.dot(w[0, :, rows:], edge[:, at], preferred_element_type=F32)
            held[i] = g.astype(BF16)
            write(held.at[i], i + 1)
            cubic[i] = cubed(g, coupling[:, at])
        for copy in copies:
            copy.wait()

    return call(
        kernel,
        "finish_first",
        in_specs=[SCALAR] + [WHOLE] * 7,
        out_specs=[HBM, WHOLE],
        out_shape=[jax.ShapeDtypeStruct((2 * rows, columns), BF16), near((3, rows, width), F32)],
        scratch_shapes=[pltpu.VMEM((3, rows, width), BF16), pltpu.SemaphoreType.DMA((4,))],
    )(me, *pieces, g_own, volterra, edge, coupling)


def memory_terms(pieces, volterra):
    rows, width = pieces[0].shape
    count = len(pieces)

    def kernel(*refs):
        pieces, (w, out) = refs[:count], refs[count:]
        for slot in range(count):
            out[slot] = jnp.dot(w[1, :, :rows], pieces[slot][...], preferred_element_type=F32)

    return call(
        kernel,
        "memory_terms",
        in_specs=[WHOLE] * (count + 1),
        out_specs=WHOLE,
        out_shape=near((count, rows, width), F32),
    )(*pieces, volterra)


def joined(a, b, *after):
    size = a.shape[0]

    def kernel(a, b, *refs):
        out = refs[-1]
        out[:size] = a[...]
        out[size:] = b[...]

    shape = (2 * size,) + a.shape[1:]
    in_specs = [WHOLE] * 2 + [FAR] * len(after)
    return call(kernel, "joined", in_specs=in_specs, out_specs=WHOLE, out_shape=near(shape, F32))(a, b, *after)


def ordered(x, after):
    def kernel(x, _, out):
        out[...] = x[...]

    return call(kernel, "ordered", in_specs=[WHOLE, FAR], out_specs=WHOLE, out_shape=near(x.shape, x.dtype))(x, after)


def finish_second(me, last, term_own, terms, volterra, cubic_own, cubic, shares, coupling, g_first, bits):
    rows, width = last.shape
    columns = coupling.shape[1]
    everyone = shares.shape[0]

    def kernel(me_ref, last, term_own, terms, w, cubic_own, cubic, shares, coupling, _, g_out, sigma, g_held, s_held, sems):
        place = Place(me_ref[0], bits)
        last_term = jnp.dot(w[1, :, :rows], last[...], preferred_element_type=F32)
        sums = jnp.sum(shares[...], axis=2, keepdims=True)
        means = sums[:, 0:1, :]
        mean = over_halves(means) * (1.0 / everyone)
        ratio = jnp.sqrt((means + EPS) / (mean + EPS))
        power, series = jnp.ones_like(ratio), jnp.zeros_like(ratio)
        for k, weight in enumerate(BINOMIAL):
            series += weight * sums[:, k + 1 : k + 2, :] * power
            power = power * ratio
        scale_0 = (1.0 / jnp.sqrt(mean + EPS))[0]
        scale_1 = (1.0 / jnp.sqrt(jnp.maximum(over_halves(series) * (1.0 / everyone), 0.0) + EPS))[0]

        copies = []

        def write(value, held, slot, out, block, at):
            held[slot] = value
            sem = sems.at[len(copies)]
            copies.append(pltpu.make_async_copy(held.at[slot], out.at[pl.ds(block * rows, rows), at], sem))
            copies[-1].start()

        for slot in (3, 0, 1, 2):
            at = columns_of(place.quarter_of(slot), width)
            before = ((cubic[slot - 1] if slot else cubic_own[...]) * scale_0).astype(BF16)
            write(before, s_held, slot, sigma, 0, at)
            g = last_term if slot == 3 else terms[slot - 1] if slot else term_own[...]
            g += jnp.dot(w[1, :, rows:], before, preferred_element_type=F32)
            write(g.astype(BF16), g_held, slot, g_out, 1, at)
            write((cubed(g, coupling[:, at]) * scale_1).astype(BF16), s_held, 4 + slot, sigma, 1, at)
        for copy in copies:
            copy.wait()

    return call(
        kernel,
        "finish_second",
        in_specs=[SCALAR] + [WHOLE] * 8 + [HBM],
        out_specs=[HBM, HBM],
        out_shape=[jax.ShapeDtypeStruct((2 * rows, columns), BF16)] * 2,
        scratch_shapes=[
            pltpu.VMEM((4, rows, width), BF16),
            pltpu.VMEM((8, rows, width), BF16),
            pltpu.SemaphoreType.DMA((12,)),
        ],
        input_output_aliases={9: 0},
    )(me, last, term_own, terms, volterra, cubic_own, cubic, shares, coupling, g_first)


def per_device(past, second, g_hist, sigma_hist, volterra, sigma_edge, coupling):
    blocks, rows = volterra.shape[:2]
    assert blocks == 2 and past >= 8
    bits = log2(past)
    half = g_hist.shape[1] // 2
    me = lax.axis_index("past").astype(jnp.int32).reshape(1)
    even = list(range(bits))
    odd = even[:1] + even[1:][::-1]

    def swap(x, level):
        pairs = [(d, d ^ (1 << (odd if d % 2 else even)[level])) for d in range(past)]
        return lax.ppermute(x, "past", pairs)

    def exchanged(kept, arrived, sent, after=None):
        mine = combined(kept, arrived, swap(sent, 1), after)
        theirs = swap(mine, 2)
        for level in range(3, bits):
            mine = (mine.astype(F32) + theirs.astype(F32)).astype(BF16)
            theirs = swap(mine, level)
        return mine, theirs

    def passed_on(kept, arrived):
        return (kept[0] + arrived[0].astype(F32)).astype(BF16)

    def widened(share, level):
        return lax.ppermute(share, "second", [(z, z ^ (1 << level)) for z in range(second)])

    send, sigma_0, g_sent, g_kept = first_product(me, sigma_hist, g_hist, rows, half, bits)
    arrived_0 = swap(send, 0)
    kept_0, send, sigma_1 = middle_products(me, sigma_0, g_kept, g_sent, sigma_hist, bits)
    sent_0 = passed_on(kept_0, arrived_0)
    arrived_1 = swap(send, 0)
    kept_1 = last_product(me, sigma_1, g_kept, bits, after=arrived_1)
    sent_1 = passed_on(kept_1, arrived_1)

    mine, theirs = exchanged(kept_0, arrived_0, sent_0, after=sent_1)
    mine_1, theirs_1 = exchanged(kept_1, arrived_1, sent_1)
    own_0, response, squares, g_own, cubic_own = own_first(
        me, mine, theirs, volterra, sigma_edge, coupling, bits, after=mine_1
    )
    own_1, share, term_own = own_second(me, mine_1, theirs_1, volterra, response, squares, coupling, bits)

    rounds = log2(second)
    share = jnp.concatenate([share, widened(share, 0)])
    partner = ordered(swap(own_0, 1), share)
    pieces = [partner, swap(own_0, 0), swap(partner, 0)]
    g_first, cubic = finish_first(me, pieces, g_own, volterra, sigma_edge, coupling, bits)
    for level in range(1, rounds):
        share = jnp.concatenate([share, widened(share, level)])
    partner = ordered(swap(own_1, 1), share)
    terms = memory_terms([partner, swap(own_1, 0)], volterra)
    last = swap(partner, 0)
    share = joined(share, swap(share, 1), cubic, terms)
    shares = jnp.concatenate([share, swap(share, 0)])
    results = finish_second(
        me, last, term_own, terms, volterra, cubic_own, cubic, shares, coupling, g_first, bits
    )
    return tuple(results)


def solution(mesh):
    return jax.shard_map(
        functools.partial(per_device, mesh.shape["past"], mesh.shape["second"]),
        mesh=mesh,
        in_specs=(P("past", "second"), P(None, "past"), P(), P(None, "second"), P(None, "second")),
        out_specs=(P(None, "second"), P(None, "second")),
        check_vma=False,
    )
```

```python
import functools

import jax
import jax.numpy as jnp
from jax import lax
from jax.experimental import pallas as pl
from jax.experimental.pallas import tpu as pltpu
from jax.sharding import PartitionSpec as P

VMEM = 20 * 1024 * 1024
F32 = jnp.float32
BF16 = jnp.bfloat16
EPS = 1e-06
BINOMIAL = (1.0, 6.0, 15.0, 20.0, 15.0, 6.0, 1.0)

WHOLE = pl.BlockSpec(memory_space=pltpu.VMEM)
FAR = pl.BlockSpec(memory_space=pl.ANY)
HBM = pl.BlockSpec(memory_space=pltpu.HBM)
SCALAR = pl.BlockSpec(memory_space=pltpu.SMEM)


def log2(n):
    bits = n.bit_length() - 1
    assert n == 1 << bits
    return bits


def near(shape, dtype):
    return pltpu.VMEM(shape, dtype)


def far(x):
    return pltpu.with_memory_space_constraint(x, pltpu.HBM)


def call(kernel, name, **kwargs):
    return pl.pallas_call(
        kernel,
        name=name,
        compiler_params=pltpu.CompilerParams(vmem_limit_bytes=VMEM),
        cost_estimate=pl.CostEstimate(flops=1024, bytes_accessed=1024, transcendentals=0),
        **kwargs,
    )


class Place:
    def __init__(self, me, bits):
        low, high = (me >> 1) & 1, (me >> (bits - 1)) & 1
        self.core = me & 1
        self.side = jnp.where(self.core == 1, high, low)
        self.other_side = jnp.where(self.core == 1, low, high)

    def quarter(self):
        return self.core * 2 + self.side

    def quarter_of(self, slot):
        if slot < 2:
            return self.core * 2 + (self.side ^ slot)
        return (self.core ^ 1) * 2 + (self.other_side ^ (slot - 2))


def halves_to(out, value, side):
    quarter = out.shape[2]
    for j in range(2):
        out[1 ^ j ^ side] = value[:, j * quarter : (j + 1) * quarter].astype(out.dtype)


def first_products(me, sigma_hist, g_hist, rows, bits):
    depth, columns = g_hist.shape
    half = columns // 2
    parts = 4
    eighth = depth // 8
    chunks = [(0, 2 * eighth), (2 * eighth, 3 * eighth), (5 * eighth, 3 * eighth)]

    def kernel(me_ref, sigma_ref, g_ref, sent, kept, sigma_next, g, sigma, total, sems):
        started = []

        def load(source, target):
            started.append(pltpu.make_async_copy(source, target, sems.at[len(started)]))
            started[-1].start()
            return started[-1]

        pieces = []
        for start, size in chunks:
            piece = []
            for i in range(parts):
                here = pl.ds(i * (rows // parts), rows // parts)
                deep = pl.ds(start, size)
                piece.append(load(sigma_ref.at[here, deep], sigma.at[here, deep]))
                here = pl.ds(start + i * (size // parts), size // parts)
                piece.append(load(g_ref.at[here, :], g.at[here, :]))
            pieces.append(piece)
        ahead = []
        for i in range(2 * parts):
            here = pl.ds(i * (rows // (2 * parts)), rows // (2 * parts))
            there = pl.ds(rows + i * (rows // (2 * parts)), rows // (2 * parts))
            ahead.append(load(sigma_ref.at[there, :], sigma_next.at[here, :]))
        for k, (start, size) in enumerate(chunks):
            for copy in pieces[k]:
                copy.wait()
            deep = pl.ds(start, size)
            term = jnp.dot(sigma[:, deep], g[deep, :], preferred_element_type=F32)
            if k == 0:
                total[...] = term
            else:
                total[...] += term
        place = Place(me_ref[0], bits)
        halves_to(sent, total[:, half_of(place.core ^ 1, half)], place.other_side)
        halves_to(kept, total[:, half_of(place.core, half)], place.side)
        for copy in ahead:
            copy.wait()

    return call(
        kernel,
        "first_products",
        in_specs=[SCALAR, HBM, HBM],
        out_specs=[WHOLE] * 4,
        out_shape=[
            near((2, rows, half // 2), BF16),
            near((2, rows, half // 2), F32),
            near((rows, depth), BF16),
            near((depth, columns), BF16),
        ],
        scratch_shapes=[
            pltpu.VMEM((rows, depth), BF16),
            pltpu.VMEM((rows, columns), F32),
            pltpu.SemaphoreType.DMA((2 * parts * (len(chunks) + 1),)),
        ],
    )(me, far(sigma_hist), far(g_hist))


def half_of(core, half):
    return pl.ds(pl.multiple_of(core * half, half), half)


def product(me, sigma, g, bits, send, after=None):
    rows, half = sigma.shape[0], g.shape[1] // 2

    def kernel(me_ref, sigma, g, *refs):
        place = Place(me_ref[0], bits)
        columns = half_of(place.core ^ int(send), half)
        term = jnp.dot(sigma[...], g[:, columns], preferred_element_type=F32)
        halves_to(refs[-1], term, place.other_side if send else place.side)

    extra = [] if after is None else [after]
    return call(
        kernel,
        "memory_product",
        in_specs=[SCALAR, WHOLE, WHOLE] + [FAR] * len(extra),
        out_specs=WHOLE,
        out_shape=near((2, rows, half // 2), BF16 if send else F32),
    )(me, sigma, g, *extra)


def combined(kept, arrived, more, after):
    rows, width = more.shape
    if after is None:
        return (kept[1] + arrived[1].astype(F32) + more.astype(F32)).astype(BF16)

    def kernel(kept, arrived, more, _, out):
        out[...] = (kept[1] + arrived[1].astype(F32) + more[...].astype(F32)).astype(BF16)

    return call(
        kernel, "combined", in_specs=[WHOLE] * 3 + [FAR], out_specs=WHOLE, out_shape=near((rows, width), BF16)
    )(kept, arrived, more, after)


def cubed(g, coupling):
    orbitals = coupling.shape[0]
    g3 = g.reshape(g.shape[0] // orbitals, orbitals, g.shape[1])
    return (g3 * g3 * g3 * coupling[None]).reshape(g.shape)


def folded(x):
    line = jnp.sum(x, axis=0, keepdims=True)
    parts = [line[:, i : i + 128] for i in range(0, line.shape[1], 128)]
    return functools.reduce(lambda a, b: a + b, parts)


def columns_of(quarter, width):
    return pl.ds(pl.multiple_of(quarter * width, width), width)


def over_halves(x):
    while x.shape[0] > 1:
        half = x.shape[0] // 2
        x = x[:half] + x[half:]
    return x


def own_first(me, mine, theirs, volterra, edge, coupling, bits, after):
    rows, width = mine.shape

    def kernel(me_ref, mine, theirs, w, edge, coupling, _, memory, response, squares, g_own, cubic_own):
        at = columns_of(Place(me_ref[0], bits).quarter(), width)
        summed = (mine[...].astype(F32) + theirs[...].astype(F32)).astype(BF16)
        memory[...] = summed
        g = jnp.dot(w[0, :, :rows], summed, preferred_element_type=F32)
        g += jnp.dot(w[0, :, rows:], edge[:, at], preferred_element_type=F32)
        g_own[...] = g.astype(BF16)
        cubic = cubed(g, coupling[:, at])
        cubic_own[...] = cubic
        line = folded(cubic * cubic * (1.0 / (rows * width)))
        squares[...] = line
        scale = lax.rsqrt(jnp.sum(line) + EPS)
        response[...] = jnp.dot(w[1, :, rows:], (cubic * scale).astype(BF16), preferred_element_type=F32)

    return call(
        kernel,
        "own_first",
        in_specs=[SCALAR] + [WHOLE] * 5 + [FAR],
        out_specs=[WHOLE] * 5,
        out_shape=[
            near((rows, width), BF16),
            near((rows, width), F32),
            near((1, 128), F32),
            near((rows, width), BF16),
            near((rows, width), F32),
        ],
    )(me, mine, theirs, volterra, edge, coupling, after)


def own_second(me, mine, theirs, volterra, response, squares, coupling, bits):
    rows, width = mine.shape
    orbitals = coupling.shape[0]

    def kernel(me_ref, mine, theirs, w, response, squares, coupling, memory, out, term_own):
        at = columns_of(Place(me_ref[0], bits).quarter(), width)
        summed = (mine[...].astype(F32) + theirs[...].astype(F32)).astype(BF16)
        memory[...] = summed
        c = coupling[:, at]
        c2 = (c * c * (1.0 / (rows * width)))[None]
        a = jnp.dot(w[1, :, :rows], summed, preferred_element_type=F32)
        term_own[...] = a
        b = response[...]
        a2, b2 = a * a, b * b
        a3, b3, a2b, ab2 = a2 * a, b2 * b, a2 * b, a * b2
        lines = [squares[...]]
        terms = (a3 * a3, a3 * a2b, a2b * a2b, a3 * b3, ab2 * ab2, ab2 * b3, b3 * b3)
        for term in terms:
            weighted = (term.reshape(rows // orbitals, orbitals, width) * c2).reshape(rows, width)
            lines.append(folded(weighted))
        out[0] = jnp.concatenate(lines, axis=0)

    return call(
        kernel,
        "own_second",
        in_specs=[SCALAR] + [WHOLE] * 6,
        out_specs=[WHOLE] * 3,
        out_shape=[near((rows, width), BF16), near((1, 8, 128), F32), near((rows, width), F32)],
    )(me, mine, theirs, volterra, response, squares, coupling)


def finish_first(me, pieces, g_own, volterra, edge, coupling, bits):
    rows, width = pieces[0].shape
    columns = coupling.shape[1]

    def kernel(me_ref, *refs):
        pieces, (g_own, w, edge, coupling, g_out, cubic, held, sems) = refs[:3], refs[3:]
        place = Place(me_ref[0], bits)

        def write(source, slot):
            at = columns_of(place.quarter_of(slot), width)
            copies.append(pltpu.make_async_copy(source, g_out.at[pl.ds(0, rows), at], sems.at[slot]))
            copies[-1].start()

        copies = []
        write(g_own, 0)
        for i in range(3):
            at = columns_of(place.quarter_of(i + 1), width)
            g = jnp.dot(w[0, :, :rows], pieces[i][...], preferred_element_type=F32)
            g += jnp.dot(w[0, :, rows:], edge[:, at], preferred_element_type=F32)
            held[i] = g.astype(BF16)
            write(held.at[i], i + 1)
            cubic[i] = cubed(g, coupling[:, at])
        for copy in copies:
            copy.wait()

    return call(
        kernel,
        "finish_first",
        in_specs=[SCALAR] + [WHOLE] * 7,
        out_specs=[HBM, WHOLE],
        out_shape=[jax.ShapeDtypeStruct((2 * rows, columns), BF16), near((3, rows, width), F32)],
        scratch_shapes=[pltpu.VMEM((3, rows, width), BF16), pltpu.SemaphoreType.DMA((4,))],
    )(me, *pieces, g_own, volterra, edge, coupling)


def memory_terms(pieces, volterra):
    rows, width = pieces[0].shape
    count = len(pieces)

    def kernel(*refs):
        pieces, (w, out) = refs[:count], refs[count:]
        for slot in range(count):
            out[slot] = jnp.dot(w[1, :, :rows], pieces[slot][...], preferred_element_type=F32)

    return call(
        kernel,
        "memory_terms",
        in_specs=[WHOLE] * (count + 1),
        out_specs=WHOLE,
        out_shape=near((count, rows, width), F32),
    )(*pieces, volterra)


def joined(a, b, *after):
    size = a.shape[0]

    def kernel(a, b, *refs):
        out = refs[-1]
        out[:size] = a[...]
        out[size:] = b[...]

    shape = (2 * size,) + a.shape[1:]
    in_specs = [WHOLE] * 2 + [FAR] * len(after)
    return call(kernel, "joined", in_specs=in_specs, out_specs=WHOLE, out_shape=near(shape, F32))(a, b, *after)


def ordered(x, after):
    def kernel(x, _, out):
        out[...] = x[...]

    return call(kernel, "ordered", in_specs=[WHOLE, FAR], out_specs=WHOLE, out_shape=near(x.shape, x.dtype))(x, after)


def finish_second(me, last, term_own, terms, volterra, cubic_own, cubic, shares, coupling, g_first, bits):
    rows, width = last.shape
    columns = coupling.shape[1]
    everyone = shares.shape[0]

    def kernel(me_ref, last, term_own, terms, w, cubic_own, cubic, shares, coupling, _, g_out, sigma, g_held, s_held, sems):
        place = Place(me_ref[0], bits)
        last_term = jnp.dot(w[1, :, :rows], last[...], preferred_element_type=F32)
        sums = jnp.sum(shares[...], axis=2, keepdims=True)
        means = sums[:, 0:1, :]
        mean = over_halves(means) * (1.0 / everyone)
        ratio = jnp.sqrt((means + EPS) / (mean + EPS))
        power, series = jnp.ones_like(ratio), jnp.zeros_like(ratio)
        for k, weight in enumerate(BINOMIAL):
            series += weight * sums[:, k + 1 : k + 2, :] * power
            power = power * ratio
        scale_0 = (1.0 / jnp.sqrt(mean + EPS))[0]
        scale_1 = (1.0 / jnp.sqrt(jnp.maximum(over_halves(series) * (1.0 / everyone), 0.0) + EPS))[0]

        copies = []

        def write(value, held, slot, out, block, at):
            held[slot] = value
            sem = sems.at[len(copies)]
            copies.append(pltpu.make_async_copy(held.at[slot], out.at[pl.ds(block * rows, rows), at], sem))
            copies[-1].start()

        for slot in (3, 0, 1, 2):
            at = columns_of(place.quarter_of(slot), width)
            before = ((cubic[slot - 1] if slot else cubic_own[...]) * scale_0).astype(BF16)
            write(before, s_held, slot, sigma, 0, at)
            g = last_term if slot == 3 else terms[slot - 1] if slot else term_own[...]
            g += jnp.dot(w[1, :, rows:], before, preferred_element_type=F32)
            write(g.astype(BF16), g_held, slot, g_out, 1, at)
            write((cubed(g, coupling[:, at]) * scale_1).astype(BF16), s_held, 4 + slot, sigma, 1, at)
        for copy in copies:
            copy.wait()

    return call(
        kernel,
        "finish_second",
        in_specs=[SCALAR] + [WHOLE] * 8 + [HBM],
        out_specs=[HBM, HBM],
        out_shape=[jax.ShapeDtypeStruct((2 * rows, columns), BF16)] * 2,
        scratch_shapes=[
            pltpu.VMEM((4, rows, width), BF16),
            pltpu.VMEM((8, rows, width), BF16),
            pltpu.SemaphoreType.DMA((12,)),
        ],
        input_output_aliases={9: 0},
    )(me, last, term_own, terms, volterra, cubic_own, cubic, shares, coupling, g_first)


def per_device(past, second, g_hist, sigma_hist, volterra, sigma_edge, coupling):
    blocks, rows = volterra.shape[:2]
    assert blocks == 2 and past >= 8
    bits = log2(past)
    me = lax.axis_index("past").astype(jnp.int32).reshape(1)
    even = list(range(bits))
    odd = even[:1] + even[1:][::-1]

    def swap(x, level):
        pairs = [(d, d ^ (1 << (odd if d % 2 else even)[level])) for d in range(past)]
        return lax.ppermute(x, "past", pairs)

    def exchanged(kept, arrived, sent, after=None):
        mine = combined(kept, arrived, swap(sent, 1), after)
        theirs = swap(mine, 2)
        for level in range(3, bits):
            mine = (mine.astype(F32) + theirs.astype(F32)).astype(BF16)
            theirs = swap(mine, level)
        return mine, theirs

    def passed_on(kept, arrived):
        return (kept[0] + arrived[0].astype(F32)).astype(BF16)

    def widened(share, level):
        return lax.ppermute(share, "second", [(z, z ^ (1 << level)) for z in range(second)])

    send, kept_0, sigma_1, g_near = first_products(me, sigma_hist, g_hist, rows, bits)
    arrived_0 = swap(send, 0)
    arrived_1 = swap(product(me, sigma_1, g_near, bits, True), 0)
    sent_0 = passed_on(kept_0, arrived_0)
    kept_1 = product(me, sigma_1, g_near, bits, False, after=arrived_1)
    sent_1 = passed_on(kept_1, arrived_1)

    mine, theirs = exchanged(kept_0, arrived_0, sent_0, after=sent_1)
    mine_1, theirs_1 = exchanged(kept_1, arrived_1, sent_1)
    own_0, response, squares, g_own, cubic_own = own_first(
        me, mine, theirs, volterra, sigma_edge, coupling, bits, after=mine_1
    )
    own_1, share, term_own = own_second(me, mine_1, theirs_1, volterra, response, squares, coupling, bits)

    rounds = log2(second)
    share = jnp.concatenate([share, widened(share, 0)])
    partner = ordered(swap(own_0, 1), share)
    pieces = [partner, swap(own_0, 0), swap(partner, 0)]
    g_first, cubic = finish_first(me, pieces, g_own, volterra, sigma_edge, coupling, bits)
    for level in range(1, rounds):
        share = jnp.concatenate([share, widened(share, level)])
    partner = ordered(swap(own_1, 1), share)
    terms = memory_terms([partner, swap(own_1, 0)], volterra)
    last = swap(partner, 0)
    share = joined(share, swap(share, 1), cubic, terms)
    shares = jnp.concatenate([share, swap(share, 0)])
    results = finish_second(
        me, last, term_own, terms, volterra, cubic_own, cubic, shares, coupling, g_first, bits
    )
    return tuple(results)


def solution(mesh):
    return jax.shard_map(
        functools.partial(per_device, mesh.shape["past"], mesh.shape["second"]),
        mesh=mesh,
        in_specs=(P("past", "second"), P(None, "past"), P(), P(None, "second"), P(None, "second")),
        out_specs=(P(None, "second"), P(None, "second")),
        check_vma=False,
    )
```

```python
import functools

import jax
import jax.numpy as jnp
from jax import lax
from jax.experimental import pallas as pl
from jax.experimental.pallas import tpu as pltpu
from jax.sharding import PartitionSpec as P

VMEM = 20 * 1024 * 1024
F32 = jnp.float32
BF16 = jnp.bfloat16
EPS = 1e-06
BINOMIAL = (1.0, 6.0, 15.0, 20.0, 15.0, 6.0, 1.0)

WHOLE = pl.BlockSpec(memory_space=pltpu.VMEM)
FAR = pl.BlockSpec(memory_space=pl.ANY)
HBM = pl.BlockSpec(memory_space=pltpu.HBM)
SCALAR = pl.BlockSpec(memory_space=pltpu.SMEM)


def log2(n):
    bits = n.bit_length() - 1
    assert n == 1 << bits
    return bits


def near(shape, dtype):
    return pltpu.VMEM(shape, dtype)


def far(x):
    return pltpu.with_memory_space_constraint(x, pltpu.HBM)


def call(kernel, name, **kwargs):
    return pl.pallas_call(
        kernel,
        name=name,
        compiler_params=pltpu.CompilerParams(vmem_limit_bytes=VMEM),
        cost_estimate=pl.CostEstimate(flops=1024, bytes_accessed=1024, transcendentals=0),
        **kwargs,
    )


class Place:
    def __init__(self, me, bits):
        low, high = (me >> 1) & 1, (me >> (bits - 1)) & 1
        self.core = me & 1
        self.side = jnp.where(self.core == 1, high, low)
        self.other_side = jnp.where(self.core == 1, low, high)

    def quarter(self):
        return self.core * 2 + self.side

    def quarter_of(self, slot):
        if slot < 2:
            return self.core * 2 + (self.side ^ slot)
        return (self.core ^ 1) * 2 + (self.other_side ^ (slot - 2))


def halves_to(out, value, side):
    quarter = out.shape[2]
    for j in range(2):
        out[1 ^ j ^ side] = value[:, j * quarter : (j + 1) * quarter].astype(out.dtype)


def first_products(me, sigma_hist, g_hist, rows, bits):
    depth, columns = g_hist.shape
    half = columns // 2
    parts = 4
    eighth = depth // 8
    chunks = [(0, eighth), (eighth, 3 * eighth), (4 * eighth, 4 * eighth)]

    def kernel(me_ref, sigma_ref, g_ref, sent, kept, sigma_next, g, sigma, total, sems):
        started = []

        def load(source, target):
            started.append(pltpu.make_async_copy(source, target, sems.at[len(started)]))
            started[-1].start()
            return started[-1]

        pieces = []
        for start, size in chunks:
            piece = []
            for i in range(parts):
                here = pl.ds(i * (rows // parts), rows // parts)
                deep = pl.ds(start, size)
                piece.append(load(sigma_ref.at[here, deep], sigma.at[here, deep]))
                here = pl.ds(start + i * (size // parts), size // parts)
                piece.append(load(g_ref.at[here, :], g.at[here, :]))
            pieces.append(piece)
        ahead = []
        for i in range(2 * parts):
            here = pl.ds(i * (rows // (2 * parts)), rows // (2 * parts))
            there = pl.ds(rows + i * (rows // (2 * parts)), rows // (2 * parts))
            ahead.append(load(sigma_ref.at[there, :], sigma_next.at[here, :]))
        for k, (start, size) in enumerate(chunks):
            for copy in pieces[k]:
                copy.wait()
            deep = pl.ds(start, size)
            term = jnp.dot(sigma[:, deep], g[deep, :], preferred_element_type=F32)
            if k == 0:
                total[...] = term
            else:
                total[...] += term
        place = Place(me_ref[0], bits)
        halves_to(sent, total[:, half_of(place.core ^ 1, half)], place.other_side)
        halves_to(kept, total[:, half_of(place.core, half)], place.side)
        for copy in ahead:
            copy.wait()

    return call(
        kernel,
        "first_products",
        in_specs=[SCALAR, HBM, HBM],
        out_specs=[WHOLE] * 4,
        out_shape=[
            near((2, rows, half // 2), BF16),
            near((2, rows, half // 2), F32),
            near((rows, depth), BF16),
            near((depth, columns), BF16),
        ],
        scratch_shapes=[
            pltpu.VMEM((rows, depth), BF16),
            pltpu.VMEM((rows, columns), F32),
            pltpu.SemaphoreType.DMA((2 * parts * (len(chunks) + 1),)),
        ],
    )(me, far(sigma_hist), far(g_hist))


def half_of(core, half):
    return pl.ds(pl.multiple_of(core * half, half), half)


def product(me, sigma, g, bits, send, after=None):
    rows, half = sigma.shape[0], g.shape[1] // 2

    def kernel(me_ref, sigma, g, *refs):
        place = Place(me_ref[0], bits)
        columns = half_of(place.core ^ int(send), half)
        term = jnp.dot(sigma[...], g[:, columns], preferred_element_type=F32)
        halves_to(refs[-1], term, place.other_side if send else place.side)

    extra = [] if after is None else [after]
    return call(
        kernel,
        "memory_product",
        in_specs=[SCALAR, WHOLE, WHOLE] + [FAR] * len(extra),
        out_specs=WHOLE,
        out_shape=near((2, rows, half // 2), BF16 if send else F32),
    )(me, sigma, g, *extra)


def combined(kept, arrived, more, after):
    rows, width = more.shape
    if after is None:
        return (kept[1] + arrived[1].astype(F32) + more.astype(F32)).astype(BF16)

    def kernel(kept, arrived, more, _, out):
        out[...] = (kept[1] + arrived[1].astype(F32) + more[...].astype(F32)).astype(BF16)

    return call(
        kernel, "combined", in_specs=[WHOLE] * 3 + [FAR], out_specs=WHOLE, out_shape=near((rows, width), BF16)
    )(kept, arrived, more, after)


def cubed(g, coupling):
    orbitals = coupling.shape[0]
    g3 = g.reshape(g.shape[0] // orbitals, orbitals, g.shape[1])
    return (g3 * g3 * g3 * coupling[None]).reshape(g.shape)


def folded(x):
    line = jnp.sum(x, axis=0, keepdims=True)
    parts = [line[:, i : i + 128] for i in range(0, line.shape[1], 128)]
    return functools.reduce(lambda a, b: a + b, parts)


def columns_of(quarter, width):
    return pl.ds(pl.multiple_of(quarter * width, width), width)


def over_halves(x):
    while x.shape[0] > 1:
        half = x.shape[0] // 2
        x = x[:half] + x[half:]
    return x


def own_first(me, mine, theirs, volterra, edge, coupling, bits, after):
    rows, width = mine.shape

    def kernel(me_ref, mine, theirs, w, edge, coupling, _, memory, response, squares, g_own, cubic_own):
        at = columns_of(Place(me_ref[0], bits).quarter(), width)
        summed = (mine[...].astype(F32) + theirs[...].astype(F32)).astype(BF16)
        memory[...] = summed
        g = jnp.dot(w[0, :, :rows], summed, preferred_element_type=F32)
        g += jnp.dot(w[0, :, rows:], edge[:, at], preferred_element_type=F32)
        g_own[...] = g.astype(BF16)
        cubic = cubed(g, coupling[:, at])
        cubic_own[...] = cubic
        line = folded(cubic * cubic * (1.0 / (rows * width)))
        squares[...] = line
        scale = lax.rsqrt(jnp.sum(line) + EPS)
        response[...] = jnp.dot(w[1, :, rows:], (cubic * scale).astype(BF16), preferred_element_type=F32)

    return call(
        kernel,
        "own_first",
        in_specs=[SCALAR] + [WHOLE] * 5 + [FAR],
        out_specs=[WHOLE] * 5,
        out_shape=[
            near((rows, width), BF16),
            near((rows, width), F32),
            near((1, 128), F32),
            near((rows, width), BF16),
            near((rows, width), F32),
        ],
    )(me, mine, theirs, volterra, edge, coupling, after)


def own_second(me, mine, theirs, volterra, response, squares, coupling, bits):
    rows, width = mine.shape
    orbitals = coupling.shape[0]

    def kernel(me_ref, mine, theirs, w, response, squares, coupling, memory, out, term_own):
        at = columns_of(Place(me_ref[0], bits).quarter(), width)
        summed = (mine[...].astype(F32) + theirs[...].astype(F32)).astype(BF16)
        memory[...] = summed
        c = coupling[:, at] * (rows * width) ** -0.5
        a = jnp.dot(w[1, :, :rows], summed, preferred_element_type=F32)
        term_own[...] = a
        b = response[...]

        def weighted(square):
            return (square.reshape(rows // orbitals, orbitals, width) * c[None]).reshape(rows, width)

        ca2, cb2 = weighted(a * a), weighted(b * b)
        ca3, ca2b, cab2, cb3 = ca2 * a, ca2 * b, cb2 * a, cb2 * b
        lines = [squares[...]]
        for x, y in ((ca3, ca3), (ca3, ca2b), (ca2b, ca2b), (ca3, cb3), (cab2, cab2), (cab2, cb3), (cb3, cb3)):
            lines.append(folded(x * y))
        out[0] = jnp.concatenate(lines, axis=0)

    return call(
        kernel,
        "own_second",
        in_specs=[SCALAR] + [WHOLE] * 6,
        out_specs=[WHOLE] * 3,
        out_shape=[near((rows, width), BF16), near((1, 8, 128), F32), near((rows, width), F32)],
    )(me, mine, theirs, volterra, response, squares, coupling)


def finish_first(me, pieces, g_own, volterra, edge, coupling, bits):
    rows, width = pieces[0].shape
    columns = coupling.shape[1]

    def kernel(me_ref, *refs):
        pieces, (g_own, w, edge, coupling, g_out, cubic, held, sems) = refs[:3], refs[3:]
        place = Place(me_ref[0], bits)

        def write(source, slot):
            at = columns_of(place.quarter_of(slot), width)
            copies.append(pltpu.make_async_copy(source, g_out.at[pl.ds(0, rows), at], sems.at[slot]))
            copies[-1].start()

        copies = []
        write(g_own, 0)
        for i in range(3):
            at = columns_of(place.quarter_of(i + 1), width)
            g = jnp.dot(w[0, :, :rows], pieces[i][...], preferred_element_type=F32)
            g += jnp.dot(w[0, :, rows:], edge[:, at], preferred_element_type=F32)
            held[i] = g.astype(BF16)
            write(held.at[i], i + 1)
            cubic[i] = cubed(g, coupling[:, at])
        for copy in copies:
            copy.wait()

    return call(
        kernel,
        "finish_first",
        in_specs=[SCALAR] + [WHOLE] * 7,
        out_specs=[HBM, WHOLE],
        out_shape=[jax.ShapeDtypeStruct((2 * rows, columns), BF16), near((3, rows, width), F32)],
        scratch_shapes=[pltpu.VMEM((3, rows, width), BF16), pltpu.SemaphoreType.DMA((4,))],
    )(me, *pieces, g_own, volterra, edge, coupling)


def memory_terms(pieces, volterra):
    rows, width = pieces[0].shape
    count = len(pieces)

    def kernel(*refs):
        pieces, (w, out) = refs[:count], refs[count:]
        for slot in range(count):
            out[slot] = jnp.dot(w[1, :, :rows], pieces[slot][...], preferred_element_type=F32)

    return call(
        kernel,
        "memory_terms",
        in_specs=[WHOLE] * (count + 1),
        out_specs=WHOLE,
        out_shape=near((count, rows, width), F32),
    )(*pieces, volterra)


def joined(a, b, *after):
    size = a.shape[0]

    def kernel(a, b, *refs):
        out = refs[-1]
        out[:size] = a[...]
        out[size:] = b[...]

    shape = (2 * size,) + a.shape[1:]
    in_specs = [WHOLE] * 2 + [FAR] * len(after)
    return call(kernel, "joined", in_specs=in_specs, out_specs=WHOLE, out_shape=near(shape, F32))(a, b, *after)


def ordered(x, after):
    def kernel(x, _, out):
        out[...] = x[...]

    return call(kernel, "ordered", in_specs=[WHOLE, FAR], out_specs=WHOLE, out_shape=near(x.shape, x.dtype))(x, after)


def finish_second(me, last, term_own, terms, volterra, cubic_own, cubic, shares, coupling, g_first, bits):
    rows, width = last.shape
    columns = coupling.shape[1]
    everyone = shares.shape[0]

    def kernel(me_ref, last, term_own, terms, w, cubic_own, cubic, shares, coupling, _, g_out, sigma, g_held, s_held, sems):
        place = Place(me_ref[0], bits)
        last_term = jnp.dot(w[1, :, :rows], last[...], preferred_element_type=F32)
        sums = jnp.sum(shares[...], axis=2, keepdims=True)
        means = sums[:, 0:1, :]
        mean = over_halves(means) * (1.0 / everyone)
        ratio = jnp.sqrt((means + EPS) / (mean + EPS))
        power, series = jnp.ones_like(ratio), jnp.zeros_like(ratio)
        for k, weight in enumerate(BINOMIAL):
            series += weight * sums[:, k + 1 : k + 2, :] * power
            power = power * ratio
        scale_0 = (1.0 / jnp.sqrt(mean + EPS))[0]
        scale_1 = (1.0 / jnp.sqrt(jnp.maximum(over_halves(series) * (1.0 / everyone), 0.0) + EPS))[0]

        copies = []

        def write(value, held, slot, out, block, at):
            held[slot] = value
            sem = sems.at[len(copies)]
            copies.append(pltpu.make_async_copy(held.at[slot], out.at[pl.ds(block * rows, rows), at], sem))
            copies[-1].start()

        for slot in (3, 0, 1, 2):
            at = columns_of(place.quarter_of(slot), width)
            before = ((cubic[slot - 1] if slot else cubic_own[...]) * scale_0).astype(BF16)
            write(before, s_held, slot, sigma, 0, at)
            g = last_term if slot == 3 else terms[slot - 1] if slot else term_own[...]
            g += jnp.dot(w[1, :, rows:], before, preferred_element_type=F32)
            write(g.astype(BF16), g_held, slot, g_out, 1, at)
            write(cubed(g, coupling[:, at] * scale_1).astype(BF16), s_held, 4 + slot, sigma, 1, at)
        for copy in copies:
            copy.wait()

    return call(
        kernel,
        "finish_second",
        in_specs=[SCALAR] + [WHOLE] * 8 + [HBM],
        out_specs=[HBM, HBM],
        out_shape=[jax.ShapeDtypeStruct((2 * rows, columns), BF16)] * 2,
        scratch_shapes=[
            pltpu.VMEM((4, rows, width), BF16),
            pltpu.VMEM((8, rows, width), BF16),
            pltpu.SemaphoreType.DMA((12,)),
        ],
        input_output_aliases={9: 0},
    )(me, last, term_own, terms, volterra, cubic_own, cubic, shares, coupling, g_first)


def per_device(past, second, g_hist, sigma_hist, volterra, sigma_edge, coupling):
    blocks, rows = volterra.shape[:2]
    assert blocks == 2 and past >= 8
    bits = log2(past)
    me = lax.axis_index("past").astype(jnp.int32).reshape(1)
    even = list(range(bits))
    odd = even[:1] + even[1:][::-1]

    def swap(x, level):
        pairs = [(d, d ^ (1 << (odd if d % 2 else even)[level])) for d in range(past)]
        return lax.ppermute(x, "past", pairs)

    def exchanged(kept, arrived, sent, after=None):
        mine = combined(kept, arrived, swap(sent, 1), after)
        theirs = swap(mine, 2)
        for level in range(3, bits):
            mine = (mine.astype(F32) + theirs.astype(F32)).astype(BF16)
            theirs = swap(mine, level)
        return mine, theirs

    def passed_on(kept, arrived):
        return (kept[0] + arrived[0].astype(F32)).astype(BF16)

    def widened(share, level):
        return lax.ppermute(share, "second", [(z, z ^ (1 << level)) for z in range(second)])

    send, kept_0, sigma_1, g_near = first_products(me, sigma_hist, g_hist, rows, bits)
    arrived_0 = swap(send, 0)
    arrived_1 = swap(product(me, sigma_1, g_near, bits, True), 0)
    sent_0 = passed_on(kept_0, arrived_0)
    kept_1 = product(me, sigma_1, g_near, bits, False, after=arrived_1)
    sent_1 = passed_on(kept_1, arrived_1)

    mine, theirs = exchanged(kept_0, arrived_0, sent_0, after=sent_1)
    mine_1, theirs_1 = exchanged(kept_1, arrived_1, sent_1)
    own_0, response, squares, g_own, cubic_own = own_first(
        me, mine, theirs, volterra, sigma_edge, coupling, bits, after=mine_1
    )
    own_1, share, term_own = own_second(me, mine_1, theirs_1, volterra, response, squares, coupling, bits)

    rounds = log2(second)
    share = jnp.concatenate([share, widened(share, rounds - 1)])
    partner = ordered(swap(own_0, 1), share)
    pieces = [partner, swap(own_0, 0), swap(partner, 0)]
    g_first, cubic = finish_first(me, pieces, g_own, volterra, sigma_edge, coupling, bits)
    for level in reversed(range(rounds - 1)):
        share = jnp.concatenate([share, widened(share, level)])
    partner = ordered(swap(own_1, 1), share)
    terms = memory_terms([partner, swap(own_1, 0)], volterra)
    last = swap(partner, 0)
    share = joined(share, swap(share, 1), cubic, terms)
    shares = jnp.concatenate([share, swap(share, 0)])
    results = finish_second(
        me, last, term_own, terms, volterra, cubic_own, cubic, shares, coupling, g_first, bits
    )
    return tuple(results)


def solution(mesh):
    return jax.shard_map(
        functools.partial(per_device, mesh.shape["past"], mesh.shape["second"]),
        mesh=mesh,
        in_specs=(P("past", "second"), P(None, "past"), P(), P(None, "second"), P(None, "second")),
        out_specs=(P(None, "second"), P(None, "second")),
        check_vma=False,
    )
```

```python
import functools

import jax
import jax.numpy as jnp
from jax import lax
from jax.experimental import pallas as pl
from jax.experimental.pallas import tpu as pltpu
from jax.sharding import PartitionSpec as P

VMEM = 20 * 1024 * 1024
F32 = jnp.float32
BF16 = jnp.bfloat16
EPS = 1e-06
BINOMIAL = (1.0, 6.0, 15.0, 20.0, 15.0, 6.0, 1.0)

WHOLE = pl.BlockSpec(memory_space=pltpu.VMEM)
FAR = pl.BlockSpec(memory_space=pl.ANY)
HBM = pl.BlockSpec(memory_space=pltpu.HBM)
SCALAR = pl.BlockSpec(memory_space=pltpu.SMEM)


def log2(n):
    bits = n.bit_length() - 1
    assert n == 1 << bits
    return bits


def near(shape, dtype):
    return pltpu.VMEM(shape, dtype)


def far(x):
    return pltpu.with_memory_space_constraint(x, pltpu.HBM)


def call(kernel, name, **kwargs):
    return pl.pallas_call(
        kernel,
        name=name,
        compiler_params=pltpu.CompilerParams(vmem_limit_bytes=VMEM),
        cost_estimate=pl.CostEstimate(flops=1024, bytes_accessed=1024, transcendentals=0),
        **kwargs,
    )


class Place:
    def __init__(self, me, bits):
        low, high = (me >> 1) & 1, (me >> (bits - 1)) & 1
        self.core = me & 1
        self.side = jnp.where(self.core == 1, high, low)
        self.other_side = jnp.where(self.core == 1, low, high)

    def quarter(self):
        return self.core * 2 + self.side

    def quarter_of(self, slot):
        if slot < 2:
            return self.core * 2 + (self.side ^ slot)
        return (self.core ^ 1) * 2 + (self.other_side ^ (slot - 2))


def halves_to(out, value, side):
    quarter = out.shape[2]
    for j in range(2):
        out[1 ^ j ^ side] = value[:, j * quarter : (j + 1) * quarter].astype(out.dtype)


def first_products(me, sigma_hist, g_hist, rows, bits):
    depth, columns = g_hist.shape
    half = columns // 2
    parts = 4
    eighth = depth // 8
    chunks = [(0, 2 * eighth), (2 * eighth, 3 * eighth), (5 * eighth, 3 * eighth)]

    def kernel(me_ref, sigma_ref, g_ref, sent, kept, sigma_next, g, sigma, total, sems):
        started = []

        def load(source, target):
            started.append(pltpu.make_async_copy(source, target, sems.at[len(started)]))
            started[-1].start()
            return started[-1]

        pieces = []
        for start, size in chunks:
            piece = []
            for i in range(parts):
                here = pl.ds(i * (rows // parts), rows // parts)
                deep = pl.ds(start, size)
                piece.append(load(sigma_ref.at[here, deep], sigma.at[here, deep]))
                here = pl.ds(start + i * (size // parts), size // parts)
                piece.append(load(g_ref.at[here, :], g.at[here, :]))
            pieces.append(piece)
        ahead = []
        for i in range(2 * parts):
            here = pl.ds(i * (rows // (2 * parts)), rows // (2 * parts))
            there = pl.ds(rows + i * (rows // (2 * parts)), rows // (2 * parts))
            ahead.append(load(sigma_ref.at[there, :], sigma_next.at[here, :]))
        for k, (start, size) in enumerate(chunks):
            for copy in pieces[k]:
                copy.wait()
            deep = pl.ds(start, size)
            term = jnp.dot(sigma[:, deep], g[deep, :], preferred_element_type=F32)
            if k == 0:
                total[...] = term
            else:
                total[...] += term
        place = Place(me_ref[0], bits)
        halves_to(sent, total[:, half_of(place.core ^ 1, half)], place.other_side)
        halves_to(kept, total[:, half_of(place.core, half)], place.side)
        for copy in ahead:
            copy.wait()

    return call(
        kernel,
        "first_products",
        in_specs=[SCALAR, HBM, HBM],
        out_specs=[WHOLE] * 4,
        out_shape=[
            near((2, rows, half // 2), BF16),
            near((2, rows, half // 2), F32),
            near((rows, depth), BF16),
            near((depth, columns), BF16),
        ],
        scratch_shapes=[
            pltpu.VMEM((rows, depth), BF16),
            pltpu.VMEM((rows, columns), F32),
            pltpu.SemaphoreType.DMA((2 * parts * (len(chunks) + 1),)),
        ],
    )(me, far(sigma_hist), far(g_hist))


def half_of(core, half):
    return pl.ds(pl.multiple_of(core * half, half), half)


def product(me, sigma, g, bits, send, after=None):
    rows, half = sigma.shape[0], g.shape[1] // 2

    def kernel(me_ref, sigma, g, *refs):
        place = Place(me_ref[0], bits)
        columns = half_of(place.core ^ int(send), half)
        term = jnp.dot(sigma[...], g[:, columns], preferred_element_type=F32)
        halves_to(refs[-1], term, place.other_side if send else place.side)

    extra = [] if after is None else [after]
    return call(
        kernel,
        "memory_product",
        in_specs=[SCALAR, WHOLE, WHOLE] + [FAR] * len(extra),
        out_specs=WHOLE,
        out_shape=near((2, rows, half // 2), BF16 if send else F32),
    )(me, sigma, g, *extra)


def combined(kept, arrived, more, after):
    rows, width = more.shape
    if after is None:
        return (kept[1] + arrived[1].astype(F32) + more.astype(F32)).astype(BF16)

    def kernel(kept, arrived, more, _, out):
        out[...] = (kept[1] + arrived[1].astype(F32) + more[...].astype(F32)).astype(BF16)

    return call(
        kernel, "combined", in_specs=[WHOLE] * 3 + [FAR], out_specs=WHOLE, out_shape=near((rows, width), BF16)
    )(kept, arrived, more, after)


def cubed(g, coupling):
    orbitals = coupling.shape[0]
    g3 = g.reshape(g.shape[0] // orbitals, orbitals, g.shape[1])
    return (g3 * g3 * g3 * coupling[None]).reshape(g.shape)


def folded(x):
    line = jnp.sum(x, axis=0, keepdims=True)
    parts = [line[:, i : i + 128] for i in range(0, line.shape[1], 128)]
    return functools.reduce(lambda a, b: a + b, parts)


def columns_of(quarter, width):
    return pl.ds(pl.multiple_of(quarter * width, width), width)


def over_halves(x):
    while x.shape[0] > 1:
        half = x.shape[0] // 2
        x = x[:half] + x[half:]
    return x


def own_first(me, mine, theirs, volterra, edge, coupling, bits, after):
    rows, width = mine.shape

    def kernel(me_ref, mine, theirs, w, edge, coupling, _, memory, response, squares, g_own, cubic_own):
        at = columns_of(Place(me_ref[0], bits).quarter(), width)
        summed = (mine[...].astype(F32) + theirs[...].astype(F32)).astype(BF16)
        memory[...] = summed
        g = jnp.dot(w[0, :, :rows], summed, preferred_element_type=F32)
        g += jnp.dot(w[0, :, rows:], edge[:, at], preferred_element_type=F32)
        g_own[...] = g.astype(BF16)
        cubic = cubed(g, coupling[:, at])
        cubic_own[...] = cubic
        line = folded(cubic * cubic * (1.0 / (rows * width)))
        squares[...] = line
        scale = lax.rsqrt(jnp.sum(line) + EPS)
        response[...] = jnp.dot(w[1, :, rows:], (cubic * scale).astype(BF16), preferred_element_type=F32)

    return call(
        kernel,
        "own_first",
        in_specs=[SCALAR] + [WHOLE] * 5 + [FAR],
        out_specs=[WHOLE] * 5,
        out_shape=[
            near((rows, width), BF16),
            near((rows, width), F32),
            near((1, 128), F32),
            near((rows, width), BF16),
            near((rows, width), F32),
        ],
    )(me, mine, theirs, volterra, edge, coupling, after)


def own_second(me, mine, theirs, volterra, response, squares, coupling, bits):
    rows, width = mine.shape
    orbitals = coupling.shape[0]

    def kernel(me_ref, mine, theirs, w, response, squares, coupling, memory, out, term_own):
        at = columns_of(Place(me_ref[0], bits).quarter(), width)
        summed = (mine[...].astype(F32) + theirs[...].astype(F32)).astype(BF16)
        memory[...] = summed
        c = coupling[:, at] * (rows * width) ** -0.5
        a = jnp.dot(w[1, :, :rows], summed, preferred_element_type=F32)
        term_own[...] = a
        b = response[...]

        def weighted(square):
            return (square.reshape(rows // orbitals, orbitals, width) * c[None]).reshape(rows, width)

        ca2, cb2 = weighted(a * a), weighted(b * b)
        ca3, ca2b, cab2, cb3 = ca2 * a, ca2 * b, cb2 * a, cb2 * b
        lines = [squares[...]]
        for x, y in ((ca3, ca3), (ca3, ca2b), (ca2b, ca2b), (ca3, cb3), (cab2, cab2), (cab2, cb3), (cb3, cb3)):
            lines.append(folded(x * y))
        out[0] = jnp.concatenate(lines, axis=0)

    return call(
        kernel,
        "own_second",
        in_specs=[SCALAR] + [WHOLE] * 6,
        out_specs=[WHOLE] * 3,
        out_shape=[near((rows, width), BF16), near((1, 8, 128), F32), near((rows, width), F32)],
    )(me, mine, theirs, volterra, response, squares, coupling)


def finish_first(me, pieces, g_own, volterra, edge, coupling, bits):
    rows, width = pieces[0].shape
    columns = coupling.shape[1]

    def kernel(me_ref, *refs):
        pieces, (g_own, w, edge, coupling, g_out, cubic, held, sems) = refs[:3], refs[3:]
        place = Place(me_ref[0], bits)

        def write(source, slot):
            at = columns_of(place.quarter_of(slot), width)
            copies.append(pltpu.make_async_copy(source, g_out.at[pl.ds(0, rows), at], sems.at[slot]))
            copies[-1].start()

        copies = []
        write(g_own, 0)
        for i in range(3):
            at = columns_of(place.quarter_of(i + 1), width)
            g = jnp.dot(w[0, :, :rows], pieces[i][...], preferred_element_type=F32)
            g += jnp.dot(w[0, :, rows:], edge[:, at], preferred_element_type=F32)
            held[i] = g.astype(BF16)
            write(held.at[i], i + 1)
            cubic[i] = cubed(g, coupling[:, at])
        for copy in copies:
            copy.wait()

    return call(
        kernel,
        "finish_first",
        in_specs=[SCALAR] + [WHOLE] * 7,
        out_specs=[HBM, WHOLE],
        out_shape=[jax.ShapeDtypeStruct((2 * rows, columns), BF16), near((3, rows, width), F32)],
        scratch_shapes=[pltpu.VMEM((3, rows, width), BF16), pltpu.SemaphoreType.DMA((4,))],
    )(me, *pieces, g_own, volterra, edge, coupling)


def memory_terms(pieces, volterra):
    rows, width = pieces[0].shape
    count = len(pieces)

    def kernel(*refs):
        pieces, (w, out) = refs[:count], refs[count:]
        for slot in range(count):
            out[slot] = jnp.dot(w[1, :, :rows], pieces[slot][...], preferred_element_type=F32)

    return call(
        kernel,
        "memory_terms",
        in_specs=[WHOLE] * (count + 1),
        out_specs=WHOLE,
        out_shape=near((count, rows, width), F32),
    )(*pieces, volterra)


def joined(parts, after=()):
    size = parts[0].shape[0]

    def kernel(*refs):
        out = refs[-1]
        for i in range(len(parts)):
            out[i * size : (i + 1) * size] = refs[i][...]

    return call(
        kernel,
        "joined",
        in_specs=[WHOLE] * len(parts) + [FAR] * len(after),
        out_specs=WHOLE,
        out_shape=near((len(parts) * size,) + parts[0].shape[1:], F32),
    )(*parts, *after)


def ordered(x, after):
    def kernel(x, _, out):
        out[...] = x[...]

    return call(kernel, "ordered", in_specs=[WHOLE, FAR], out_specs=WHOLE, out_shape=near(x.shape, x.dtype))(x, after)


def finish_second(me, last, term_own, terms, volterra, cubic_own, cubic, shares, coupling, g_first, bits):
    rows, width = last.shape
    columns = coupling.shape[1]
    everyone = shares.shape[0]

    def kernel(me_ref, last, term_own, terms, w, cubic_own, cubic, shares, coupling, _, g_out, sigma, g_held, s_held, sems):
        place = Place(me_ref[0], bits)
        last_term = jnp.dot(w[1, :, :rows], last[...], preferred_element_type=F32)
        sums = jnp.sum(shares[...], axis=2, keepdims=True)
        means = sums[:, 0:1, :]
        mean = over_halves(means) * (1.0 / everyone)
        ratio = jnp.sqrt((means + EPS) / (mean + EPS))
        power, series = jnp.ones_like(ratio), jnp.zeros_like(ratio)
        for k, weight in enumerate(BINOMIAL):
            series += weight * sums[:, k + 1 : k + 2, :] * power
            power = power * ratio
        scale_0 = (1.0 / jnp.sqrt(mean + EPS))[0]
        scale_1 = (1.0 / jnp.sqrt(jnp.maximum(over_halves(series) * (1.0 / everyone), 0.0) + EPS))[0]

        copies = []

        def write(value, held, slot, out, block, at):
            held[slot] = value
            sem = sems.at[len(copies)]
            copies.append(pltpu.make_async_copy(held.at[slot], out.at[pl.ds(block * rows, rows), at], sem))
            copies[-1].start()

        for slot in (3, 0, 1, 2):
            at = columns_of(place.quarter_of(slot), width)
            before = ((cubic[slot - 1] if slot else cubic_own[...]) * scale_0).astype(BF16)
            write(before, s_held, slot, sigma, 0, at)
            g = last_term if slot == 3 else terms[slot - 1] if slot else term_own[...]
            g += jnp.dot(w[1, :, rows:], before, preferred_element_type=F32)
            write(g.astype(BF16), g_held, slot, g_out, 1, at)
            write(cubed(g, coupling[:, at] * scale_1).astype(BF16), s_held, 4 + slot, sigma, 1, at)
        for copy in copies:
            copy.wait()

    return call(
        kernel,
        "finish_second",
        in_specs=[SCALAR] + [WHOLE] * 8 + [HBM],
        out_specs=[HBM, HBM],
        out_shape=[jax.ShapeDtypeStruct((2 * rows, columns), BF16)] * 2,
        scratch_shapes=[
            pltpu.VMEM((4, rows, width), BF16),
            pltpu.VMEM((8, rows, width), BF16),
            pltpu.SemaphoreType.DMA((12,)),
        ],
        input_output_aliases={9: 0},
    )(me, last, term_own, terms, volterra, cubic_own, cubic, shares, coupling, g_first)


def per_device(past, second, g_hist, sigma_hist, volterra, sigma_edge, coupling):
    blocks, rows = volterra.shape[:2]
    assert blocks == 2 and past >= 8
    bits = log2(past)
    me = lax.axis_index("past").astype(jnp.int32).reshape(1)
    even = list(range(bits))
    odd = even[:1] + even[1:][::-1]

    def swap(x, level):
        pairs = [(d, d ^ (1 << (odd if d % 2 else even)[level])) for d in range(past)]
        return lax.ppermute(x, "past", pairs)

    def exchanged(kept, arrived, sent, after=None):
        mine = combined(kept, arrived, swap(sent, 1), after)
        theirs = swap(mine, 2)
        for level in range(3, bits):
            mine = (mine.astype(F32) + theirs.astype(F32)).astype(BF16)
            theirs = swap(mine, level)
        return mine, theirs

    def passed_on(kept, arrived):
        return (kept[0] + arrived[0].astype(F32)).astype(BF16)

    def from_far(x):
        flip = [d ^ 1 ^ (1 << (even if d % 2 else odd)[1]) for d in range(past)]
        return lax.ppermute(x, "past", [(flip[d], d) for d in range(past)])

    def widened(share, level):
        return lax.ppermute(share, "second", [(z, z ^ (1 << level)) for z in range(second)])

    send, kept_0, sigma_1, g_near = first_products(me, sigma_hist, g_hist, rows, bits)
    arrived_0 = swap(send, 0)
    arrived_1 = swap(product(me, sigma_1, g_near, bits, True), 0)
    sent_0 = passed_on(kept_0, arrived_0)
    kept_1 = product(me, sigma_1, g_near, bits, False, after=arrived_1)
    sent_1 = passed_on(kept_1, arrived_1)

    mine, theirs = exchanged(kept_0, arrived_0, sent_0, after=sent_1)
    mine_1, theirs_1 = exchanged(kept_1, arrived_1, sent_1)
    own_0, response, squares, g_own, cubic_own = own_first(
        me, mine, theirs, volterra, sigma_edge, coupling, bits, after=mine_1
    )
    own_1, share, term_own = own_second(me, mine_1, theirs_1, volterra, response, squares, coupling, bits)

    rounds = log2(second)
    share = jnp.concatenate([share, widened(share, rounds - 1)])
    partner = ordered(swap(own_0, 1), share)
    pieces = [partner, swap(own_0, 0), swap(partner, 0)]
    g_first, cubic = finish_first(me, pieces, g_own, volterra, sigma_edge, coupling, bits)
    for level in reversed(range(rounds - 1)):
        share = jnp.concatenate([share, widened(share, level)])
    partner = ordered(swap(own_1, 1), share)
    terms = memory_terms([partner, swap(own_1, 0)], volterra)
    last = swap(partner, 0)
    shares = joined([share, swap(share, 0), swap(share, 1), from_far(share)], [cubic, terms])
    results = finish_second(
        me, last, term_own, terms, volterra, cubic_own, cubic, shares, coupling, g_first, bits
    )
    return tuple(results)


def solution(mesh):
    return jax.shard_map(
        functools.partial(per_device, mesh.shape["past"], mesh.shape["second"]),
        mesh=mesh,
        in_specs=(P("past", "second"), P(None, "past"), P(), P(None, "second"), P(None, "second")),
        out_specs=(P(None, "second"), P(None, "second")),
        check_vma=False,
    )
```

```python
import functools

import jax
import jax.numpy as jnp
from jax import lax
from jax.experimental import pallas as pl
from jax.experimental.pallas import tpu as pltpu
from jax.sharding import PartitionSpec as P

VMEM = 20 * 1024 * 1024
F32 = jnp.float32
BF16 = jnp.bfloat16
EPS = 1e-06
BINOMIAL = (1.0, 6.0, 15.0, 20.0, 15.0, 6.0, 1.0)

WHOLE = pl.BlockSpec(memory_space=pltpu.VMEM)
FAR = pl.BlockSpec(memory_space=pl.ANY)
HBM = pl.BlockSpec(memory_space=pltpu.HBM)
SCALAR = pl.BlockSpec(memory_space=pltpu.SMEM)


def log2(n):
    bits = n.bit_length() - 1
    assert n == 1 << bits
    return bits


def near(shape, dtype):
    return pltpu.VMEM(shape, dtype)


def far(x):
    return pltpu.with_memory_space_constraint(x, pltpu.HBM)


def call(kernel, name, **kwargs):
    return pl.pallas_call(
        kernel,
        name=name,
        compiler_params=pltpu.CompilerParams(vmem_limit_bytes=VMEM),
        cost_estimate=pl.CostEstimate(flops=1024, bytes_accessed=1024, transcendentals=0),
        **kwargs,
    )


class Place:
    def __init__(self, me, bits):
        low, high = (me >> 1) & 1, (me >> (bits - 1)) & 1
        self.core = me & 1
        self.side = jnp.where(self.core == 1, high, low)
        self.other_side = jnp.where(self.core == 1, low, high)

    def quarter(self):
        return self.core * 2 + self.side

    def quarter_of(self, slot):
        if slot < 2:
            return self.core * 2 + (self.side ^ slot)
        return (self.core ^ 1) * 2 + (self.other_side ^ (slot - 2))


def halves_to(out, value, side):
    quarter = out.shape[2]
    for j in range(2):
        out[1 ^ j ^ side] = value[:, j * quarter : (j + 1) * quarter].astype(out.dtype)


def first_products(me, sigma_hist, g_hist, rows, bits):
    depth, columns = g_hist.shape
    half = columns // 2
    parts = 4
    eighth = depth // 8
    chunks = [(0, 2 * eighth), (2 * eighth, 3 * eighth), (5 * eighth, 3 * eighth)]

    def kernel(me_ref, sigma_ref, g_ref, sent, kept, sigma_next, g, sigma, total, sems):
        started = []

        def load(source, target):
            started.append(pltpu.make_async_copy(source, target, sems.at[len(started)]))
            started[-1].start()
            return started[-1]

        pieces = []
        for start, size in chunks:
            piece = []
            for i in range(parts):
                here = pl.ds(i * (rows // parts), rows // parts)
                deep = pl.ds(start, size)
                piece.append(load(sigma_ref.at[here, deep], sigma.at[here, deep]))
                here = pl.ds(start + i * (size // parts), size // parts)
                piece.append(load(g_ref.at[here, :], g.at[here, :]))
            pieces.append(piece)
        ahead = []
        for i in range(2 * parts):
            here = pl.ds(i * (rows // (2 * parts)), rows // (2 * parts))
            there = pl.ds(rows + i * (rows // (2 * parts)), rows // (2 * parts))
            ahead.append(load(sigma_ref.at[there, :], sigma_next.at[here, :]))
        for k, (start, size) in enumerate(chunks):
            for copy in pieces[k]:
                copy.wait()
            deep = pl.ds(start, size)
            term = jnp.dot(sigma[:, deep], g[deep, :], preferred_element_type=F32)
            if k == 0:
                total[...] = term
            else:
                total[...] += term
        place = Place(me_ref[0], bits)
        halves_to(sent, total[:, half_of(place.core ^ 1, half)], place.other_side)
        halves_to(kept, total[:, half_of(place.core, half)], place.side)
        for copy in ahead:
            copy.wait()

    return call(
        kernel,
        "first_products",
        in_specs=[SCALAR, HBM, HBM],
        out_specs=[WHOLE] * 4,
        out_shape=[
            near((2, rows, half // 2), BF16),
            near((2, rows, half // 2), F32),
            near((rows, depth), BF16),
            near((depth, columns), BF16),
        ],
        scratch_shapes=[
            pltpu.VMEM((rows, depth), BF16),
            pltpu.VMEM((rows, columns), F32),
            pltpu.SemaphoreType.DMA((2 * parts * (len(chunks) + 1),)),
        ],
    )(me, far(sigma_hist), far(g_hist))


def half_of(core, half):
    return pl.ds(pl.multiple_of(core * half, half), half)


def product(me, sigma, g, bits, send, after=None):
    rows, half = sigma.shape[0], g.shape[1] // 2

    def kernel(me_ref, sigma, g, *refs):
        place = Place(me_ref[0], bits)
        columns = half_of(place.core ^ int(send), half)
        term = jnp.dot(sigma[...], g[:, columns], preferred_element_type=F32)
        halves_to(refs[-1], term, place.other_side if send else place.side)

    extra = [] if after is None else [after]
    return call(
        kernel,
        "memory_product",
        in_specs=[SCALAR, WHOLE, WHOLE] + [FAR] * len(extra),
        out_specs=WHOLE,
        out_shape=near((2, rows, half // 2), BF16 if send else F32),
    )(me, sigma, g, *extra)


def combined(kept, arrived, more, after):
    rows, width = more.shape
    if after is None:
        return (kept[1] + arrived[1].astype(F32) + more.astype(F32)).astype(BF16)

    def kernel(kept, arrived, more, _, out):
        out[...] = (kept[1] + arrived[1].astype(F32) + more[...].astype(F32)).astype(BF16)

    return call(
        kernel, "combined", in_specs=[WHOLE] * 3 + [FAR], out_specs=WHOLE, out_shape=near((rows, width), BF16)
    )(kept, arrived, more, after)


def cubed(g, coupling):
    orbitals = coupling.shape[0]
    g3 = g.reshape(g.shape[0] // orbitals, orbitals, g.shape[1])
    return (g3 * g3 * g3 * coupling[None]).reshape(g.shape)


def folded(x):
    line = jnp.sum(x, axis=0, keepdims=True)
    parts = [line[:, i : i + 128] for i in range(0, line.shape[1], 128)]
    return functools.reduce(lambda a, b: a + b, parts)


def columns_of(quarter, width):
    return pl.ds(pl.multiple_of(quarter * width, width), width)


def over_halves(x):
    while x.shape[0] > 1:
        half = x.shape[0] // 2
        x = x[:half] + x[half:]
    return x


def own_first(me, mine, theirs, volterra, edge, coupling, bits, after):
    rows, width = mine.shape

    def kernel(me_ref, mine, theirs, w, edge, coupling, _, memory, response, squares, g_own, cubic_own):
        at = columns_of(Place(me_ref[0], bits).quarter(), width)
        summed = (mine[...].astype(F32) + theirs[...].astype(F32)).astype(BF16)
        memory[...] = summed
        g = jnp.dot(w[0, :, :rows], summed, preferred_element_type=F32)
        g += jnp.dot(w[0, :, rows:], edge[:, at], preferred_element_type=F32)
        g_own[...] = g.astype(BF16)
        cubic = cubed(g, coupling[:, at])
        cubic_own[...] = cubic
        line = folded(cubic * cubic * (1.0 / (rows * width)))
        squares[...] = line
        scale = lax.rsqrt(jnp.sum(line) + EPS)
        response[...] = jnp.dot(w[1, :, rows:], (cubic * scale).astype(BF16), preferred_element_type=F32)

    return call(
        kernel,
        "own_first",
        in_specs=[SCALAR] + [WHOLE] * 5 + [FAR],
        out_specs=[WHOLE] * 5,
        out_shape=[
            near((rows, width), BF16),
            near((rows, width), F32),
            near((1, 128), F32),
            near((rows, width), BF16),
            near((rows, width), F32),
        ],
    )(me, mine, theirs, volterra, edge, coupling, after)


def own_second(me, mine, theirs, volterra, response, squares, coupling, bits):
    rows, width = mine.shape
    orbitals = coupling.shape[0]

    def kernel(me_ref, mine, theirs, w, response, squares, coupling, memory, out, term_own):
        at = columns_of(Place(me_ref[0], bits).quarter(), width)
        summed = (mine[...].astype(F32) + theirs[...].astype(F32)).astype(BF16)
        memory[...] = summed
        c = coupling[:, at] * (rows * width) ** -0.5
        a = jnp.dot(w[1, :, :rows], summed, preferred_element_type=F32)
        term_own[...] = a
        b = response[...]

        def weighted(square):
            return (square.reshape(rows // orbitals, orbitals, width) * c[None]).reshape(rows, width)

        ca2, cb2 = weighted(a * a), weighted(b * b)
        ca3, ca2b, cab2, cb3 = ca2 * a, ca2 * b, cb2 * a, cb2 * b
        lines = [squares[...]]
        for x, y in ((ca3, ca3), (ca3, ca2b), (ca2b, ca2b), (ca3, cb3), (cab2, cab2), (cab2, cb3), (cb3, cb3)):
            lines.append(folded(x * y))
        out[0] = jnp.concatenate(lines, axis=0)

    return call(
        kernel,
        "own_second",
        in_specs=[SCALAR] + [WHOLE] * 6,
        out_specs=[WHOLE] * 3,
        out_shape=[near((rows, width), BF16), near((1, 8, 128), F32), near((rows, width), F32)],
    )(me, mine, theirs, volterra, response, squares, coupling)


def finish_other(me, piece, volterra, edge, coupling, bits):
    rows, width = piece.shape

    def kernel(me_ref, piece, w, edge, coupling, g_out, cubic):
        at = columns_of(Place(me_ref[0], bits).quarter_of(2), width)
        g = jnp.dot(w[0, :, :rows], piece[...], preferred_element_type=F32)
        g += jnp.dot(w[0, :, rows:], edge[:, at], preferred_element_type=F32)
        g_out[...] = g.astype(BF16)
        cubic[...] = cubed(g, coupling[:, at])

    return call(
        kernel,
        "finish_other",
        in_specs=[SCALAR] + [WHOLE] * 4,
        out_specs=[WHOLE] * 2,
        out_shape=[near((rows, width), BF16), near((rows, width), F32)],
    )(me, piece, volterra, edge, coupling)


def finish_first(me, pieces, g_own, g_other, volterra, edge, coupling, bits):
    rows, width = pieces[0].shape
    columns = coupling.shape[1]

    def kernel(me_ref, *refs):
        pieces, (g_own, g_other, w, edge, coupling, g_out, cubic, held, sems) = refs[:2], refs[2:]
        place = Place(me_ref[0], bits)

        def write(source, slot):
            at = columns_of(place.quarter_of(slot), width)
            copies.append(pltpu.make_async_copy(source, g_out.at[pl.ds(0, rows), at], sems.at[slot]))
            copies[-1].start()

        copies = []
        write(g_own, 0)
        write(g_other, 2)
        for i, slot in enumerate((1, 3)):
            at = columns_of(place.quarter_of(slot), width)
            g = jnp.dot(w[0, :, :rows], pieces[i][...], preferred_element_type=F32)
            g += jnp.dot(w[0, :, rows:], edge[:, at], preferred_element_type=F32)
            held[i] = g.astype(BF16)
            write(held.at[i], slot)
            cubic[i] = cubed(g, coupling[:, at])
        for copy in copies:
            copy.wait()

    return call(
        kernel,
        "finish_first",
        in_specs=[SCALAR] + [WHOLE] * 7,
        out_specs=[HBM, WHOLE],
        out_shape=[jax.ShapeDtypeStruct((2 * rows, columns), BF16), near((2, rows, width), F32)],
        scratch_shapes=[pltpu.VMEM((2, rows, width), BF16), pltpu.SemaphoreType.DMA((4,))],
    )(me, *pieces, g_own, g_other, volterra, edge, coupling)


def memory_terms(pieces, volterra):
    rows, width = pieces[0].shape
    count = len(pieces)

    def kernel(*refs):
        pieces, (w, out) = refs[:count], refs[count:]
        for slot in range(count):
            out[slot] = jnp.dot(w[1, :, :rows], pieces[slot][...], preferred_element_type=F32)

    return call(
        kernel,
        "memory_terms",
        in_specs=[WHOLE] * (count + 1),
        out_specs=WHOLE,
        out_shape=near((count, rows, width), F32),
    )(*pieces, volterra)


def joined(parts, after=()):
    size = parts[0].shape[0]

    def kernel(*refs):
        out = refs[-1]
        for i in range(len(parts)):
            out[i * size : (i + 1) * size] = refs[i][...]

    return call(
        kernel,
        "joined",
        in_specs=[WHOLE] * len(parts) + [FAR] * len(after),
        out_specs=WHOLE,
        out_shape=near((len(parts) * size,) + parts[0].shape[1:], F32),
    )(*parts, *after)


def ordered(x, *after):
    def kernel(x, *refs):
        refs[-1][...] = x[...]

    in_specs = [WHOLE] + [FAR] * len(after)
    return call(kernel, "ordered", in_specs=in_specs, out_specs=WHOLE, out_shape=near(x.shape, x.dtype))(x, *after)


def finish_second(me, last, term_own, terms, volterra, cubic_own, cubic_other, cubic, shares, coupling, g_first, bits):
    rows, width = last.shape
    columns = coupling.shape[1]
    everyone = shares.shape[0]

    def kernel(me_ref, *refs):
        last, term_own, terms, w, cubic_own, cubic_other, cubic, shares, coupling, _ = refs[:10]
        g_out, sigma, g_held, s_held, sems = refs[10:]
        place = Place(me_ref[0], bits)
        last_term = jnp.dot(w[1, :, :rows], last[...], preferred_element_type=F32)
        sums = jnp.sum(shares[...], axis=2, keepdims=True)
        means = sums[:, 0:1, :]
        mean = over_halves(means) * (1.0 / everyone)
        ratio = jnp.sqrt((means + EPS) / (mean + EPS))
        power, series = jnp.ones_like(ratio), jnp.zeros_like(ratio)
        for k, weight in enumerate(BINOMIAL):
            series += weight * sums[:, k + 1 : k + 2, :] * power
            power = power * ratio
        scale_0 = (1.0 / jnp.sqrt(mean + EPS))[0]
        scale_1 = (1.0 / jnp.sqrt(jnp.maximum(over_halves(series) * (1.0 / everyone), 0.0) + EPS))[0]

        copies = []

        def write(value, held, slot, out, block, at):
            held[slot] = value
            sem = sems.at[len(copies)]
            copies.append(pltpu.make_async_copy(held.at[slot], out.at[pl.ds(block * rows, rows), at], sem))
            copies[-1].start()

        cubic_at = [cubic_own, cubic.at[0], cubic_other, cubic.at[1]]
        for slot in (3, 0, 1, 2):
            at = columns_of(place.quarter_of(slot), width)
            before = (cubic_at[slot][...] * scale_0).astype(BF16)
            write(before, s_held, slot, sigma, 0, at)
            g = last_term if slot == 3 else terms[slot - 1] if slot else term_own[...]
            g += jnp.dot(w[1, :, rows:], before, preferred_element_type=F32)
            write(g.astype(BF16), g_held, slot, g_out, 1, at)
            write(cubed(g, coupling[:, at] * scale_1).astype(BF16), s_held, 4 + slot, sigma, 1, at)
        for copy in copies:
            copy.wait()

    return call(
        kernel,
        "finish_second",
        in_specs=[SCALAR] + [WHOLE] * 9 + [HBM],
        out_specs=[HBM, HBM],
        out_shape=[jax.ShapeDtypeStruct((2 * rows, columns), BF16)] * 2,
        scratch_shapes=[
            pltpu.VMEM((4, rows, width), BF16),
            pltpu.VMEM((8, rows, width), BF16),
            pltpu.SemaphoreType.DMA((12,)),
        ],
        input_output_aliases={10: 0},
    )(me, last, term_own, terms, volterra, cubic_own, cubic_other, cubic, shares, coupling, g_first)


def per_device(past, second, g_hist, sigma_hist, volterra, sigma_edge, coupling):
    blocks, rows = volterra.shape[:2]
    assert blocks == 2 and past >= 8
    bits = log2(past)
    me = lax.axis_index("past").astype(jnp.int32).reshape(1)
    even = list(range(bits))
    odd = even[:1] + even[1:][::-1]

    def swap(x, level):
        pairs = [(d, d ^ (1 << (odd if d % 2 else even)[level])) for d in range(past)]
        return lax.ppermute(x, "past", pairs)

    def exchanged(kept, arrived, sent, after=None):
        mine = combined(kept, arrived, swap(sent, 1), after)
        theirs = swap(mine, 2)
        for level in range(3, bits):
            mine = (mine.astype(F32) + theirs.astype(F32)).astype(BF16)
            theirs = swap(mine, level)
        return mine, theirs

    def passed_on(kept, arrived):
        return (kept[0] + arrived[0].astype(F32)).astype(BF16)

    def from_far(x):
        flip = [d ^ 1 ^ (1 << (even if d % 2 else odd)[1]) for d in range(past)]
        return lax.ppermute(x, "past", [(flip[d], d) for d in range(past)])

    def widened(share, level):
        return lax.ppermute(share, "second", [(z, z ^ (1 << level)) for z in range(second)])

    send, kept_0, sigma_1, g_near = first_products(me, sigma_hist, g_hist, rows, bits)
    arrived_0 = swap(send, 0)
    arrived_1 = swap(product(me, sigma_1, g_near, bits, True), 0)
    sent_0 = passed_on(kept_0, arrived_0)
    kept_1 = product(me, sigma_1, g_near, bits, False, after=arrived_1)
    sent_1 = passed_on(kept_1, arrived_1)

    mine, theirs = exchanged(kept_0, arrived_0, sent_0, after=sent_1)
    mine_1, theirs_1 = exchanged(kept_1, arrived_1, sent_1)
    own_0, response, squares, g_own, cubic_own = own_first(
        me, mine, theirs, volterra, sigma_edge, coupling, bits, after=mine_1
    )
    own_1, share, term_own = own_second(me, mine_1, theirs_1, volterra, response, squares, coupling, bits)
    g_other, cubic_other = finish_other(me, swap(own_0, 0), volterra, sigma_edge, coupling, bits)

    rounds = log2(second)
    share = jnp.concatenate([share, widened(share, 0)])
    partner = ordered(swap(own_0, 1), share, cubic_other)
    pieces = [partner, swap(partner, 0)]
    g_first, cubic = finish_first(me, pieces, g_own, g_other, volterra, sigma_edge, coupling, bits)
    for level in range(1, rounds):
        share = jnp.concatenate([share, widened(share, level)])
    partner = ordered(swap(own_1, 1), share)
    terms = memory_terms([partner, swap(own_1, 0)], volterra)
    last = swap(partner, 0)
    shares = joined([share, swap(share, 0), swap(share, 1), from_far(share)], [cubic, terms])
    results = finish_second(
        me, last, term_own, terms, volterra, cubic_own, cubic_other, cubic, shares, coupling, g_first, bits
    )
    return tuple(results)


def solution(mesh):
    return jax.shard_map(
        functools.partial(per_device, mesh.shape["past"], mesh.shape["second"]),
        mesh=mesh,
        in_specs=(P("past", "second"), P(None, "past"), P(), P(None, "second"), P(None, "second")),
        out_specs=(P(None, "second"), P(None, "second")),
        check_vma=False,
    )
```

```python
import functools

import jax
import jax.numpy as jnp
from jax import lax
from jax.experimental import pallas as pl
from jax.experimental.pallas import tpu as pltpu
from jax.sharding import PartitionSpec as P

VMEM = 20 * 1024 * 1024
F32 = jnp.float32
BF16 = jnp.bfloat16
EPS = 1e-06
BINOMIAL = (1.0, 6.0, 15.0, 20.0, 15.0, 6.0, 1.0)

WHOLE = pl.BlockSpec(memory_space=pltpu.VMEM)
FAR = pl.BlockSpec(memory_space=pl.ANY)
HBM = pl.BlockSpec(memory_space=pltpu.HBM)
SCALAR = pl.BlockSpec(memory_space=pltpu.SMEM)


def log2(n):
    bits = n.bit_length() - 1
    assert n == 1 << bits
    return bits


def near(shape, dtype):
    return pltpu.VMEM(shape, dtype)


def far(x):
    return pltpu.with_memory_space_constraint(x, pltpu.HBM)


def call(kernel, name, **kwargs):
    return pl.pallas_call(
        kernel,
        name=name,
        compiler_params=pltpu.CompilerParams(vmem_limit_bytes=VMEM),
        cost_estimate=pl.CostEstimate(flops=1024, bytes_accessed=1024, transcendentals=0),
        **kwargs,
    )


class Place:
    def __init__(self, me, bits):
        low, high = (me >> 1) & 1, (me >> (bits - 1)) & 1
        self.core = me & 1
        self.side = jnp.where(self.core == 1, high, low)
        self.other_side = jnp.where(self.core == 1, low, high)

    def quarter(self):
        return self.core * 2 + self.side

    def quarter_of(self, slot):
        if slot < 2:
            return self.core * 2 + (self.side ^ slot)
        return (self.core ^ 1) * 2 + (self.other_side ^ (slot - 2))


def halves_to(out, value, side):
    quarter = out.shape[2]
    for j in range(2):
        out[1 ^ j ^ side] = value[:, j * quarter : (j + 1) * quarter].astype(out.dtype)


def first_products(me, sigma_hist, g_hist, rows, bits):
    depth, columns = g_hist.shape
    half = columns // 2
    parts = 4
    unit = depth // 16
    chunks, start = [], 0
    for units in (2, 3, 4, 4, 3):
        chunks.append((start * unit, units * unit))
        start += units

    def kernel(me_ref, sigma_ref, g_ref, sent, kept, sigma_next, g, sigma, total, sems):
        started = []

        def load(source, target):
            started.append(pltpu.make_async_copy(source, target, sems.at[len(started)]))
            started[-1].start()
            return started[-1]

        pieces = []
        for start, size in chunks:
            piece = []
            for i in range(parts):
                here = pl.ds(i * (rows // parts), rows // parts)
                deep = pl.ds(start, size)
                piece.append(load(sigma_ref.at[here, deep], sigma.at[here, deep]))
                here = pl.ds(start + i * (size // parts), size // parts)
                piece.append(load(g_ref.at[here, :], g.at[here, :]))
            pieces.append(piece)
        ahead = []
        for i in range(2 * parts):
            here = pl.ds(i * (rows // (2 * parts)), rows // (2 * parts))
            there = pl.ds(rows + i * (rows // (2 * parts)), rows // (2 * parts))
            ahead.append(load(sigma_ref.at[there, :], sigma_next.at[here, :]))
        for k, (start, size) in enumerate(chunks):
            for copy in pieces[k]:
                copy.wait()
            deep = pl.ds(start, size)
            term = jnp.dot(sigma[:, deep], g[deep, :], preferred_element_type=F32)
            if k == 0:
                total[...] = term
            else:
                total[...] += term
        place = Place(me_ref[0], bits)
        halves_to(sent, total[:, half_of(place.core ^ 1, half)], place.other_side)
        halves_to(kept, total[:, half_of(place.core, half)], place.side)
        for copy in ahead:
            copy.wait()

    return call(
        kernel,
        "first_products",
        in_specs=[SCALAR, HBM, HBM],
        out_specs=[WHOLE] * 4,
        out_shape=[
            near((2, rows, half // 2), BF16),
            near((2, rows, half // 2), F32),
            near((rows, depth), BF16),
            near((depth, columns), BF16),
        ],
        scratch_shapes=[
            pltpu.VMEM((rows, depth), BF16),
            pltpu.VMEM((rows, columns), F32),
            pltpu.SemaphoreType.DMA((2 * parts * (len(chunks) + 1),)),
        ],
    )(me, far(sigma_hist), far(g_hist))


def half_of(core, half):
    return pl.ds(pl.multiple_of(core * half, half), half)


def product(me, sigma, g, bits, send, after=None):
    rows, half = sigma.shape[0], g.shape[1] // 2

    def kernel(me_ref, sigma, g, *refs):
        place = Place(me_ref[0], bits)
        columns = half_of(place.core ^ int(send), half)
        term = jnp.dot(sigma[...], g[:, columns], preferred_element_type=F32)
        halves_to(refs[-1], term, place.other_side if send else place.side)

    extra = [] if after is None else [after]
    return call(
        kernel,
        "memory_product",
        in_specs=[SCALAR, WHOLE, WHOLE] + [FAR] * len(extra),
        out_specs=WHOLE,
        out_shape=near((2, rows, half // 2), BF16 if send else F32),
    )(me, sigma, g, *extra)


def combined(kept, arrived, more, after):
    rows, width = more.shape
    if after is None:
        return (kept[1] + arrived[1].astype(F32) + more.astype(F32)).astype(BF16)

    def kernel(kept, arrived, more, _, out):
        out[...] = (kept[1] + arrived[1].astype(F32) + more[...].astype(F32)).astype(BF16)

    return call(
        kernel, "combined", in_specs=[WHOLE] * 3 + [FAR], out_specs=WHOLE, out_shape=near((rows, width), BF16)
    )(kept, arrived, more, after)


def cubed(g, coupling):
    orbitals = coupling.shape[0]
    g3 = g.reshape(g.shape[0] // orbitals, orbitals, g.shape[1])
    return (g3 * g3 * g3 * coupling[None]).reshape(g.shape)


def folded(x):
    line = jnp.sum(x, axis=0, keepdims=True)
    parts = [line[:, i : i + 128] for i in range(0, line.shape[1], 128)]
    return functools.reduce(lambda a, b: a + b, parts)


def columns_of(quarter, width):
    return pl.ds(pl.multiple_of(quarter * width, width), width)


def over_halves(x):
    while x.shape[0] > 1:
        half = x.shape[0] // 2
        x = x[:half] + x[half:]
    return x


def own_first(me, mine, theirs, volterra, edge, coupling, bits, after):
    rows, width = mine.shape

    def kernel(me_ref, mine, theirs, w, edge, coupling, _, memory, response, squares, g_own, cubic_own):
        at = columns_of(Place(me_ref[0], bits).quarter(), width)
        summed = (mine[...].astype(F32) + theirs[...].astype(F32)).astype(BF16)
        memory[...] = summed
        g = jnp.dot(w[0, :, :rows], summed, preferred_element_type=F32)
        g += jnp.dot(w[0, :, rows:], edge[:, at], preferred_element_type=F32)
        g_own[...] = g.astype(BF16)
        cubic = cubed(g, coupling[:, at])
        cubic_own[...] = cubic
        line = folded(cubic * cubic * (1.0 / (rows * width)))
        squares[...] = line
        scale = lax.rsqrt(jnp.sum(line) + EPS)
        response[...] = jnp.dot(w[1, :, rows:], (cubic * scale).astype(BF16), preferred_element_type=F32)

    return call(
        kernel,
        "own_first",
        in_specs=[SCALAR] + [WHOLE] * 5 + [FAR],
        out_specs=[WHOLE] * 5,
        out_shape=[
            near((rows, width), BF16),
            near((rows, width), F32),
            near((1, 128), F32),
            near((rows, width), BF16),
            near((rows, width), F32),
        ],
    )(me, mine, theirs, volterra, edge, coupling, after)


def own_second(me, mine, theirs, volterra, response, squares, coupling, bits):
    rows, width = mine.shape
    orbitals = coupling.shape[0]

    def kernel(me_ref, mine, theirs, w, response, squares, coupling, memory, out, term_own):
        at = columns_of(Place(me_ref[0], bits).quarter(), width)
        summed = (mine[...].astype(F32) + theirs[...].astype(F32)).astype(BF16)
        memory[...] = summed
        c = coupling[:, at] * (rows * width) ** -0.5
        a = jnp.dot(w[1, :, :rows], summed, preferred_element_type=F32)
        term_own[...] = a
        b = response[...]

        def weighted(square):
            return (square.reshape(rows // orbitals, orbitals, width) * c[None]).reshape(rows, width)

        ca2, cb2 = weighted(a * a), weighted(b * b)
        ca3, ca2b, cab2, cb3 = ca2 * a, ca2 * b, cb2 * a, cb2 * b
        lines = [squares[...]]
        for x, y in ((ca3, ca3), (ca3, ca2b), (ca2b, ca2b), (ca3, cb3), (cab2, cab2), (cab2, cb3), (cb3, cb3)):
            lines.append(folded(x * y))
        out[0] = jnp.concatenate(lines, axis=0)

    return call(
        kernel,
        "own_second",
        in_specs=[SCALAR] + [WHOLE] * 6,
        out_specs=[WHOLE] * 3,
        out_shape=[near((rows, width), BF16), near((1, 8, 128), F32), near((rows, width), F32)],
    )(me, mine, theirs, volterra, response, squares, coupling)


def finish_other(me, piece, volterra, edge, coupling, bits):
    rows, width = piece.shape

    def kernel(me_ref, piece, w, edge, coupling, g_out, cubic):
        at = columns_of(Place(me_ref[0], bits).quarter_of(2), width)
        g = jnp.dot(w[0, :, :rows], piece[...], preferred_element_type=F32)
        g += jnp.dot(w[0, :, rows:], edge[:, at], preferred_element_type=F32)
        g_out[...] = g.astype(BF16)
        cubic[...] = cubed(g, coupling[:, at])

    return call(
        kernel,
        "finish_other",
        in_specs=[SCALAR] + [WHOLE] * 4,
        out_specs=[WHOLE] * 2,
        out_shape=[near((rows, width), BF16), near((rows, width), F32)],
    )(me, piece, volterra, edge, coupling)


def finish_first(me, pieces, g_own, g_other, volterra, edge, coupling, bits):
    rows, width = pieces[0].shape
    columns = coupling.shape[1]

    def kernel(me_ref, *refs):
        pieces, (g_own, g_other, w, edge, coupling, g_out, cubic, held, sems) = refs[:2], refs[2:]
        place = Place(me_ref[0], bits)

        def write(source, slot):
            at = columns_of(place.quarter_of(slot), width)
            copies.append(pltpu.make_async_copy(source, g_out.at[pl.ds(0, rows), at], sems.at[slot]))
            copies[-1].start()

        copies = []
        write(g_own, 0)
        write(g_other, 2)
        for i, slot in enumerate((1, 3)):
            at = columns_of(place.quarter_of(slot), width)
            g = jnp.dot(w[0, :, :rows], pieces[i][...], preferred_element_type=F32)
            g += jnp.dot(w[0, :, rows:], edge[:, at], preferred_element_type=F32)
            held[i] = g.astype(BF16)
            write(held.at[i], slot)
            cubic[i] = cubed(g, coupling[:, at])
        for copy in copies:
            copy.wait()

    return call(
        kernel,
        "finish_first",
        in_specs=[SCALAR] + [WHOLE] * 7,
        out_specs=[HBM, WHOLE],
        out_shape=[jax.ShapeDtypeStruct((2 * rows, columns), BF16), near((2, rows, width), F32)],
        scratch_shapes=[pltpu.VMEM((2, rows, width), BF16), pltpu.SemaphoreType.DMA((4,))],
    )(me, *pieces, g_own, g_other, volterra, edge, coupling)


def memory_terms(pieces, volterra):
    rows, width = pieces[0].shape
    count = len(pieces)

    def kernel(*refs):
        pieces, (w, out) = refs[:count], refs[count:]
        for slot in range(count):
            out[slot] = jnp.dot(w[1, :, :rows], pieces[slot][...], preferred_element_type=F32)

    return call(
        kernel,
        "memory_terms",
        in_specs=[WHOLE] * (count + 1),
        out_specs=WHOLE,
        out_shape=near((count, rows, width), F32),
    )(*pieces, volterra)


def joined(parts, after=()):
    size = parts[0].shape[0]

    def kernel(*refs):
        out = refs[-1]
        for i in range(len(parts)):
            out[i * size : (i + 1) * size] = refs[i][...]

    return call(
        kernel,
        "joined",
        in_specs=[WHOLE] * len(parts) + [FAR] * len(after),
        out_specs=WHOLE,
        out_shape=near((len(parts) * size,) + parts[0].shape[1:], F32),
    )(*parts, *after)


def ordered(x, *after):
    def kernel(x, *refs):
        refs[-1][...] = x[...]

    in_specs = [WHOLE] + [FAR] * len(after)
    return call(kernel, "ordered", in_specs=in_specs, out_specs=WHOLE, out_shape=near(x.shape, x.dtype))(x, *after)


def finish_second(me, last, term_own, terms, volterra, cubic_own, cubic_other, cubic, shares, coupling, g_first, bits):
    rows, width = last.shape
    columns = coupling.shape[1]
    everyone = shares.shape[0]

    def kernel(me_ref, *refs):
        last, term_own, terms, w, cubic_own, cubic_other, cubic, shares, coupling, _ = refs[:10]
        g_out, sigma, g_held, s_held, sems = refs[10:]
        place = Place(me_ref[0], bits)
        last_term = jnp.dot(w[1, :, :rows], last[...], preferred_element_type=F32)
        sums = jnp.sum(shares[...], axis=2, keepdims=True)
        means = sums[:, 0:1, :]
        mean = over_halves(means) * (1.0 / everyone)
        ratio = jnp.sqrt((means + EPS) / (mean + EPS))
        power, series = jnp.ones_like(ratio), jnp.zeros_like(ratio)
        for k, weight in enumerate(BINOMIAL):
            series += weight * sums[:, k + 1 : k + 2, :] * power
            power = power * ratio
        scale_0 = (1.0 / jnp.sqrt(mean + EPS))[0]
        scale_1 = (1.0 / jnp.sqrt(jnp.maximum(over_halves(series) * (1.0 / everyone), 0.0) + EPS))[0]

        copies = []

        def write(value, held, slot, out, block, at):
            held[slot] = value
            sem = sems.at[len(copies)]
            copies.append(pltpu.make_async_copy(held.at[slot], out.at[pl.ds(block * rows, rows), at], sem))
            copies[-1].start()

        cubic_at = [cubic_own, cubic.at[0], cubic_other, cubic.at[1]]
        def response(slot):
            before = (cubic_at[slot][...] * scale_0).astype(BF16)
            write(before, s_held, slot, sigma, 0, columns_of(place.quarter_of(slot), width))
            g = last_term if slot == 3 else terms[slot - 1] if slot else term_own[...]
            return g + jnp.dot(w[1, :, rows:], before, preferred_element_type=F32)

        slots = (3, 0, 1, 2)
        g = response(slots[0])
        for i, slot in enumerate(slots):
            following = response(slots[i + 1]) if i + 1 < len(slots) else None
            at = columns_of(place.quarter_of(slot), width)
            write(g.astype(BF16), g_held, slot, g_out, 1, at)
            write(cubed(g, coupling[:, at] * scale_1).astype(BF16), s_held, 4 + slot, sigma, 1, at)
            g = following
        for copy in copies:
            copy.wait()

    return call(
        kernel,
        "finish_second",
        in_specs=[SCALAR] + [WHOLE] * 9 + [HBM],
        out_specs=[HBM, HBM],
        out_shape=[jax.ShapeDtypeStruct((2 * rows, columns), BF16)] * 2,
        scratch_shapes=[
            pltpu.VMEM((4, rows, width), BF16),
            pltpu.VMEM((8, rows, width), BF16),
            pltpu.SemaphoreType.DMA((12,)),
        ],
        input_output_aliases={10: 0},
    )(me, last, term_own, terms, volterra, cubic_own, cubic_other, cubic, shares, coupling, g_first)


def per_device(past, second, g_hist, sigma_hist, volterra, sigma_edge, coupling):
    blocks, rows = volterra.shape[:2]
    assert blocks == 2 and past >= 8
    bits = log2(past)
    me = lax.axis_index("past").astype(jnp.int32).reshape(1)
    even = list(range(bits))
    odd = even[:1] + even[1:][::-1]

    def swap(x, level):
        pairs = [(d, d ^ (1 << (odd if d % 2 else even)[level])) for d in range(past)]
        return lax.ppermute(x, "past", pairs)

    def exchanged(kept, arrived, sent, after=None):
        mine = combined(kept, arrived, swap(sent, 1), after)
        theirs = swap(mine, 2)
        for level in range(3, bits):
            mine = (mine.astype(F32) + theirs.astype(F32)).astype(BF16)
            theirs = swap(mine, level)
        return mine, theirs

    def passed_on(kept, arrived):
        return (kept[0] + arrived[0].astype(F32)).astype(BF16)

    def from_far(x):
        flip = [d ^ 1 ^ (1 << (even if d % 2 else odd)[1]) for d in range(past)]
        return lax.ppermute(x, "past", [(flip[d], d) for d in range(past)])

    def widened(share, level):
        return lax.ppermute(share, "second", [(z, z ^ (1 << level)) for z in range(second)])

    send, kept_0, sigma_1, g_near = first_products(me, sigma_hist, g_hist, rows, bits)
    arrived_0 = swap(send, 0)
    arrived_1 = swap(product(me, sigma_1, g_near, bits, True), 0)
    sent_0 = passed_on(kept_0, arrived_0)
    kept_1 = product(me, sigma_1, g_near, bits, False, after=arrived_1)
    sent_1 = passed_on(kept_1, arrived_1)

    mine, theirs = exchanged(kept_0, arrived_0, sent_0, after=sent_1)
    mine_1, theirs_1 = exchanged(kept_1, arrived_1, sent_1)
    own_0, response, squares, g_own, cubic_own = own_first(
        me, mine, theirs, volterra, sigma_edge, coupling, bits, after=mine_1
    )
    own_1, share, term_own = own_second(me, mine_1, theirs_1, volterra, response, squares, coupling, bits)
    g_other, cubic_other = finish_other(me, swap(own_0, 0), volterra, sigma_edge, coupling, bits)

    rounds = log2(second)
    share = jnp.concatenate([share, widened(share, 0)])
    partner = ordered(swap(own_0, 1), share, cubic_other)
    pieces = [partner, swap(partner, 0)]
    g_first, cubic = finish_first(me, pieces, g_own, g_other, volterra, sigma_edge, coupling, bits)
    for level in range(1, rounds):
        share = jnp.concatenate([share, widened(share, level)])
    partner = ordered(swap(own_1, 1), share)
    terms = memory_terms([partner, swap(own_1, 0)], volterra)
    last = swap(partner, 0)
    shares = joined([share, swap(share, 0), swap(share, 1), from_far(share)], [cubic, terms])
    results = finish_second(
        me, last, term_own, terms, volterra, cubic_own, cubic_other, cubic, shares, coupling, g_first, bits
    )
    return tuple(results)


def solution(mesh):
    return jax.shard_map(
        functools.partial(per_device, mesh.shape["past"], mesh.shape["second"]),
        mesh=mesh,
        in_specs=(P("past", "second"), P(None, "past"), P(), P(None, "second"), P(None, "second")),
        out_specs=(P(None, "second"), P(None, "second")),
        check_vma=False,
    )
```

```python
import functools

import jax
import jax.numpy as jnp
from jax import lax
from jax.experimental import pallas as pl
from jax.experimental.pallas import tpu as pltpu
from jax.sharding import PartitionSpec as P

VMEM = 20 * 1024 * 1024
F32 = jnp.float32
BF16 = jnp.bfloat16
EPS = 1e-06
BINOMIAL = (1.0, 6.0, 15.0, 20.0, 15.0, 6.0, 1.0)

WHOLE = pl.BlockSpec(memory_space=pltpu.VMEM)
FAR = pl.BlockSpec(memory_space=pl.ANY)
HBM = pl.BlockSpec(memory_space=pltpu.HBM)
SCALAR = pl.BlockSpec(memory_space=pltpu.SMEM)


def log2(n):
    bits = n.bit_length() - 1
    assert n == 1 << bits
    return bits


def near(shape, dtype):
    return pltpu.VMEM(shape, dtype)


def far(x):
    return pltpu.with_memory_space_constraint(x, pltpu.HBM)


def call(kernel, name, **kwargs):
    return pl.pallas_call(
        kernel,
        name=name,
        compiler_params=pltpu.CompilerParams(vmem_limit_bytes=VMEM),
        cost_estimate=pl.CostEstimate(flops=1024, bytes_accessed=1024, transcendentals=0),
        **kwargs,
    )


class Place:
    def __init__(self, me, bits):
        low, high = (me >> 1) & 1, (me >> (bits - 1)) & 1
        self.core = me & 1
        self.side = jnp.where(self.core == 1, high, low)
        self.other_side = jnp.where(self.core == 1, low, high)

    def quarter(self):
        return self.core * 2 + self.side

    def quarter_of(self, slot):
        if slot < 2:
            return self.core * 2 + (self.side ^ slot)
        return (self.core ^ 1) * 2 + (self.other_side ^ (slot - 2))


def halves_to(out, value, side):
    quarter = out.shape[2]
    for j in range(2):
        out[1 ^ j ^ side] = value[:, j * quarter : (j + 1) * quarter].astype(out.dtype)


def first_products(me, sigma_hist, g_hist, rows, bits):
    depth, columns = g_hist.shape
    half = columns // 2
    parts = 4
    eighth = depth // 8
    chunks = [(0, 2 * eighth), (2 * eighth, 3 * eighth), (5 * eighth, 3 * eighth)]

    def kernel(me_ref, sigma_ref, g_ref, sent, kept, sigma_next, g, sigma, total, sems):
        def piece(k):
            start, size = chunks[k]
            copies, deep = [], pl.ds(start, size)
            for i in range(parts):
                here = pl.ds(i * (rows // parts), rows // parts)
                copies.append((sigma_ref.at[here, deep], sigma.at[here, deep]))
                here = pl.ds(start + i * (size // parts), size // parts)
                copies.append((g_ref.at[here, :], g.at[here, :]))
            return copies

        def next_rows():
            copies, part = [], rows // (2 * parts)
            for i in range(2 * parts):
                here = pl.ds(i * part, part)
                copies.append((sigma_ref.at[pl.ds(rows + i * part, part), :], sigma_next.at[here, :]))
            return copies

        def start(copies, group):
            copies = [
                pltpu.make_async_copy(source, target, sems.at[2 * parts * group + i])
                for i, (source, target) in enumerate(copies)
            ]
            for copy in copies:
                copy.start()
            return copies

        loads = [start(piece(0), 0), start(piece(1), 1)]
        for k, (first, size) in enumerate(chunks):
            for copy in loads[k]:
                copy.wait()
            if k + 2 < len(chunks):
                loads.append(start(piece(k + 2), k + 2))
            if k + 3 == len(chunks):
                loads.append(start(next_rows(), len(chunks)))
            deep = pl.ds(first, size)
            term = jnp.dot(sigma[:, deep], g[deep, :], preferred_element_type=F32)
            if k == 0:
                total[...] = term
            else:
                total[...] += term
        place = Place(me_ref[0], bits)
        halves_to(sent, total[:, half_of(place.core ^ 1, half)], place.other_side)
        halves_to(kept, total[:, half_of(place.core, half)], place.side)
        for copy in loads[-1]:
            copy.wait()

    return call(
        kernel,
        "first_products",
        in_specs=[SCALAR, HBM, HBM],
        out_specs=[WHOLE] * 4,
        out_shape=[
            near((2, rows, half // 2), BF16),
            near((2, rows, half // 2), F32),
            near((rows, depth), BF16),
            near((depth, columns), BF16),
        ],
        scratch_shapes=[
            pltpu.VMEM((rows, depth), BF16),
            pltpu.VMEM((rows, columns), F32),
            pltpu.SemaphoreType.DMA((2 * parts * (len(chunks) + 1),)),
        ],
    )(me, far(sigma_hist), far(g_hist))


def half_of(core, half):
    return pl.ds(pl.multiple_of(core * half, half), half)


def product(me, sigma, g, bits, send, after=None):
    rows, half = sigma.shape[0], g.shape[1] // 2

    def kernel(me_ref, sigma, g, *refs):
        place = Place(me_ref[0], bits)
        columns = half_of(place.core ^ int(send), half)
        term = jnp.dot(sigma[...], g[:, columns], preferred_element_type=F32)
        halves_to(refs[-1], term, place.other_side if send else place.side)

    extra = [] if after is None else [after]
    return call(
        kernel,
        "memory_product",
        in_specs=[SCALAR, WHOLE, WHOLE] + [FAR] * len(extra),
        out_specs=WHOLE,
        out_shape=near((2, rows, half // 2), BF16 if send else F32),
    )(me, sigma, g, *extra)


def combined(kept, arrived, more, after):
    rows, width = more.shape
    if after is None:
        return (kept[1] + arrived[1].astype(F32) + more.astype(F32)).astype(BF16)

    def kernel(kept, arrived, more, _, out):
        out[...] = (kept[1] + arrived[1].astype(F32) + more[...].astype(F32)).astype(BF16)

    return call(
        kernel, "combined", in_specs=[WHOLE] * 3 + [FAR], out_specs=WHOLE, out_shape=near((rows, width), BF16)
    )(kept, arrived, more, after)


def cubed(g, coupling):
    orbitals = coupling.shape[0]
    g3 = g.reshape(g.shape[0] // orbitals, orbitals, g.shape[1])
    return (g3 * g3 * g3 * coupling[None]).reshape(g.shape)


def folded(x):
    line = jnp.sum(x, axis=0, keepdims=True)
    parts = [line[:, i : i + 128] for i in range(0, line.shape[1], 128)]
    return functools.reduce(lambda a, b: a + b, parts)


def columns_of(quarter, width):
    return pl.ds(pl.multiple_of(quarter * width, width), width)


def over_halves(x):
    while x.shape[0] > 1:
        half = x.shape[0] // 2
        x = x[:half] + x[half:]
    return x


def own_first(me, mine, theirs, volterra, edge, coupling, bits, after):
    rows, width = mine.shape

    def kernel(me_ref, mine, theirs, w, edge, coupling, _, memory, response, squares, g_own, cubic_own):
        at = columns_of(Place(me_ref[0], bits).quarter(), width)
        summed = (mine[...].astype(F32) + theirs[...].astype(F32)).astype(BF16)
        memory[...] = summed
        g = jnp.dot(w[0, :, :rows], summed, preferred_element_type=F32)
        g += jnp.dot(w[0, :, rows:], edge[:, at], preferred_element_type=F32)
        g_own[...] = g.astype(BF16)
        cubic = cubed(g, coupling[:, at])
        cubic_own[...] = cubic
        line = folded(cubic * cubic * (1.0 / (rows * width)))
        squares[...] = line
        scale = lax.rsqrt(jnp.sum(line) + EPS)
        response[...] = jnp.dot(w[1, :, rows:], (cubic * scale).astype(BF16), preferred_element_type=F32)

    return call(
        kernel,
        "own_first",
        in_specs=[SCALAR] + [WHOLE] * 5 + [FAR],
        out_specs=[WHOLE] * 5,
        out_shape=[
            near((rows, width), BF16),
            near((rows, width), F32),
            near((1, 128), F32),
            near((rows, width), BF16),
            near((rows, width), F32),
        ],
    )(me, mine, theirs, volterra, edge, coupling, after)


def own_second(me, mine, theirs, volterra, response, squares, coupling, bits):
    rows, width = mine.shape
    orbitals = coupling.shape[0]

    def kernel(me_ref, mine, theirs, w, response, squares, coupling, memory, out, term_own):
        at = columns_of(Place(me_ref[0], bits).quarter(), width)
        summed = (mine[...].astype(F32) + theirs[...].astype(F32)).astype(BF16)
        memory[...] = summed
        c = coupling[:, at] * (rows * width) ** -0.5
        a = jnp.dot(w[1, :, :rows], summed, preferred_element_type=F32)
        term_own[...] = a
        b = response[...]

        def weighted(square):
            return (square.reshape(rows // orbitals, orbitals, width) * c[None]).reshape(rows, width)

        ca2, cb2 = weighted(a * a), weighted(b * b)
        ca3, ca2b, cab2, cb3 = ca2 * a, ca2 * b, cb2 * a, cb2 * b
        lines = [squares[...]]
        for x, y in ((ca3, ca3), (ca3, ca2b), (ca2b, ca2b), (ca3, cb3), (cab2, cab2), (cab2, cb3), (cb3, cb3)):
            lines.append(folded(x * y))
        out[0] = jnp.concatenate(lines, axis=0)

    return call(
        kernel,
        "own_second",
        in_specs=[SCALAR] + [WHOLE] * 6,
        out_specs=[WHOLE] * 3,
        out_shape=[near((rows, width), BF16), near((1, 8, 128), F32), near((rows, width), F32)],
    )(me, mine, theirs, volterra, response, squares, coupling)


def finish_other(me, piece, volterra, edge, coupling, bits):
    rows, width = piece.shape

    def kernel(me_ref, piece, w, edge, coupling, g_out, cubic):
        at = columns_of(Place(me_ref[0], bits).quarter_of(2), width)
        g = jnp.dot(w[0, :, :rows], piece[...], preferred_element_type=F32)
        g += jnp.dot(w[0, :, rows:], edge[:, at], preferred_element_type=F32)
        g_out[...] = g.astype(BF16)
        cubic[...] = cubed(g, coupling[:, at])

    return call(
        kernel,
        "finish_other",
        in_specs=[SCALAR] + [WHOLE] * 4,
        out_specs=[WHOLE] * 2,
        out_shape=[near((rows, width), BF16), near((rows, width), F32)],
    )(me, piece, volterra, edge, coupling)


def finish_first(me, pieces, g_own, g_other, volterra, edge, coupling, bits):
    rows, width = pieces[0].shape
    columns = coupling.shape[1]

    def kernel(me_ref, *refs):
        pieces, (g_own, g_other, w, edge, coupling, g_out, cubic, held, sems) = refs[:2], refs[2:]
        place = Place(me_ref[0], bits)

        def write(source, slot):
            at = columns_of(place.quarter_of(slot), width)
            copies.append(pltpu.make_async_copy(source, g_out.at[pl.ds(0, rows), at], sems.at[slot]))
            copies[-1].start()

        copies = []
        write(g_own, 0)
        write(g_other, 2)
        for i, slot in enumerate((1, 3)):
            at = columns_of(place.quarter_of(slot), width)
            g = jnp.dot(w[0, :, :rows], pieces[i][...], preferred_element_type=F32)
            g += jnp.dot(w[0, :, rows:], edge[:, at], preferred_element_type=F32)
            held[i] = g.astype(BF16)
            write(held.at[i], slot)
            cubic[i] = cubed(g, coupling[:, at])
        for copy in copies:
            copy.wait()

    return call(
        kernel,
        "finish_first",
        in_specs=[SCALAR] + [WHOLE] * 7,
        out_specs=[HBM, WHOLE],
        out_shape=[jax.ShapeDtypeStruct((2 * rows, columns), BF16), near((2, rows, width), F32)],
        scratch_shapes=[pltpu.VMEM((2, rows, width), BF16), pltpu.SemaphoreType.DMA((4,))],
    )(me, *pieces, g_own, g_other, volterra, edge, coupling)


def memory_terms(pieces, volterra):
    rows, width = pieces[0].shape
    count = len(pieces)

    def kernel(*refs):
        pieces, (w, out) = refs[:count], refs[count:]
        for slot in range(count):
            out[slot] = jnp.dot(w[1, :, :rows], pieces[slot][...], preferred_element_type=F32)

    return call(
        kernel,
        "memory_terms",
        in_specs=[WHOLE] * (count + 1),
        out_specs=WHOLE,
        out_shape=near((count, rows, width), F32),
    )(*pieces, volterra)


def joined(parts, after=()):
    size = parts[0].shape[0]

    def kernel(*refs):
        out = refs[-1]
        for i in range(len(parts)):
            out[i * size : (i + 1) * size] = refs[i][...]

    return call(
        kernel,
        "joined",
        in_specs=[WHOLE] * len(parts) + [FAR] * len(after),
        out_specs=WHOLE,
        out_shape=near((len(parts) * size,) + parts[0].shape[1:], F32),
    )(*parts, *after)


def ordered(x, *after):
    def kernel(x, *refs):
        refs[-1][...] = x[...]

    in_specs = [WHOLE] + [FAR] * len(after)
    return call(kernel, "ordered", in_specs=in_specs, out_specs=WHOLE, out_shape=near(x.shape, x.dtype))(x, *after)


def finish_second(me, last, term_own, terms, volterra, cubic_own, cubic_other, cubic, shares, coupling, g_first, bits):
    rows, width = last.shape
    columns = coupling.shape[1]
    everyone = shares.shape[0]

    def kernel(me_ref, *refs):
        last, term_own, terms, w, cubic_own, cubic_other, cubic, shares, coupling, _ = refs[:10]
        g_out, sigma, g_held, s_held, sems = refs[10:]
        place = Place(me_ref[0], bits)
        last_term = jnp.dot(w[1, :, :rows], last[...], preferred_element_type=F32)
        sums = jnp.sum(shares[...], axis=2, keepdims=True)
        means = sums[:, 0:1, :]
        mean = over_halves(means) * (1.0 / everyone)
        ratio = jnp.sqrt((means + EPS) / (mean + EPS))
        power, series = jnp.ones_like(ratio), jnp.zeros_like(ratio)
        for k, weight in enumerate(BINOMIAL):
            series += weight * sums[:, k + 1 : k + 2, :] * power
            power = power * ratio
        scale_0 = (1.0 / jnp.sqrt(mean + EPS))[0]
        scale_1 = (1.0 / jnp.sqrt(jnp.maximum(over_halves(series) * (1.0 / everyone), 0.0) + EPS))[0]

        copies = []

        def write(value, held, slot, out, block, at):
            held[slot] = value
            sem = sems.at[len(copies)]
            copies.append(pltpu.make_async_copy(held.at[slot], out.at[pl.ds(block * rows, rows), at], sem))
            copies[-1].start()

        cubic_at = [cubic_own, cubic.at[0], cubic_other, cubic.at[1]]
        def response(slot):
            before = (cubic_at[slot][...] * scale_0).astype(BF16)
            write(before, s_held, slot, sigma, 0, columns_of(place.quarter_of(slot), width))
            g = last_term if slot == 3 else terms[slot - 1] if slot else term_own[...]
            return g + jnp.dot(w[1, :, rows:], before, preferred_element_type=F32)

        slots = (3, 0, 1, 2)
        g = response(slots[0])
        for i, slot in enumerate(slots):
            following = response(slots[i + 1]) if i + 1 < len(slots) else None
            at = columns_of(place.quarter_of(slot), width)
            write(g.astype(BF16), g_held, slot, g_out, 1, at)
            write(cubed(g, coupling[:, at] * scale_1).astype(BF16), s_held, 4 + slot, sigma, 1, at)
            g = following
        for copy in copies:
            copy.wait()

    return call(
        kernel,
        "finish_second",
        in_specs=[SCALAR] + [WHOLE] * 9 + [HBM],
        out_specs=[HBM, HBM],
        out_shape=[jax.ShapeDtypeStruct((2 * rows, columns), BF16)] * 2,
        scratch_shapes=[
            pltpu.VMEM((4, rows, width), BF16),
            pltpu.VMEM((8, rows, width), BF16),
            pltpu.SemaphoreType.DMA((12,)),
        ],
        input_output_aliases={10: 0},
    )(me, last, term_own, terms, volterra, cubic_own, cubic_other, cubic, shares, coupling, g_first)


def per_device(past, second, g_hist, sigma_hist, volterra, sigma_edge, coupling):
    blocks, rows = volterra.shape[:2]
    assert blocks == 2 and past >= 8
    bits = log2(past)
    me = lax.axis_index("past").astype(jnp.int32).reshape(1)
    even = list(range(bits))
    odd = even[:1] + even[1:][::-1]

    def swap(x, level):
        pairs = [(d, d ^ (1 << (odd if d % 2 else even)[level])) for d in range(past)]
        return lax.ppermute(x, "past", pairs)

    def exchanged(kept, arrived, sent, after=None):
        mine = combined(kept, arrived, swap(sent, 1), after)
        theirs = swap(mine, 2)
        for level in range(3, bits):
            mine = (mine.astype(F32) + theirs.astype(F32)).astype(BF16)
            theirs = swap(mine, level)
        return mine, theirs

    def passed_on(kept, arrived):
        return (kept[0] + arrived[0].astype(F32)).astype(BF16)

    def from_far(x):
        flip = [d ^ 1 ^ (1 << (even if d % 2 else odd)[1]) for d in range(past)]
        return lax.ppermute(x, "past", [(flip[d], d) for d in range(past)])

    def widened(share, level):
        return lax.ppermute(share, "second", [(z, z ^ (1 << level)) for z in range(second)])

    send, kept_0, sigma_1, g_near = first_products(me, sigma_hist, g_hist, rows, bits)
    arrived_0 = swap(send, 0)
    arrived_1 = swap(product(me, sigma_1, g_near, bits, True), 0)
    sent_0 = passed_on(kept_0, arrived_0)
    kept_1 = product(me, sigma_1, g_near, bits, False, after=arrived_1)
    sent_1 = passed_on(kept_1, arrived_1)

    mine, theirs = exchanged(kept_0, arrived_0, sent_0, after=sent_1)
    mine_1, theirs_1 = exchanged(kept_1, arrived_1, sent_1)
    own_0, response, squares, g_own, cubic_own = own_first(
        me, mine, theirs, volterra, sigma_edge, coupling, bits, after=mine_1
    )
    own_1, share, term_own = own_second(me, mine_1, theirs_1, volterra, response, squares, coupling, bits)
    g_other, cubic_other = finish_other(me, swap(own_0, 0), volterra, sigma_edge, coupling, bits)

    rounds = log2(second)
    share = jnp.concatenate([share, widened(share, 0)])
    partner = ordered(swap(own_0, 1), share, cubic_other)
    pieces = [partner, swap(partner, 0)]
    g_first, cubic = finish_first(me, pieces, g_own, g_other, volterra, sigma_edge, coupling, bits)
    for level in range(1, rounds):
        share = jnp.concatenate([share, widened(share, level)])
    partner = ordered(swap(own_1, 1), share)
    terms = memory_terms([partner, swap(own_1, 0)], volterra)
    last = swap(partner, 0)
    shares = joined([share, swap(share, 0), swap(share, 1), from_far(share)], [cubic, terms])
    results = finish_second(
        me, last, term_own, terms, volterra, cubic_own, cubic_other, cubic, shares, coupling, g_first, bits
    )
    return tuple(results)


def solution(mesh):
    return jax.shard_map(
        functools.partial(per_device, mesh.shape["past"], mesh.shape["second"]),
        mesh=mesh,
        in_specs=(P("past", "second"), P(None, "past"), P(), P(None, "second"), P(None, "second")),
        out_specs=(P(None, "second"), P(None, "second")),
        check_vma=False,
    )
```

```python
import functools

import jax
import jax.numpy as jnp
from jax import lax
from jax.experimental import pallas as pl
from jax.experimental.pallas import tpu as pltpu
from jax.sharding import PartitionSpec as P

VMEM = 20 * 1024 * 1024
F32 = jnp.float32
BF16 = jnp.bfloat16
EPS = 1e-06
BINOMIAL = (1.0, 6.0, 15.0, 20.0, 15.0, 6.0, 1.0)

WHOLE = pl.BlockSpec(memory_space=pltpu.VMEM)
FAR = pl.BlockSpec(memory_space=pl.ANY)
HBM = pl.BlockSpec(memory_space=pltpu.HBM)
SCALAR = pl.BlockSpec(memory_space=pltpu.SMEM)


def log2(n):
    bits = n.bit_length() - 1
    assert n == 1 << bits
    return bits


def near(shape, dtype):
    return pltpu.VMEM(shape, dtype)


def far(x):
    return pltpu.with_memory_space_constraint(x, pltpu.HBM)


def call(kernel, name, **kwargs):
    return pl.pallas_call(
        kernel,
        name=name,
        compiler_params=pltpu.CompilerParams(vmem_limit_bytes=VMEM),
        cost_estimate=pl.CostEstimate(flops=1024, bytes_accessed=1024, transcendentals=0),
        **kwargs,
    )


class Place:
    def __init__(self, me, bits):
        low, high = (me >> 1) & 1, (me >> (bits - 1)) & 1
        self.core = me & 1
        self.side = jnp.where(self.core == 1, high, low)
        self.other_side = jnp.where(self.core == 1, low, high)

    def quarter(self):
        return self.core * 2 + self.side

    def quarter_of(self, slot):
        if slot < 2:
            return self.core * 2 + (self.side ^ slot)
        return (self.core ^ 1) * 2 + (self.other_side ^ (slot - 2))


def halves_to(out, value, side):
    quarter = out.shape[2]
    for j in range(2):
        out[1 ^ j ^ side] = value[:, j * quarter : (j + 1) * quarter].astype(out.dtype)


def first_products(me, sigma_hist, g_hist, rows, bits):
    depth, columns = g_hist.shape
    half = columns // 2
    parts = 4
    eighth = depth // 8
    chunks = [(0, 2 * eighth), (2 * eighth, 3 * eighth), (5 * eighth, 3 * eighth)]

    def kernel(me_ref, sigma_ref, g_ref, sent, kept, sigma_next, g, sigma, total, sems):
        started = []

        def load(source, target):
            started.append(pltpu.make_async_copy(source, target, sems.at[len(started)]))
            started[-1].start()
            return started[-1]

        pieces = []
        for start, size in chunks:
            piece = []
            for i in range(parts):
                here = pl.ds(i * (rows // parts), rows // parts)
                deep = pl.ds(start, size)
                piece.append(load(sigma_ref.at[here, deep], sigma.at[here, deep]))
                here = pl.ds(start + i * (size // parts), size // parts)
                piece.append(load(g_ref.at[here, :], g.at[here, :]))
            pieces.append(piece)
        ahead = []
        for i in range(2 * parts):
            here = pl.ds(i * (rows // (2 * parts)), rows // (2 * parts))
            there = pl.ds(rows + i * (rows // (2 * parts)), rows // (2 * parts))
            ahead.append(load(sigma_ref.at[there, :], sigma_next.at[here, :]))
        for k, (start, size) in enumerate(chunks):
            for copy in pieces[k]:
                copy.wait()
            deep = pl.ds(start, size)
            term = jnp.dot(sigma[:, deep], g[deep, :], preferred_element_type=F32)
            if k == 0:
                total[...] = term
            else:
                total[...] += term
        place = Place(me_ref[0], bits)
        halves_to(sent, total[:, half_of(place.core ^ 1, half)], place.other_side)
        halves_to(kept, total[:, half_of(place.core, half)], place.side)
        for copy in ahead:
            copy.wait()

    return call(
        kernel,
        "first_products",
        in_specs=[SCALAR, HBM, HBM],
        out_specs=[WHOLE] * 4,
        out_shape=[
            near((2, rows, half // 2), BF16),
            near((2, rows, half // 2), F32),
            near((rows, depth), BF16),
            near((depth, columns), BF16),
        ],
        scratch_shapes=[
            pltpu.VMEM((rows, depth), BF16),
            pltpu.VMEM((rows, columns), F32),
            pltpu.SemaphoreType.DMA((2 * parts * (len(chunks) + 1),)),
        ],
    )(me, far(sigma_hist), far(g_hist))


def half_of(core, half):
    return pl.ds(pl.multiple_of(core * half, half), half)


def product(me, sigma, g, bits, send, after=None):
    rows, half = sigma.shape[0], g.shape[1] // 2

    def kernel(me_ref, sigma, g, *refs):
        place = Place(me_ref[0], bits)
        columns = half_of(place.core ^ int(send), half)
        term = jnp.dot(sigma[...], g[:, columns], preferred_element_type=F32)
        halves_to(refs[-1], term, place.other_side if send else place.side)

    extra = [] if after is None else [after]
    return call(
        kernel,
        "memory_product",
        in_specs=[SCALAR, WHOLE, WHOLE] + [FAR] * len(extra),
        out_specs=WHOLE,
        out_shape=near((2, rows, half // 2), BF16 if send else F32),
    )(me, sigma, g, *extra)


def combined(kept, arrived, more, after):
    rows, width = more.shape
    if after is None:
        return (kept[1] + arrived[1].astype(F32) + more.astype(F32)).astype(BF16)

    def kernel(kept, arrived, more, _, out):
        out[...] = (kept[1] + arrived[1].astype(F32) + more[...].astype(F32)).astype(BF16)

    return call(
        kernel, "combined", in_specs=[WHOLE] * 3 + [FAR], out_specs=WHOLE, out_shape=near((rows, width), BF16)
    )(kept, arrived, more, after)


def cubed(g, coupling):
    orbitals = coupling.shape[0]
    g3 = g.reshape(g.shape[0] // orbitals, orbitals, g.shape[1])
    return (g3 * g3 * g3 * coupling[None]).reshape(g.shape)


def folded(x):
    line = jnp.sum(x, axis=0, keepdims=True)
    parts = [line[:, i : i + 128] for i in range(0, line.shape[1], 128)]
    return functools.reduce(lambda a, b: a + b, parts)


def columns_of(quarter, width):
    return pl.ds(pl.multiple_of(quarter * width, width), width)


def over_halves(x):
    while x.shape[0] > 1:
        half = x.shape[0] // 2
        x = x[:half] + x[half:]
    return x


def own_first(me, mine, theirs, volterra, edge, coupling, bits, after):
    rows, width = mine.shape

    def kernel(me_ref, mine, theirs, w, edge, coupling, _, memory, response, squares, g_own, cubic_own):
        at = columns_of(Place(me_ref[0], bits).quarter(), width)
        summed = (mine[...].astype(F32) + theirs[...].astype(F32)).astype(BF16)
        memory[...] = summed
        g = jnp.dot(w[0, :, :rows], summed, preferred_element_type=F32)
        g += jnp.dot(w[0, :, rows:], edge[:, at], preferred_element_type=F32)
        g_own[...] = g.astype(BF16)
        cubic = cubed(g, coupling[:, at])
        cubic_own[...] = cubic
        line = folded(cubic * cubic * (1.0 / (rows * width)))
        squares[...] = line
        scale = lax.rsqrt(jnp.sum(line) + EPS)
        response[...] = jnp.dot(w[1, :, rows:], (cubic * scale).astype(BF16), preferred_element_type=F32)

    return call(
        kernel,
        "own_first",
        in_specs=[SCALAR] + [WHOLE] * 5 + [FAR],
        out_specs=[WHOLE] * 5,
        out_shape=[
            near((rows, width), BF16),
            near((rows, width), F32),
            near((1, 128), F32),
            near((rows, width), BF16),
            near((rows, width), F32),
        ],
    )(me, mine, theirs, volterra, edge, coupling, after)


def own_second(me, mine, theirs, volterra, response, squares, coupling, bits):
    rows, width = mine.shape
    orbitals = coupling.shape[0]

    def kernel(me_ref, mine, theirs, w, response, squares, coupling, memory, out, term_own):
        at = columns_of(Place(me_ref[0], bits).quarter(), width)
        summed = (mine[...].astype(F32) + theirs[...].astype(F32)).astype(BF16)
        memory[...] = summed
        c = coupling[:, at] * (rows * width) ** -0.5
        a = jnp.dot(w[1, :, :rows], summed, preferred_element_type=F32)
        term_own[...] = a
        b = response[...]

        def weighted(square):
            return (square.reshape(rows // orbitals, orbitals, width) * c[None]).reshape(rows, width)

        ca2, cb2 = weighted(a * a), weighted(b * b)
        ca3, ca2b, cab2, cb3 = ca2 * a, ca2 * b, cb2 * a, cb2 * b
        lines = [squares[...]]
        for x, y in ((ca3, ca3), (ca3, ca2b), (ca2b, ca2b), (ca3, cb3), (cab2, cab2), (cab2, cb3), (cb3, cb3)):
            lines.append(folded(x * y))
        out[0] = jnp.concatenate(lines, axis=0)

    return call(
        kernel,
        "own_second",
        in_specs=[SCALAR] + [WHOLE] * 6,
        out_specs=[WHOLE] * 3,
        out_shape=[near((rows, width), BF16), near((1, 8, 128), F32), near((rows, width), F32)],
    )(me, mine, theirs, volterra, response, squares, coupling)


def finish_other(me, piece, volterra, edge, coupling, bits):
    rows, width = piece.shape

    def kernel(me_ref, piece, w, edge, coupling, g_out, cubic):
        at = columns_of(Place(me_ref[0], bits).quarter_of(2), width)
        g = jnp.dot(w[0, :, :rows], piece[...], preferred_element_type=F32)
        g += jnp.dot(w[0, :, rows:], edge[:, at], preferred_element_type=F32)
        g_out[...] = g.astype(BF16)
        cubic[...] = cubed(g, coupling[:, at])

    return call(
        kernel,
        "finish_other",
        in_specs=[SCALAR] + [WHOLE] * 4,
        out_specs=[WHOLE] * 2,
        out_shape=[near((rows, width), BF16), near((rows, width), F32)],
    )(me, piece, volterra, edge, coupling)


def finish_first(me, pieces, g_own, g_other, volterra, edge, coupling, bits):
    rows, width = pieces[0].shape
    columns = coupling.shape[1]

    def kernel(me_ref, *refs):
        pieces, (g_own, g_other, w, edge, coupling, g_out, cubic, held, sems) = refs[:2], refs[2:]
        place = Place(me_ref[0], bits)

        def write(source, slot):
            at = columns_of(place.quarter_of(slot), width)
            copies.append(pltpu.make_async_copy(source, g_out.at[pl.ds(0, rows), at], sems.at[slot]))
            copies[-1].start()

        copies = []
        write(g_own, 0)
        write(g_other, 2)
        for i, slot in enumerate((1, 3)):
            at = columns_of(place.quarter_of(slot), width)
            g = jnp.dot(w[0, :, :rows], pieces[i][...], preferred_element_type=F32)
            g += jnp.dot(w[0, :, rows:], edge[:, at], preferred_element_type=F32)
            held[i] = g.astype(BF16)
            write(held.at[i], slot)
            cubic[i] = cubed(g, coupling[:, at])
        for copy in copies:
            copy.wait()

    return call(
        kernel,
        "finish_first",
        in_specs=[SCALAR] + [WHOLE] * 7,
        out_specs=[HBM, WHOLE],
        out_shape=[jax.ShapeDtypeStruct((2 * rows, columns), BF16), near((2, rows, width), F32)],
        scratch_shapes=[pltpu.VMEM((2, rows, width), BF16), pltpu.SemaphoreType.DMA((4,))],
    )(me, *pieces, g_own, g_other, volterra, edge, coupling)


def memory_terms(pieces, volterra):
    rows, width = pieces[0].shape
    count = len(pieces)

    def kernel(*refs):
        pieces, (w, out) = refs[:count], refs[count:]
        for slot in range(count):
            out[slot] = jnp.dot(w[1, :, :rows], pieces[slot][...], preferred_element_type=F32)

    return call(
        kernel,
        "memory_terms",
        in_specs=[WHOLE] * (count + 1),
        out_specs=WHOLE,
        out_shape=near((count, rows, width), F32),
    )(*pieces, volterra)


def joined(parts, after=()):
    size = parts[0].shape[0]

    def kernel(*refs):
        out = refs[-1]
        for i in range(len(parts)):
            out[i * size : (i + 1) * size] = refs[i][...]

    return call(
        kernel,
        "joined",
        in_specs=[WHOLE] * len(parts) + [FAR] * len(after),
        out_specs=WHOLE,
        out_shape=near((len(parts) * size,) + parts[0].shape[1:], F32),
    )(*parts, *after)


def ordered(x, *after):
    def kernel(x, *refs):
        refs[-1][...] = x[...]

    in_specs = [WHOLE] + [FAR] * len(after)
    return call(kernel, "ordered", in_specs=in_specs, out_specs=WHOLE, out_shape=near(x.shape, x.dtype))(x, *after)


def finish_second(me, last, term_own, terms, volterra, cubic_own, cubic_other, cubic, shares, coupling, g_first, bits):
    rows, width = last.shape
    columns = coupling.shape[1]
    everyone = shares.shape[0]

    def kernel(me_ref, *refs):
        last, term_own, terms, w, cubic_own, cubic_other, cubic, shares, coupling, _ = refs[:10]
        g_out, sigma, g_held, s_held, sems = refs[10:]
        place = Place(me_ref[0], bits)
        last_term = jnp.dot(w[1, :, :rows], last[...], preferred_element_type=F32)
        sums = jnp.sum(shares[...], axis=2, keepdims=True)
        means = sums[:, 0:1, :]
        mean = over_halves(means) * (1.0 / everyone)
        ratio = jnp.sqrt((means + EPS) / (mean + EPS))
        power, series = jnp.ones_like(ratio), jnp.zeros_like(ratio)
        for k, weight in enumerate(BINOMIAL):
            series += weight * sums[:, k + 1 : k + 2, :] * power
            power = power * ratio
        scale_0 = (1.0 / jnp.sqrt(mean + EPS))[0]
        scale_1 = (1.0 / jnp.sqrt(jnp.maximum(over_halves(series) * (1.0 / everyone), 0.0) + EPS))[0]

        copies = []

        def write(value, held, slot, out, block, at):
            held[slot] = value
            sem = sems.at[len(copies)]
            copies.append(pltpu.make_async_copy(held.at[slot], out.at[pl.ds(block * rows, rows), at], sem))
            copies[-1].start()

        cubic_at = [cubic_own, cubic.at[0], cubic_other, cubic.at[1]]
        def response(slot):
            before = (cubic_at[slot][...] * scale_0).astype(BF16)
            write(before, s_held, slot, sigma, 0, columns_of(place.quarter_of(slot), width))
            g = last_term if slot == 3 else terms[slot - 1] if slot else term_own[...]
            return g + jnp.dot(w[1, :, rows:], before, preferred_element_type=F32)

        slots = (3, 0, 1, 2)
        g = response(slots[0])
        for i, slot in enumerate(slots):
            following = response(slots[i + 1]) if i + 1 < len(slots) else None
            at = columns_of(place.quarter_of(slot), width)
            write(g.astype(BF16), g_held, slot, g_out, 1, at)
            write(cubed(g, coupling[:, at] * scale_1).astype(BF16), s_held, 4 + slot, sigma, 1, at)
            g = following
        for copy in copies:
            copy.wait()

    return call(
        kernel,
        "finish_second",
        in_specs=[SCALAR] + [WHOLE] * 9 + [HBM],
        out_specs=[HBM, HBM],
        out_shape=[jax.ShapeDtypeStruct((2 * rows, columns), BF16)] * 2,
        scratch_shapes=[
            pltpu.VMEM((4, rows, width), BF16),
            pltpu.VMEM((8, rows, width), BF16),
            pltpu.SemaphoreType.DMA((12,)),
        ],
        input_output_aliases={10: 0},
    )(me, last, term_own, terms, volterra, cubic_own, cubic_other, cubic, shares, coupling, g_first)


def per_device(past, second, g_hist, sigma_hist, volterra, sigma_edge, coupling):
    blocks, rows = volterra.shape[:2]
    assert blocks == 2 and past >= 8
    bits = log2(past)
    me = lax.axis_index("past").astype(jnp.int32).reshape(1)
    even = list(range(bits))
    odd = even[:1] + even[1:][::-1]

    def swap(x, level):
        pairs = [(d, d ^ (1 << (odd if d % 2 else even)[level])) for d in range(past)]
        return lax.ppermute(x, "past", pairs)

    def exchanged(kept, arrived, sent, after=None):
        mine = combined(kept, arrived, swap(sent, 1), after)
        theirs = swap(mine, 2)
        for level in range(3, bits):
            mine = (mine.astype(F32) + theirs.astype(F32)).astype(BF16)
            theirs = swap(mine, level)
        return mine, theirs

    def passed_on(kept, arrived):
        return (kept[0] + arrived[0].astype(F32)).astype(BF16)

    def from_far(x):
        flip = [d ^ 1 ^ (1 << (even if d % 2 else odd)[1]) for d in range(past)]
        return lax.ppermute(x, "past", [(flip[d], d) for d in range(past)])

    def widened(share, level):
        return lax.ppermute(share, "second", [(z, z ^ (1 << level)) for z in range(second)])

    send, kept_0, sigma_1, g_near = first_products(me, sigma_hist, g_hist, rows, bits)
    arrived_0 = swap(send, 0)
    arrived_1 = swap(product(me, sigma_1, g_near, bits, True), 0)
    sent_0 = passed_on(kept_0, arrived_0)
    kept_1 = product(me, sigma_1, g_near, bits, False, after=arrived_1)
    sent_1 = passed_on(kept_1, arrived_1)

    mine, theirs = exchanged(kept_0, arrived_0, sent_0, after=sent_1)
    mine_1, theirs_1 = exchanged(kept_1, arrived_1, sent_1)
    own_0, response, squares, g_own, cubic_own = own_first(
        me, mine, theirs, volterra, sigma_edge, coupling, bits, after=mine_1
    )
    own_1, share, term_own = own_second(me, mine_1, theirs_1, volterra, response, squares, coupling, bits)
    g_other, cubic_other = finish_other(me, swap(own_0, 0), volterra, sigma_edge, coupling, bits)

    rounds = log2(second)
    share = jnp.concatenate([share, widened(share, 0)])
    partner = ordered(swap(own_0, 1), share, cubic_other)
    pieces = [partner, swap(partner, 0)]
    g_first, cubic = finish_first(me, pieces, g_own, g_other, volterra, sigma_edge, coupling, bits)
    for level in range(1, rounds):
        share = jnp.concatenate([share, widened(share, level)])
    partner = ordered(swap(own_1, 1), share)
    terms = memory_terms([partner, swap(own_1, 0)], volterra)
    last = swap(partner, 0)
    shares = joined([share, swap(share, 0), swap(share, 1), from_far(share)], [cubic, terms])
    results = finish_second(
        me, last, term_own, terms, volterra, cubic_own, cubic_other, cubic, shares, coupling, g_first, bits
    )
    return tuple(results)


def solution(mesh):
    return jax.shard_map(
        functools.partial(per_device, mesh.shape["past"], mesh.shape["second"]),
        mesh=mesh,
        in_specs=(P("past", "second"), P(None, "past"), P(), P(None, "second"), P(None, "second")),
        out_specs=(P(None, "second"), P(None, "second")),
        check_vma=False,
    )
```

```python
import functools

import jax
import jax.numpy as jnp
from jax import lax
from jax.experimental import pallas as pl
from jax.experimental.pallas import tpu as pltpu
from jax.sharding import PartitionSpec as P

VMEM = 20 * 1024 * 1024
F32 = jnp.float32
BF16 = jnp.bfloat16
EPS = 1e-06
BINOMIAL = (1.0, 6.0, 15.0, 20.0, 15.0, 6.0, 1.0)

WHOLE = pl.BlockSpec(memory_space=pltpu.VMEM)
FAR = pl.BlockSpec(memory_space=pl.ANY)
HBM = pl.BlockSpec(memory_space=pltpu.HBM)
SCALAR = pl.BlockSpec(memory_space=pltpu.SMEM)


def log2(n):
    bits = n.bit_length() - 1
    assert n == 1 << bits
    return bits


def near(shape, dtype):
    return pltpu.VMEM(shape, dtype)


def far(x):
    return pltpu.with_memory_space_constraint(x, pltpu.HBM)


def call(kernel, name, **kwargs):
    return pl.pallas_call(
        kernel,
        name=name,
        compiler_params=pltpu.CompilerParams(vmem_limit_bytes=VMEM),
        cost_estimate=pl.CostEstimate(flops=1024, bytes_accessed=1024, transcendentals=0),
        **kwargs,
    )


class Place:
    def __init__(self, me, bits):
        low, high = (me >> 1) & 1, (me >> (bits - 1)) & 1
        self.core = me & 1
        self.side = jnp.where(self.core == 1, high, low)
        self.other_side = jnp.where(self.core == 1, low, high)

    def quarter(self):
        return self.core * 2 + self.side

    def quarter_of(self, slot):
        if slot < 2:
            return self.core * 2 + (self.side ^ slot)
        return (self.core ^ 1) * 2 + (self.other_side ^ (slot - 2))


def halves_to(out, value, side):
    quarter = out.shape[2]
    for j in range(2):
        out[1 ^ j ^ side] = value[:, j * quarter : (j + 1) * quarter].astype(out.dtype)


def first_products(me, sigma_hist, g_hist, rows, bits):
    depth, columns = g_hist.shape
    half = columns // 2
    tall = sigma_hist.shape[0]
    parts = 4
    eighth = depth // 8
    chunks = [(0, 2 * eighth), (2 * eighth, 3 * eighth), (5 * eighth, 3 * eighth)]

    def kernel(me_ref, sigma_ref, g_ref, sent_0, sent_1, sigma, g_kept, g_sent, total, sems):
        place = Place(me_ref[0], bits)
        sent_at, kept_at = half_of(place.core ^ 1, half), half_of(place.core, half)
        started = []

        def load(source, target):
            started.append(pltpu.make_async_copy(source, target, sems.at[len(started)]))
            started[-1].start()
            return started[-1]

        pieces = []
        for start, size in chunks:
            piece = []
            for i in range(parts):
                here = pl.ds(i * (tall // parts), tall // parts)
                deep = pl.ds(start, size)
                piece.append(load(sigma_ref.at[here, deep], sigma.at[here, deep]))
                here = pl.ds(start + i * (size // parts), size // parts)
                piece.append(load(g_ref.at[here, sent_at], g_sent.at[here, :]))
            pieces.append(piece)
        ahead = []
        for i in range(2 * parts):
            here = pl.ds(i * (depth // (2 * parts)), depth // (2 * parts))
            ahead.append(load(g_ref.at[here, kept_at], g_kept.at[here, :]))
        for k, (start, size) in enumerate(chunks):
            for copy in pieces[k]:
                copy.wait()
            deep = pl.ds(start, size)
            term = jnp.dot(sigma[:, deep], g_sent[deep, :], preferred_element_type=F32)
            if k == 0:
                total[...] = term
            elif k < len(chunks) - 1:
                total[...] += term
            else:
                term += total[...]
                halves_to(sent_0, term[:rows], place.other_side)
                halves_to(sent_1, term[rows:], place.other_side)
        for copy in ahead:
            copy.wait()

    return call(
        kernel,
        "first_products",
        in_specs=[SCALAR, HBM, HBM],
        out_specs=[WHOLE] * 4,
        out_shape=[near((2, rows, half // 2), BF16)] * 2 + [near((tall, depth), BF16), near((depth, half), BF16)],
        scratch_shapes=[
            pltpu.VMEM((depth, half), BF16),
            pltpu.VMEM((tall, half), F32),
            pltpu.SemaphoreType.DMA((2 * parts * (len(chunks) + 1),)),
        ],
    )(me, far(sigma_hist), far(g_hist))


def half_of(core, half):
    return pl.ds(pl.multiple_of(core * half, half), half)


def product(me, sigma, g, block, rows, bits, after=None):
    half = g.shape[1]

    def kernel(me_ref, sigma, g, *refs):
        term = jnp.dot(sigma[block * rows : (block + 1) * rows], g[...], preferred_element_type=F32)
        halves_to(refs[-1], term, Place(me_ref[0], bits).side)

    extra = [] if after is None else [after]
    return call(
        kernel,
        "memory_product",
        in_specs=[SCALAR, WHOLE, WHOLE] + [FAR] * len(extra),
        out_specs=WHOLE,
        out_shape=near((2, rows, half // 2), F32),
    )(me, sigma, g, *extra)


def combined(kept, arrived, more, after):
    rows, width = more.shape
    if after is None:
        return (kept[1] + arrived[1].astype(F32) + more.astype(F32)).astype(BF16)

    def kernel(kept, arrived, more, _, out):
        out[...] = (kept[1] + arrived[1].astype(F32) + more[...].astype(F32)).astype(BF16)

    return call(
        kernel, "combined", in_specs=[WHOLE] * 3 + [FAR], out_specs=WHOLE, out_shape=near((rows, width), BF16)
    )(kept, arrived, more, after)


def cubed(g, coupling):
    orbitals = coupling.shape[0]
    g3 = g.reshape(g.shape[0] // orbitals, orbitals, g.shape[1])
    return (g3 * g3 * g3 * coupling[None]).reshape(g.shape)


def folded(x):
    line = jnp.sum(x, axis=0, keepdims=True)
    parts = [line[:, i : i + 128] for i in range(0, line.shape[1], 128)]
    return functools.reduce(lambda a, b: a + b, parts)


def columns_of(quarter, width):
    return pl.ds(pl.multiple_of(quarter * width, width), width)


def over_halves(x):
    while x.shape[0] > 1:
        half = x.shape[0] // 2
        x = x[:half] + x[half:]
    return x


def own_first(me, mine, theirs, volterra, edge, coupling, bits, after):
    rows, width = mine.shape

    def kernel(me_ref, mine, theirs, w, edge, coupling, _, memory, response, squares, g_own, cubic_own):
        at = columns_of(Place(me_ref[0], bits).quarter(), width)
        summed = (mine[...].astype(F32) + theirs[...].astype(F32)).astype(BF16)
        memory[...] = summed
        g = jnp.dot(w[0, :, :rows], summed, preferred_element_type=F32)
        g += jnp.dot(w[0, :, rows:], edge[:, at], preferred_element_type=F32)
        g_own[...] = g.astype(BF16)
        cubic = cubed(g, coupling[:, at])
        cubic_own[...] = cubic
        line = folded(cubic * cubic * (1.0 / (rows * width)))
        squares[...] = line
        scale = lax.rsqrt(jnp.sum(line) + EPS)
        response[...] = jnp.dot(w[1, :, rows:], (cubic * scale).astype(BF16), preferred_element_type=F32)

    return call(
        kernel,
        "own_first",
        in_specs=[SCALAR] + [WHOLE] * 5 + [FAR],
        out_specs=[WHOLE] * 5,
        out_shape=[
            near((rows, width), BF16),
            near((rows, width), F32),
            near((1, 128), F32),
            near((rows, width), BF16),
            near((rows, width), F32),
        ],
    )(me, mine, theirs, volterra, edge, coupling, after)


def own_second(me, mine, theirs, volterra, response, squares, coupling, bits):
    rows, width = mine.shape
    orbitals = coupling.shape[0]

    def kernel(me_ref, mine, theirs, w, response, squares, coupling, memory, out, term_own):
        at = columns_of(Place(me_ref[0], bits).quarter(), width)
        summed = (mine[...].astype(F32) + theirs[...].astype(F32)).astype(BF16)
        memory[...] = summed
        c = coupling[:, at] * (rows * width) ** -0.5
        a = jnp.dot(w[1, :, :rows], summed, preferred_element_type=F32)
        term_own[...] = a
        b = response[...]

        def weighted(square):
            return (square.reshape(rows // orbitals, orbitals, width) * c[None]).reshape(rows, width)

        ca2, cb2 = weighted(a * a), weighted(b * b)
        ca3, ca2b, cab2, cb3 = ca2 * a, ca2 * b, cb2 * a, cb2 * b
        lines = [squares[...]]
        for x, y in ((ca3, ca3), (ca3, ca2b), (ca2b, ca2b), (ca3, cb3), (cab2, cab2), (cab2, cb3), (cb3, cb3)):
            lines.append(folded(x * y))
        out[0] = jnp.concatenate(lines, axis=0)

    return call(
        kernel,
        "own_second",
        in_specs=[SCALAR] + [WHOLE] * 6,
        out_specs=[WHOLE] * 3,
        out_shape=[near((rows, width), BF16), near((1, 8, 128), F32), near((rows, width), F32)],
    )(me, mine, theirs, volterra, response, squares, coupling)


def finish_other(me, piece, volterra, edge, coupling, bits):
    rows, width = piece.shape

    def kernel(me_ref, piece, w, edge, coupling, g_out, cubic):
        at = columns_of(Place(me_ref[0], bits).quarter_of(2), width)
        g = jnp.dot(w[0, :, :rows], piece[...], preferred_element_type=F32)
        g += jnp.dot(w[0, :, rows:], edge[:, at], preferred_element_type=F32)
        g_out[...] = g.astype(BF16)
        cubic[...] = cubed(g, coupling[:, at])

    return call(
        kernel,
        "finish_other",
        in_specs=[SCALAR] + [WHOLE] * 4,
        out_specs=[WHOLE] * 2,
        out_shape=[near((rows, width), BF16), near((rows, width), F32)],
    )(me, piece, volterra, edge, coupling)


def finish_first(me, pieces, g_own, g_other, volterra, edge, coupling, bits):
    rows, width = pieces[0].shape
    columns = coupling.shape[1]

    def kernel(me_ref, *refs):
        pieces, (g_own, g_other, w, edge, coupling, g_out, cubic, held, sems) = refs[:2], refs[2:]
        place = Place(me_ref[0], bits)

        def write(source, slot):
            at = columns_of(place.quarter_of(slot), width)
            copies.append(pltpu.make_async_copy(source, g_out.at[pl.ds(0, rows), at], sems.at[slot]))
            copies[-1].start()

        copies = []
        write(g_own, 0)
        write(g_other, 2)
        for i, slot in enumerate((1, 3)):
            at = columns_of(place.quarter_of(slot), width)
            g = jnp.dot(w[0, :, :rows], pieces[i][...], preferred_element_type=F32)
            g += jnp.dot(w[0, :, rows:], edge[:, at], preferred_element_type=F32)
            held[i] = g.astype(BF16)
            write(held.at[i], slot)
            cubic[i] = cubed(g, coupling[:, at])
        for copy in copies:
            copy.wait()

    return call(
        kernel,
        "finish_first",
        in_specs=[SCALAR] + [WHOLE] * 7,
        out_specs=[HBM, WHOLE],
        out_shape=[jax.ShapeDtypeStruct((2 * rows, columns), BF16), near((2, rows, width), F32)],
        scratch_shapes=[pltpu.VMEM((2, rows, width), BF16), pltpu.SemaphoreType.DMA((4,))],
    )(me, *pieces, g_own, g_other, volterra, edge, coupling)


def memory_terms(pieces, volterra):
    rows, width = pieces[0].shape
    count = len(pieces)

    def kernel(*refs):
        pieces, (w, out) = refs[:count], refs[count:]
        for slot in range(count):
            out[slot] = jnp.dot(w[1, :, :rows], pieces[slot][...], preferred_element_type=F32)

    return call(
        kernel,
        "memory_terms",
        in_specs=[WHOLE] * (count + 1),
        out_specs=WHOLE,
        out_shape=near((count, rows, width), F32),
    )(*pieces, volterra)


def joined(parts, after=()):
    size = parts[0].shape[0]

    def kernel(*refs):
        out = refs[-1]
        for i in range(len(parts)):
            out[i * size : (i + 1) * size] = refs[i][...]

    return call(
        kernel,
        "joined",
        in_specs=[WHOLE] * len(parts) + [FAR] * len(after),
        out_specs=WHOLE,
        out_shape=near((len(parts) * size,) + parts[0].shape[1:], F32),
    )(*parts, *after)


def ordered(x, *after):
    def kernel(x, *refs):
        refs[-1][...] = x[...]

    in_specs = [WHOLE] + [FAR] * len(after)
    return call(kernel, "ordered", in_specs=in_specs, out_specs=WHOLE, out_shape=near(x.shape, x.dtype))(x, *after)


def finish_second(me, last, term_own, terms, volterra, cubic_own, cubic_other, cubic, shares, coupling, g_first, bits):
    rows, width = last.shape
    columns = coupling.shape[1]
    everyone = shares.shape[0]

    def kernel(me_ref, *refs):
        last, term_own, terms, w, cubic_own, cubic_other, cubic, shares, coupling, _ = refs[:10]
        g_out, sigma, g_held, s_held, sems = refs[10:]
        place = Place(me_ref[0], bits)
        last_term = jnp.dot(w[1, :, :rows], last[...], preferred_element_type=F32)
        sums = jnp.sum(shares[...], axis=2, keepdims=True)
        means = sums[:, 0:1, :]
        mean = over_halves(means) * (1.0 / everyone)
        ratio = jnp.sqrt((means + EPS) / (mean + EPS))
        power, series = jnp.ones_like(ratio), jnp.zeros_like(ratio)
        for k, weight in enumerate(BINOMIAL):
            series += weight * sums[:, k + 1 : k + 2, :] * power
            power = power * ratio
        scale_0 = (1.0 / jnp.sqrt(mean + EPS))[0]
        scale_1 = (1.0 / jnp.sqrt(jnp.maximum(over_halves(series) * (1.0 / everyone), 0.0) + EPS))[0]

        copies = []

        def write(value, held, slot, out, block, at):
            held[slot] = value
            sem = sems.at[len(copies)]
            copies.append(pltpu.make_async_copy(held.at[slot], out.at[pl.ds(block * rows, rows), at], sem))
            copies[-1].start()

        cubic_at = [cubic_own, cubic.at[0], cubic_other, cubic.at[1]]
        def response(slot):
            before = (cubic_at[slot][...] * scale_0).astype(BF16)
            write(before, s_held, slot, sigma, 0, columns_of(place.quarter_of(slot), width))
            g = last_term if slot == 3 else terms[slot - 1] if slot else term_own[...]
            return g + jnp.dot(w[1, :, rows:], before, preferred_element_type=F32)

        slots = (3, 0, 1, 2)
        g = response(slots[0])
        for i, slot in enumerate(slots):
            following = response(slots[i + 1]) if i + 1 < len(slots) else None
            at = columns_of(place.quarter_of(slot), width)
            write(g.astype(BF16), g_held, slot, g_out, 1, at)
            write(cubed(g, coupling[:, at] * scale_1).astype(BF16), s_held, 4 + slot, sigma, 1, at)
            g = following
        for copy in copies:
            copy.wait()

    return call(
        kernel,
        "finish_second",
        in_specs=[SCALAR] + [WHOLE] * 9 + [HBM],
        out_specs=[HBM, HBM],
        out_shape=[jax.ShapeDtypeStruct((2 * rows, columns), BF16)] * 2,
        scratch_shapes=[
            pltpu.VMEM((4, rows, width), BF16),
            pltpu.VMEM((8, rows, width), BF16),
            pltpu.SemaphoreType.DMA((12,)),
        ],
        input_output_aliases={10: 0},
    )(me, last, term_own, terms, volterra, cubic_own, cubic_other, cubic, shares, coupling, g_first)


def per_device(past, second, g_hist, sigma_hist, volterra, sigma_edge, coupling):
    blocks, rows = volterra.shape[:2]
    assert blocks == 2 and past >= 8
    bits = log2(past)
    me = lax.axis_index("past").astype(jnp.int32).reshape(1)
    even = list(range(bits))
    odd = even[:1] + even[1:][::-1]

    def swap(x, level):
        pairs = [(d, d ^ (1 << (odd if d % 2 else even)[level])) for d in range(past)]
        return lax.ppermute(x, "past", pairs)

    def exchanged(kept, arrived, sent, after=None):
        mine = combined(kept, arrived, swap(sent, 1), after)
        theirs = swap(mine, 2)
        for level in range(3, bits):
            mine = (mine.astype(F32) + theirs.astype(F32)).astype(BF16)
            theirs = swap(mine, level)
        return mine, theirs

    def passed_on(kept, arrived):
        return (kept[0] + arrived[0].astype(F32)).astype(BF16)

    def from_far(x):
        flip = [d ^ 1 ^ (1 << (even if d % 2 else odd)[1]) for d in range(past)]
        return lax.ppermute(x, "past", [(flip[d], d) for d in range(past)])

    def widened(share, level):
        return lax.ppermute(share, "second", [(z, z ^ (1 << level)) for z in range(second)])

    send_0, send_1, sigma, g_kept = first_products(me, sigma_hist, g_hist, rows, bits)
    arrived_0, arrived_1 = swap(send_0, 0), swap(send_1, 0)
    kept_0 = product(me, sigma, g_kept, 0, rows, bits)
    sent_0 = passed_on(kept_0, arrived_0)
    kept_1 = product(me, sigma, g_kept, 1, rows, bits, after=arrived_1)
    sent_1 = passed_on(kept_1, arrived_1)

    mine, theirs = exchanged(kept_0, arrived_0, sent_0, after=sent_1)
    mine_1, theirs_1 = exchanged(kept_1, arrived_1, sent_1)
    own_0, response, squares, g_own, cubic_own = own_first(
        me, mine, theirs, volterra, sigma_edge, coupling, bits, after=mine_1
    )
    own_1, share, term_own = own_second(me, mine_1, theirs_1, volterra, response, squares, coupling, bits)
    g_other, cubic_other = finish_other(me, swap(own_0, 0), volterra, sigma_edge, coupling, bits)

    rounds = log2(second)
    share = jnp.concatenate([share, widened(share, 0)])
    partner = ordered(swap(own_0, 1), share, cubic_other)
    pieces = [partner, swap(partner, 0)]
    g_first, cubic = finish_first(me, pieces, g_own, g_other, volterra, sigma_edge, coupling, bits)
    for level in range(1, rounds):
        share = jnp.concatenate([share, widened(share, level)])
    partner = ordered(swap(own_1, 1), share)
    terms = memory_terms([partner, swap(own_1, 0)], volterra)
    last = swap(partner, 0)
    shares = joined([share, swap(share, 0), swap(share, 1), from_far(share)], [cubic, terms])
    results = finish_second(
        me, last, term_own, terms, volterra, cubic_own, cubic_other, cubic, shares, coupling, g_first, bits
    )
    return tuple(results)


def solution(mesh):
    return jax.shard_map(
        functools.partial(per_device, mesh.shape["past"], mesh.shape["second"]),
        mesh=mesh,
        in_specs=(P("past", "second"), P(None, "past"), P(), P(None, "second"), P(None, "second")),
        out_specs=(P(None, "second"), P(None, "second")),
        check_vma=False,
    )
```

```python
import functools

import jax
import jax.numpy as jnp
from jax import lax
from jax.experimental import pallas as pl
from jax.experimental.pallas import tpu as pltpu
from jax.sharding import PartitionSpec as P

VMEM = 20 * 1024 * 1024
F32 = jnp.float32
BF16 = jnp.bfloat16
EPS = 1e-06
BINOMIAL = (1.0, 6.0, 15.0, 20.0, 15.0, 6.0, 1.0)

WHOLE = pl.BlockSpec(memory_space=pltpu.VMEM)
FAR = pl.BlockSpec(memory_space=pl.ANY)
HBM = pl.BlockSpec(memory_space=pltpu.HBM)
SCALAR = pl.BlockSpec(memory_space=pltpu.SMEM)


def log2(n):
    bits = n.bit_length() - 1
    assert n == 1 << bits
    return bits


def near(shape, dtype):
    return pltpu.VMEM(shape, dtype)


def far(x):
    return pltpu.with_memory_space_constraint(x, pltpu.HBM)


def call(kernel, name, **kwargs):
    return pl.pallas_call(
        kernel,
        name=name,
        compiler_params=pltpu.CompilerParams(vmem_limit_bytes=VMEM),
        cost_estimate=pl.CostEstimate(flops=1024, bytes_accessed=1024, transcendentals=0),
        **kwargs,
    )


class Place:
    def __init__(self, me, bits):
        low, high = (me >> 1) & 1, (me >> (bits - 1)) & 1
        self.core = me & 1
        self.side = jnp.where(self.core == 1, high, low)
        self.other_side = jnp.where(self.core == 1, low, high)

    def quarter(self):
        return self.core * 2 + self.side

    def quarter_of(self, slot):
        if slot < 2:
            return self.core * 2 + (self.side ^ slot)
        return (self.core ^ 1) * 2 + (self.other_side ^ (slot - 2))


def halves_to(out, value, side):
    quarter = out.shape[2]
    for j in range(2):
        out[1 ^ j ^ side] = value[:, j * quarter : (j + 1) * quarter].astype(out.dtype)


def first_products(me, sigma_hist, g_hist, rows, bits):
    depth, columns = g_hist.shape
    half = columns // 2
    tall = sigma_hist.shape[0]
    parts = 4
    eighth = depth // 8
    chunks = [(0, 2 * eighth), (2 * eighth, 3 * eighth), (5 * eighth, 3 * eighth)]

    def kernel(me_ref, sigma_ref, g_ref, on_0, on_1, kept_0, kept_1, sigma, g_kept, g_sent, total, sems):
        place = Place(me_ref[0], bits)
        sent_at, kept_at = half_of(place.core ^ 1, half), half_of(place.core, half)
        started = []

        def load(source, target):
            started.append(pltpu.make_async_copy(source, target, sems.at[len(started)]))
            started[-1].start()
            return started[-1]

        pieces = []
        for start, size in chunks:
            piece = []
            for i in range(parts):
                here = pl.ds(i * (tall // parts), tall // parts)
                deep = pl.ds(start, size)
                piece.append(load(sigma_ref.at[here, deep], sigma.at[here, deep]))
                here = pl.ds(start + i * (size // parts), size // parts)
                piece.append(load(g_ref.at[here, sent_at], g_sent.at[here, :]))
            pieces.append(piece)
        ahead = []
        for i in range(2 * parts):
            here = pl.ds(i * (depth // (2 * parts)), depth // (2 * parts))
            ahead.append(load(g_ref.at[here, kept_at], g_kept.at[here, :]))
        for k, (start, size) in enumerate(chunks):
            for copy in pieces[k]:
                copy.wait()
            deep = pl.ds(start, size)
            term = jnp.dot(sigma[:, deep], g_sent[deep, :], preferred_element_type=F32)
            if k == 0:
                total[...] = term
            elif k < len(chunks) - 1:
                total[...] += term
            else:
                term += total[...]
                left, right = term[:, : half // 2], term[:, half // 2 :]
                on = jnp.where(place.other_side == 0, right, left).astype(BF16)
                on_0[...], on_1[...] = on[:rows], on[rows:]
                keep = jnp.where(place.other_side == 0, left, right)
                kept_0[...], kept_1[...] = keep[:rows], keep[rows:]
        for copy in ahead:
            copy.wait()

    return call(
        kernel,
        "first_products",
        in_specs=[SCALAR, HBM, HBM],
        out_specs=[WHOLE] * 6,
        out_shape=[near((rows, half // 2), BF16)] * 2
        + [near((rows, half // 2), F32)] * 2
        + [near((tall, depth), BF16), near((depth, half), BF16)],
        scratch_shapes=[
            pltpu.VMEM((depth, half), BF16),
            pltpu.VMEM((tall, half), F32),
            pltpu.SemaphoreType.DMA((2 * parts * (len(chunks) + 1),)),
        ],
    )(me, far(sigma_hist), far(g_hist))


def half_of(core, half):
    return pl.ds(pl.multiple_of(core * half, half), half)


def product(me, sigma, g, block, rows, bits, after=None):
    half = g.shape[1]

    def kernel(me_ref, sigma, g, *refs):
        term = jnp.dot(sigma[block * rows : (block + 1) * rows], g[...], preferred_element_type=F32)
        halves_to(refs[-1], term, Place(me_ref[0], bits).side)

    extra = [] if after is None else [after]
    return call(
        kernel,
        "memory_product",
        in_specs=[SCALAR, WHOLE, WHOLE] + [FAR] * len(extra),
        out_specs=WHOLE,
        out_shape=near((2, rows, half // 2), F32),
    )(me, sigma, g, *extra)


def combined(kept, arrived, more, after):
    rows, width = more.shape
    if after is None:
        return (kept[1] + arrived + more.astype(F32)).astype(BF16)

    def kernel(kept, arrived, more, _, out):
        out[...] = (kept[1] + arrived[...] + more[...].astype(F32)).astype(BF16)

    return call(
        kernel, "combined", in_specs=[WHOLE] * 3 + [FAR], out_specs=WHOLE, out_shape=near((rows, width), BF16)
    )(kept, arrived, more, after)


def cubed(g, coupling):
    orbitals = coupling.shape[0]
    g3 = g.reshape(g.shape[0] // orbitals, orbitals, g.shape[1])
    return (g3 * g3 * g3 * coupling[None]).reshape(g.shape)


def folded(x):
    line = jnp.sum(x, axis=0, keepdims=True)
    parts = [line[:, i : i + 128] for i in range(0, line.shape[1], 128)]
    return functools.reduce(lambda a, b: a + b, parts)


def columns_of(quarter, width):
    return pl.ds(pl.multiple_of(quarter * width, width), width)


def over_halves(x):
    while x.shape[0] > 1:
        half = x.shape[0] // 2
        x = x[:half] + x[half:]
    return x


def own_first(me, mine, theirs, volterra, edge, coupling, bits, after):
    rows, width = mine.shape

    def kernel(me_ref, mine, theirs, w, edge, coupling, _, memory, response, squares, g_own, cubic_own):
        at = columns_of(Place(me_ref[0], bits).quarter(), width)
        summed = (mine[...].astype(F32) + theirs[...].astype(F32)).astype(BF16)
        memory[...] = summed
        g = jnp.dot(w[0, :, :rows], summed, preferred_element_type=F32)
        g += jnp.dot(w[0, :, rows:], edge[:, at], preferred_element_type=F32)
        g_own[...] = g.astype(BF16)
        cubic = cubed(g, coupling[:, at])
        cubic_own[...] = cubic
        line = folded(cubic * cubic * (1.0 / (rows * width)))
        squares[...] = line
        scale = lax.rsqrt(jnp.sum(line) + EPS)
        response[...] = jnp.dot(w[1, :, rows:], (cubic * scale).astype(BF16), preferred_element_type=F32)

    return call(
        kernel,
        "own_first",
        in_specs=[SCALAR] + [WHOLE] * 5 + [FAR],
        out_specs=[WHOLE] * 5,
        out_shape=[
            near((rows, width), BF16),
            near((rows, width), F32),
            near((1, 128), F32),
            near((rows, width), BF16),
            near((rows, width), F32),
        ],
    )(me, mine, theirs, volterra, edge, coupling, after)


def own_second(me, mine, theirs, volterra, response, squares, coupling, bits):
    rows, width = mine.shape
    orbitals = coupling.shape[0]

    def kernel(me_ref, mine, theirs, w, response, squares, coupling, memory, out, term_own):
        at = columns_of(Place(me_ref[0], bits).quarter(), width)
        summed = (mine[...].astype(F32) + theirs[...].astype(F32)).astype(BF16)
        memory[...] = summed
        c = coupling[:, at] * (rows * width) ** -0.5
        a = jnp.dot(w[1, :, :rows], summed, preferred_element_type=F32)
        term_own[...] = a
        b = response[...]

        def weighted(square):
            return (square.reshape(rows // orbitals, orbitals, width) * c[None]).reshape(rows, width)

        ca2, cb2 = weighted(a * a), weighted(b * b)
        ca3, ca2b, cab2, cb3 = ca2 * a, ca2 * b, cb2 * a, cb2 * b
        lines = [squares[...]]
        for x, y in ((ca3, ca3), (ca3, ca2b), (ca2b, ca2b), (ca3, cb3), (cab2, cab2), (cab2, cb3), (cb3, cb3)):
            lines.append(folded(x * y))
        out[0] = jnp.concatenate(lines, axis=0)

    return call(
        kernel,
        "own_second",
        in_specs=[SCALAR] + [WHOLE] * 6,
        out_specs=[WHOLE] * 3,
        out_shape=[near((rows, width), BF16), near((1, 8, 128), F32), near((rows, width), F32)],
    )(me, mine, theirs, volterra, response, squares, coupling)


def finish_other(me, piece, volterra, edge, coupling, bits):
    rows, width = piece.shape

    def kernel(me_ref, piece, w, edge, coupling, g_out, cubic):
        at = columns_of(Place(me_ref[0], bits).quarter_of(2), width)
        g = jnp.dot(w[0, :, :rows], piece[...], preferred_element_type=F32)
        g += jnp.dot(w[0, :, rows:], edge[:, at], preferred_element_type=F32)
        g_out[...] = g.astype(BF16)
        cubic[...] = cubed(g, coupling[:, at])

    return call(
        kernel,
        "finish_other",
        in_specs=[SCALAR] + [WHOLE] * 4,
        out_specs=[WHOLE] * 2,
        out_shape=[near((rows, width), BF16), near((rows, width), F32)],
    )(me, piece, volterra, edge, coupling)


def finish_first(me, pieces, g_own, g_other, volterra, edge, coupling, bits):
    rows, width = pieces[0].shape
    columns = coupling.shape[1]

    def kernel(me_ref, *refs):
        pieces, (g_own, g_other, w, edge, coupling, g_out, cubic, held, sems) = refs[:2], refs[2:]
        place = Place(me_ref[0], bits)

        def write(source, slot):
            at = columns_of(place.quarter_of(slot), width)
            copies.append(pltpu.make_async_copy(source, g_out.at[pl.ds(0, rows), at], sems.at[slot]))
            copies[-1].start()

        copies = []
        write(g_own, 0)
        write(g_other, 2)
        for i, slot in enumerate((1, 3)):
            at = columns_of(place.quarter_of(slot), width)
            g = jnp.dot(w[0, :, :rows], pieces[i][...], preferred_element_type=F32)
            g += jnp.dot(w[0, :, rows:], edge[:, at], preferred_element_type=F32)
            held[i] = g.astype(BF16)
            write(held.at[i], slot)
            cubic[i] = cubed(g, coupling[:, at])
        for copy in copies:
            copy.wait()

    return call(
        kernel,
        "finish_first",
        in_specs=[SCALAR] + [WHOLE] * 7,
        out_specs=[HBM, WHOLE],
        out_shape=[jax.ShapeDtypeStruct((2 * rows, columns), BF16), near((2, rows, width), F32)],
        scratch_shapes=[pltpu.VMEM((2, rows, width), BF16), pltpu.SemaphoreType.DMA((4,))],
    )(me, *pieces, g_own, g_other, volterra, edge, coupling)


def memory_terms(pieces, volterra):
    rows, width = pieces[0].shape
    count = len(pieces)

    def kernel(*refs):
        pieces, (w, out) = refs[:count], refs[count:]
        for slot in range(count):
            out[slot] = jnp.dot(w[1, :, :rows], pieces[slot][...], preferred_element_type=F32)

    return call(
        kernel,
        "memory_terms",
        in_specs=[WHOLE] * (count + 1),
        out_specs=WHOLE,
        out_shape=near((count, rows, width), F32),
    )(*pieces, volterra)


def joined(parts, after=()):
    size = parts[0].shape[0]

    def kernel(*refs):
        out = refs[-1]
        for i in range(len(parts)):
            out[i * size : (i + 1) * size] = refs[i][...]

    return call(
        kernel,
        "joined",
        in_specs=[WHOLE] * len(parts) + [FAR] * len(after),
        out_specs=WHOLE,
        out_shape=near((len(parts) * size,) + parts[0].shape[1:], F32),
    )(*parts, *after)


def ordered(x, *after):
    def kernel(x, *refs):
        refs[-1][...] = x[...]

    in_specs = [WHOLE] + [FAR] * len(after)
    return call(kernel, "ordered", in_specs=in_specs, out_specs=WHOLE, out_shape=near(x.shape, x.dtype))(x, *after)


def finish_second(me, last, term_own, terms, volterra, cubic_own, cubic_other, cubic, shares, coupling, g_first, bits):
    rows, width = last.shape
    columns = coupling.shape[1]
    everyone = shares.shape[0]

    def kernel(me_ref, *refs):
        last, term_own, terms, w, cubic_own, cubic_other, cubic, shares, coupling, _ = refs[:10]
        g_out, sigma, g_held, s_held, sems = refs[10:]
        place = Place(me_ref[0], bits)
        last_term = jnp.dot(w[1, :, :rows], last[...], preferred_element_type=F32)
        sums = jnp.sum(shares[...], axis=2, keepdims=True)
        means = sums[:, 0:1, :]
        mean = over_halves(means) * (1.0 / everyone)
        ratio = jnp.sqrt((means + EPS) / (mean + EPS))
        power, series = jnp.ones_like(ratio), jnp.zeros_like(ratio)
        for k, weight in enumerate(BINOMIAL):
            series += weight * sums[:, k + 1 : k + 2, :] * power
            power = power * ratio
        scale_0 = (1.0 / jnp.sqrt(mean + EPS))[0]
        scale_1 = (1.0 / jnp.sqrt(jnp.maximum(over_halves(series) * (1.0 / everyone), 0.0) + EPS))[0]

        copies = []

        def write(value, held, slot, out, block, at):
            held[slot] = value
            sem = sems.at[len(copies)]
            copies.append(pltpu.make_async_copy(held.at[slot], out.at[pl.ds(block * rows, rows), at], sem))
            copies[-1].start()

        cubic_at = [cubic_own, cubic.at[0], cubic_other, cubic.at[1]]
        def response(slot):
            before = (cubic_at[slot][...] * scale_0).astype(BF16)
            write(before, s_held, slot, sigma, 0, columns_of(place.quarter_of(slot), width))
            g = last_term if slot == 3 else terms[slot - 1] if slot else term_own[...]
            return g + jnp.dot(w[1, :, rows:], before, preferred_element_type=F32)

        slots = (3, 0, 1, 2)
        g = response(slots[0])
        for i, slot in enumerate(slots):
            following = response(slots[i + 1]) if i + 1 < len(slots) else None
            at = columns_of(place.quarter_of(slot), width)
            write(g.astype(BF16), g_held, slot, g_out, 1, at)
            write(cubed(g, coupling[:, at] * scale_1).astype(BF16), s_held, 4 + slot, sigma, 1, at)
            g = following
        for copy in copies:
            copy.wait()

    return call(
        kernel,
        "finish_second",
        in_specs=[SCALAR] + [WHOLE] * 9 + [HBM],
        out_specs=[HBM, HBM],
        out_shape=[jax.ShapeDtypeStruct((2 * rows, columns), BF16)] * 2,
        scratch_shapes=[
            pltpu.VMEM((4, rows, width), BF16),
            pltpu.VMEM((8, rows, width), BF16),
            pltpu.SemaphoreType.DMA((12,)),
        ],
        input_output_aliases={10: 0},
    )(me, last, term_own, terms, volterra, cubic_own, cubic_other, cubic, shares, coupling, g_first)


def per_device(past, second, g_hist, sigma_hist, volterra, sigma_edge, coupling):
    blocks, rows = volterra.shape[:2]
    assert blocks == 2 and past >= 8
    bits = log2(past)
    me = lax.axis_index("past").astype(jnp.int32).reshape(1)
    even = list(range(bits))
    odd = even[:1] + even[1:][::-1]

    def swap(x, level):
        pairs = [(d, d ^ (1 << (odd if d % 2 else even)[level])) for d in range(past)]
        return lax.ppermute(x, "past", pairs)

    def exchanged(kept, arrived, sent, after=None):
        mine = combined(kept, arrived, swap(sent, 1), after)
        theirs = swap(mine, 2)
        for level in range(3, bits):
            mine = (mine.astype(F32) + theirs.astype(F32)).astype(BF16)
            theirs = swap(mine, level)
        return mine, theirs

    def passed_on(kept, arrived):
        return (kept[0] + arrived.astype(F32)).astype(BF16)

    def from_far(x):
        flip = [d ^ 1 ^ (1 << (even if d % 2 else odd)[1]) for d in range(past)]
        return lax.ppermute(x, "past", [(flip[d], d) for d in range(past)])

    def widened(share, level):
        return lax.ppermute(share, "second", [(z, z ^ (1 << level)) for z in range(second)])

    on_0, on_1, keep_0, keep_1, sigma, g_kept = first_products(me, sigma_hist, g_hist, rows, bits)
    arrived_on_1 = swap(on_1, 0)
    kept_0 = product(me, sigma, g_kept, 0, rows, bits)
    sent_0 = passed_on(kept_0, swap(on_0, 0))
    kept_1 = product(me, sigma, g_kept, 1, rows, bits, after=arrived_on_1)
    sent_1 = passed_on(kept_1, arrived_on_1)
    arrived_0, arrived_1 = swap(keep_0, 0), swap(keep_1, 0)

    mine, theirs = exchanged(kept_0, arrived_0, sent_0, after=sent_1)
    mine_1, theirs_1 = exchanged(kept_1, arrived_1, sent_1)
    own_0, response, squares, g_own, cubic_own = own_first(
        me, mine, theirs, volterra, sigma_edge, coupling, bits, after=mine_1
    )
    own_1, share, term_own = own_second(me, mine_1, theirs_1, volterra, response, squares, coupling, bits)
    g_other, cubic_other = finish_other(me, swap(own_0, 0), volterra, sigma_edge, coupling, bits)

    rounds = log2(second)
    share = jnp.concatenate([share, widened(share, 0)])
    partner = ordered(swap(own_0, 1), share, cubic_other)
    pieces = [partner, swap(partner, 0)]
    g_first, cubic = finish_first(me, pieces, g_own, g_other, volterra, sigma_edge, coupling, bits)
    for level in range(1, rounds):
        share = jnp.concatenate([share, widened(share, level)])
    partner = ordered(swap(own_1, 1), share)
    terms = memory_terms([partner, swap(own_1, 0)], volterra)
    last = swap(partner, 0)
    shares = joined([share, swap(share, 0), swap(share, 1), from_far(share)], [cubic, terms])
    results = finish_second(
        me, last, term_own, terms, volterra, cubic_own, cubic_other, cubic, shares, coupling, g_first, bits
    )
    return tuple(results)


def solution(mesh):
    return jax.shard_map(
        functools.partial(per_device, mesh.shape["past"], mesh.shape["second"]),
        mesh=mesh,
        in_specs=(P("past", "second"), P(None, "past"), P(), P(None, "second"), P(None, "second")),
        out_specs=(P(None, "second"), P(None, "second")),
        check_vma=False,
    )
```
